128 devices in a mesh: dp: 8 (over x, core), fsdp: 16 (over y, z).
Axes of the slice: x: 4, y: 4, z: 4, core: 2. Of those that a mesh axis runs over, the one named last changes fastest.
Arguments:
- queries: bfloat16 [24576, 4096], P(('dp', 'fsdp')), may hold values from -6 to 6
- passages: bfloat16 [24576, 4096], P(('dp', 'fsdp')), may hold values from -6 to 6
- head_weight: bfloat16 [4096, 2048], P('fsdp'), may hold values from -0.09375 to 0.09375
- send_lists: int32 [8, 16, 8, 48], P('dp', 'fsdp'), may hold values from 0 to 191
- neg_slots: int32 [24576, 16], P(('dp', 'fsdp')), may hold values from 0 to 383
Outputs:
- query_grads: bfloat16 [24576, 4096], P(('dp', 'fsdp'))
- passage_grads: bfloat16 [24576, 4096], P(('dp', 'fsdp'))
- head_grads: float32 [4096, 2048], P('fsdp', 'dp')
The draws below stay inside these ranges and needn't reach their ends.
All inputs are finite; a program needn't handle non-finite values.
Results may differ from the reference program's by a relative error of at most 0.025.
Values may be sent and summed in bfloat16 or wider, within the bound.
No kernel may reach another device: no remote copies, remote signals or barrier semaphores. Data moves between devices by JAX's collectives and lax.ppermute only.
A program may use at most 128 MiB of HBM per device.

```python
import jax
import jax.numpy as jnp
from jax import lax

D = 4096
E = 2048
NEG = 16
ROWS_DEV = 192
CAP = 48
SLOTS = 384
QUERIES = 24576
PASSAGES = 24576
N_DP = 8
N_FSDP = 16
DEVICES = 128


def set_ends(values, key, smallest, top_value):
    spot = [jax.random.randint(jax.random.fold_in(key, axis), (), 0, length) for axis, length in enumerate(values.shape)]
    longest = values.shape.index(max(values.shape))
    next_to = spot[:longest] + [(spot[longest] + 1) % values.shape[longest]] + spot[longest + 1:]
    return values.at[tuple(spot)].set(smallest).at[tuple(next_to)].set(top_value)


def levels(stream_key, dims, cuts, least, high):
    gain, own = 1.0, jax.random.fold_in(stream_key, 6)
    for axis_at, shards_of in cuts:
        draws = jnp.exp(jax.random.uniform(jax.random.fold_in(own, axis_at), (shards_of,), jnp.float32, least / len(cuts), high / len(cuts)))
        gain = gain * jnp.repeat(draws, dims[axis_at] // shards_of).reshape([-1 if axis == axis_at else 1 for axis in range(len(dims))])
    return gain


def bell_draw(own_key, shape, scale, limit, pieces=(), held_as=jnp.bfloat16):
    values = jax.random.normal(own_key, shape, jnp.float32) * scale
    if len(pieces) > 0:
        values = levels(own_key, shape, pieces, -0.22, 0.18) * values
    return jnp.clip(values, min=-limit, max=limit).astype(held_as)


def setup_inputs(seed: int = 0) -> dict:
    streams_of = jax.random.split(jax.random.key(seed), 6)
    return {
        "queries": bell_draw(streams_of[0], (QUERIES, D), 1.0, 6.0, ((0, 128),)),
        "passages": bell_draw(streams_of[1], (PASSAGES, D), 1.0, 6.0, ((0, 128),)),
        "head_weight": bell_draw(streams_of[2], (D, E), D ** -0.5, 0.09375, ((0, 16),)),
        "send_lists": set_ends(jax.random.randint(streams_of[3], (N_DP, N_FSDP, N_DP, CAP), 0, ROWS_DEV), jax.random.fold_in(streams_of[3], 1), 0, ROWS_DEV - 1).astype(jnp.int32),
        "neg_slots": set_ends(jax.random.randint(streams_of[4], (QUERIES, NEG), 0, SLOTS), jax.random.fold_in(streams_of[4], 1), 0, SLOTS - 1).astype(jnp.int32),
    }


EPSILON = 1e-06

def rms_scale(values):
    return values * lax.rsqrt(lax.optimization_barrier(jnp.mean(values * values, axis=-1, keepdims=True)) + EPSILON)

def reference(queries, passages, head_weight, send_lists, neg_slots):
    width = head_weight.shape[1]
    scale = 16.0 / width
    query_pre = jnp.dot(queries, head_weight, preferred_element_type=jnp.float32)
    passage_pre = jnp.dot(passages, head_weight, preferred_element_type=jnp.float32)
    query_emb = rms_scale(query_pre).astype(jnp.bfloat16)
    passage_emb = rms_scale(passage_pre).astype(jnp.bfloat16)
    query_grid = query_emb.reshape(N_DP, N_FSDP, ROWS_DEV, width)
    passage_grid = passage_emb.reshape(N_DP, N_FSDP, ROWS_DEV, width)
    lists_dest = jnp.transpose(send_lists, (2, 1, 0, 3))
    source_index = jnp.arange(N_DP, dtype=jnp.int32)[None, None, :, None]
    column_index = jnp.arange(N_FSDP, dtype=jnp.int32)[None, :, None, None]
    fetched = passage_grid[source_index, column_index, lists_dest].reshape(N_DP, N_FSDP, SLOTS, width)
    query_wide = query_grid.astype(jnp.float32)
    passage_wide = passage_grid.astype(jnp.float32)
    fetched_wide = fetched.astype(jnp.float32)
    positive = lax.optimization_barrier(jnp.sum(query_wide * passage_wide, axis=-1)) * scale
    table = jnp.einsum('abqe,abre->abqr', query_wide, fetched_wide) * scale
    slots = neg_slots.reshape(N_DP, N_FSDP, ROWS_DEV, NEG)
    negative = jnp.take_along_axis(table, slots, axis=3)
    logits = jnp.concatenate([positive[..., None], negative], axis=-1)
    probs = jax.nn.softmax(logits, axis=-1)
    target = (jnp.arange(NEG + 1) == 0).astype(jnp.float32)
    weights = (probs - target).astype(jnp.bfloat16)
    selector = (slots[..., None] == jnp.arange(SLOTS, dtype=jnp.int32)).astype(jnp.float32)
    mixing = jnp.einsum('abqn,abqnr->abqr', weights[..., 1:].astype(jnp.float32), selector).astype(jnp.bfloat16)
    first = weights[..., :1].astype(jnp.float32)
    query_emb_grad = first * passage_wide + jnp.einsum('abqr,abre->abqe', mixing.astype(jnp.float32), fetched_wide)
    fetched_grad = jnp.einsum('abqr,abqe->abre', mixing.astype(jnp.float32), query_wide).astype(jnp.bfloat16)
    returned = fetched_grad.reshape(N_DP, N_FSDP, N_DP, CAP, width)
    returned = jnp.transpose(returned, (2, 1, 0, 3, 4)).reshape(N_DP, N_FSDP, SLOTS, width)
    owner_lists = send_lists.reshape(N_DP, N_FSDP, SLOTS)
    matrix = (owner_lists[:, :, None, :] == jnp.arange(ROWS_DEV, dtype=jnp.int32)[:, None]).astype(jnp.float32)
    passage_emb_grad = first * query_wide + jnp.einsum('sbpr,sbre->sbpe', matrix, returned.astype(jnp.float32))
    query_emb_grad = query_emb_grad.reshape(QUERIES, width)
    passage_emb_grad = passage_emb_grad.reshape(PASSAGES, width)
    _, query_back = jax.vjp(rms_scale, query_pre)
    _, passage_back = jax.vjp(rms_scale, passage_pre)
    query_dy = query_back(query_emb_grad)[0].astype(jnp.bfloat16)
    passage_dy = passage_back(passage_emb_grad)[0].astype(jnp.bfloat16)
    contract = (((1,), (1,)), ((), ()))
    query_grads = lax.dot_general(query_dy, head_weight, contract, preferred_element_type=jnp.float32).astype(jnp.bfloat16)
    passage_grads = lax.dot_general(passage_dy, head_weight, contract, preferred_element_type=jnp.float32).astype(jnp.bfloat16)
    states = jnp.concatenate([queries.reshape(DEVICES, ROWS_DEV, D), passages.reshape(DEVICES, ROWS_DEV, D)], axis=1)
    dys = jnp.concatenate([query_dy.reshape(DEVICES, ROWS_DEV, width), passage_dy.reshape(DEVICES, ROWS_DEV, width)], axis=1)

    def accumulate(total, pair):
        block, slope = pair
        part = lax.dot_general(block, slope, (((0,), (0,)), ((), ())), preferred_element_type=jnp.float32) / 128.0
        part = lax.optimization_barrier(part.astype(jnp.bfloat16))
        return (total + part.astype(jnp.float32), None)
    head_grads, _ = lax.scan(accumulate, jnp.zeros((D, width), jnp.float32), (states, dys))
    return (query_grads, passage_grads, head_grads)
```

```python
import jax
import jax.numpy as jnp
from jax import lax
from jax.experimental import pallas as pl
from jax.experimental.pallas import tpu as pltpu
from jax.sharding import Mesh, PartitionSpec as P

EPSILON = 1e-06
BLOCK = 256
RING = 4
SWAP = [(0, 1), (1, 0)]
BF16 = jnp.bfloat16
F32 = jnp.float32


def shift(value, place, step):
    pairs = []
    for c in range(2):
        for y in range(RING):
            for z in range(RING):
                to_y, to_z = y, z
                if (place == 1) == (c == 0):
                    to_y = (y + step) % RING
                else:
                    to_z = (z + step) % RING
                pairs.append((c * 16 + y * 4 + z, c * 16 + to_y * 4 + to_z))
    return lax.ppermute(value, ("c", "y", "z"), pairs)


def swap(value):
    return lax.ppermute(value, "c", SWAP)


def block_at(core, d1, d2):
    y, z = lax.axis_index("y"), lax.axis_index("z")
    far_y = jnp.where(core == 0, d1, d2)
    far_z = jnp.where(core == 0, d2, d1)
    return ((y + far_y) % RING) * RING + (z + far_z) % RING


def gather_head(own):
    up = shift(own, 1, 1)
    down = shift(own, 1, -1)
    half = own.shape[0] // 2
    first = jnp.concatenate([own, up], axis=0)
    first_up = shift(first, 2, 1)
    first_down = shift(first, 2, -1)
    far_a = shift(up[:half], 1, 1)
    far_b = shift(down[half:], 1, -1)
    second = jnp.concatenate([down, far_a, far_b], axis=0)
    second_up = shift(second, 2, 1)
    second_down = shift(second, 2, -1)
    first_far = shift(first_up, 2, 1)
    second_far = shift(second_down, 2, -1)
    pieces = [first, second, first_up, first_down, second_up, second_down, first_far, second_far]
    a, b = (0, -1), (1, 2)
    places = [(a, 0), (b, 0), (a, -1), (a, 1), (b, -1), (b, 1), (a, 2), (b, 2)]
    return pieces, [(d1, d2) for d1s, d2 in places for d1 in d1s]


def place_kernel(at_ref, *refs):
    pieces, out_ref, sems = refs[:16], refs[16], refs[17]
    copies = []
    for i, piece in enumerate(pieces):
        for j in range(2):
            k = 2 * i + j
            row = pl.multiple_of(at_ref[0, k] * BLOCK, BLOCK)
            col = pl.multiple_of(at_ref[1, k] * 1024, 1024)
            copies.append(
                pltpu.make_async_copy(
                    piece.at[pl.ds(j * BLOCK, BLOCK), :],
                    out_ref.at[pl.ds(row, BLOCK), pl.ds(col, 1024)],
                    sems.at[k],
                )
            )
    for copy in copies:
        copy.start()
    for copy in copies:
        copy.wait()


def place_head(pieces, at):
    return pl.pallas_call(
        place_kernel,
        grid_spec=pltpu.PrefetchScalarGridSpec(
            num_scalar_prefetch=1,
            grid=(1,),
            in_specs=[pl.BlockSpec(memory_space=pl.ANY)] * 16,
            out_specs=pl.BlockSpec(memory_space=pl.ANY),
            scratch_shapes=[pltpu.SemaphoreType.DMA((32,))],
        ),
        out_shape=jax.ShapeDtypeStruct((4096, 2048), BF16),
        name="place_head",
    )(at, *pieces)


def partial_kernel(at_ref, states_ref, slopes_ref, *refs):
    out_ref = refs[-1]
    total = lax.dot_general(
        states_ref[...], slopes_ref[...], (((0,), (0,)), ((), ())), preferred_element_type=F32
    ) * (1.0 / 128.0)
    for ref in refs[:-1]:
        total = total + ref[...].astype(F32)
    out_ref[...] = total.astype(BF16)


def head_partial(states, slopes, at, adds=()):
    count = at.shape[0]
    rows, width = slopes.shape
    return pl.pallas_call(
        partial_kernel,
        grid_spec=pltpu.PrefetchScalarGridSpec(
            num_scalar_prefetch=1,
            grid=(count,),
            in_specs=[
                pl.BlockSpec((rows, BLOCK), lambda k, at: (0, at[k])),
                pl.BlockSpec((rows, width), lambda k, at: (0, 0)),
            ]
            + [pl.BlockSpec((BLOCK, width), lambda k, at: (k, 0))] * len(adds),
            out_specs=pl.BlockSpec((BLOCK, width), lambda k, at: (k, 0)),
        ),
        out_shape=jax.ShapeDtypeStruct((count * BLOCK, width), BF16),
        compiler_params=pltpu.CompilerParams(vmem_limit_bytes=32 * 1024 * 1024),
        name="head_partial",
    )(at, states, slopes, *adds)


def add(*values):
    total = values[0].astype(F32)
    for value in values[1:]:
        total = total + value.astype(F32)
    return total.astype(BF16)


def scatter_head(states, slopes, core):
    def part(d1, d2s, *adds):
        at = jnp.stack([block_at(core, d1, d2) for d2 in d2s]).astype(jnp.int32)
        return head_partial(states, slopes, at, adds)

    a, b = (2, 1), (-1, 0)
    far_a = shift(part(2, a), 1, 1)
    far_b = shift(part(2, b), 1, -1)
    up_b = shift(part(1, b), 1, 1)
    down_a = shift(part(-1, a), 1, -1)
    up_a = shift(part(1, a, far_a), 1, 1)
    down_b = shift(part(-1, b, far_b), 1, -1)
    mine_a = part(0, a, down_a, up_a)
    mine_b = part(0, b, up_b, down_b)
    far, up, down, mine = mine_a[:BLOCK], mine_a[BLOCK:], mine_b[:BLOCK], mine_b[BLOCK:]
    half = BLOCK // 2
    far_a = shift(far[:half], 2, 1)
    far_b = shift(far[half:], 2, -1)
    up_b = shift(up[half:], 2, 1)
    down_a = shift(down[:half], 2, -1)
    up_a = shift(add(up[:half], far_a), 2, 1)
    down_b = shift(add(down[half:], far_b), 2, -1)
    total = jnp.concatenate(
        [add(mine[:half], down_a, up_a), add(mine[half:], up_b, down_b)], axis=0
    )
    out = total[:, :BLOCK].astype(F32)
    for step in (1, 2, 3):
        sent = total[:, step * BLOCK : (step + 1) * BLOCK]
        out = out + lax.ppermute(
            sent, "x", [(i, (i + step) % RING) for i in range(RING)]
        ).astype(F32)
    return out


def inverse_rms(values):
    return lax.rsqrt(jnp.mean(values * values, axis=-1, keepdims=True) + EPSILON)


def rms_back(values, inverse, grad):
    along = jnp.mean(grad * values, axis=-1, keepdims=True)
    return (inverse * grad - values * (inverse * inverse * inverse * along)).astype(BF16)


def dot(a, b, contract=((1,), (0,))):
    return lax.dot_general(a, b, (contract, ((), ())), preferred_element_type=F32)


def per_device(queries, passages, head_weight, send_lists, neg_slots):
    core, x = lax.axis_index("c"), lax.axis_index("x")
    rows_dev, depth = queries.shape
    width = head_weight.shape[1]
    scale = 16.0 / width
    groups, capacity = send_lists.shape[2], send_lists.shape[3]
    slot_count = groups * capacity
    flat_lists = send_lists.reshape(slot_count)

    own_half = lax.dynamic_slice_in_dim(head_weight, core * (width // 2), width // 2, axis=1)
    pieces, places = gather_head(own_half)

    owner = (flat_lists[None, :] == jnp.arange(rows_dev, dtype=jnp.int32)[:, None]).astype(BF16)
    picked = dot(owner, passages, ((0,), (0,))).astype(BF16).reshape(groups, capacity, depth)
    arrived = lax.all_to_all(picked, ("x", "c"), split_axis=0, concat_axis=0, tiled=True)
    arrived = arrived.reshape(slot_count, depth)
    states = jnp.concatenate([queries, passages], axis=0)
    both_states = jnp.concatenate([states, swap(states)], axis=0)
    slot_ids = jnp.arange(slot_count, dtype=jnp.int32)[None, :]
    counts = jnp.zeros((rows_dev, slot_count), F32)
    for j in range(neg_slots.shape[1]):
        counts = counts + (neg_slots[:, j : j + 1] == slot_ids).astype(F32)

    at = jnp.stack(
        [block_at(core, d1, d2) for d1, d2 in places]
        + [block_at(1 - core, d1, d2) for d1, d2 in places]
    )
    side = jnp.concatenate([jnp.full((16,), core), jnp.full((16,), 1 - core)])
    head = place_head(pieces + [swap(piece) for piece in pieces], jnp.stack([at, side]).astype(jnp.int32))

    pre = dot(states, head)
    arrived_pre = dot(arrived, head)
    inverse = inverse_rms(pre)
    emb = (pre * inverse).astype(BF16)
    query_emb, passage_emb = emb[:rows_dev], emb[rows_dev:]
    fetched = (arrived_pre * inverse_rms(arrived_pre)).astype(BF16)

    positive = (
        jnp.sum(query_emb.astype(F32) * passage_emb.astype(F32), axis=1, keepdims=True) * scale
    )
    table = dot(query_emb, fetched, ((1,), (1,))) * scale
    top = jnp.maximum(
        positive, jnp.max(jnp.where(counts > 0, table, -jnp.inf), axis=1, keepdims=True)
    )
    raised = jnp.where(counts > 0, jnp.exp(table - top), 0.0)
    raised_positive = jnp.exp(positive - top)
    whole = raised_positive + jnp.sum(raised * counts, axis=1, keepdims=True)
    first = (raised_positive / whole - 1.0).astype(BF16).astype(F32)
    mixing = ((raised / whole).astype(BF16).astype(F32) * counts).astype(BF16)

    fetched_grad = dot(mixing, query_emb, ((0,), (0,))).astype(BF16)
    returned = lax.all_to_all(
        fetched_grad.reshape(groups, capacity, width),
        ("x", "c"),
        split_axis=0,
        concat_axis=0,
        tiled=True,
    ).reshape(slot_count, width)

    def split(slopes):
        cut = slopes.reshape(slopes.shape[0], RING, 2, BLOCK)
        cut = jnp.concatenate([cut, cut], axis=1)
        cut = lax.dynamic_slice_in_dim(cut, x, RING, axis=1)
        keep = lax.dynamic_index_in_dim(cut, core, 2, keepdims=False)
        send = lax.dynamic_index_in_dim(cut, 1 - core, 2, keepdims=False)
        shape = (slopes.shape[0], RING * BLOCK)
        return keep.reshape(shape), swap(send.reshape(shape))

    query_emb_grad = first * passage_emb.astype(F32) + dot(mixing, fetched)
    query_dy = rms_back(pre[:rows_dev], inverse[:rows_dev], query_emb_grad)
    query_keep, query_other = split(query_dy)
    query_grads = dot(query_dy, head, ((1,), (1,))).astype(BF16)

    passage_emb_grad = first * query_emb.astype(F32) + dot(owner, returned)
    passage_dy = rms_back(pre[rows_dev:], inverse[rows_dev:], passage_emb_grad)
    passage_keep, passage_other = split(passage_dy)
    slopes = jnp.concatenate([query_keep, passage_keep, query_other, passage_other], axis=0)
    head_grads = scatter_head(both_states, slopes, core)
    passage_grads = dot(passage_dy, head, ((1,), (1,))).astype(BF16)
    return (query_grads, passage_grads, head_grads)


def solution(mesh):
    fine = Mesh(mesh.devices.reshape(4, 2, 4, 4), ("x", "c", "y", "z"))
    every = ("x", "c", "y", "z")
    return jax.shard_map(
        per_device,
        mesh=fine,
        in_specs=(
            P(every, None),
            P(every, None),
            P(("y", "z"), None),
            P(("x", "c"), ("y", "z"), None, None),
            P(every, None),
        ),
        out_specs=(P(every, None), P(every, None), P(("y", "z"), ("x", "c"))),
        check_vma=False,
    )
```

```python
import jax
import jax.numpy as jnp
from jax import lax
from jax.experimental import pallas as pl
from jax.experimental.pallas import tpu as pltpu
from jax.sharding import Mesh, PartitionSpec as P

EPSILON = 1e-06
BLOCK = 256
RING = 4
SWAP = [(0, 1), (1, 0)]
BF16 = jnp.bfloat16
F32 = jnp.float32


def shift(value, place, step):
    pairs = []
    for c in range(2):
        for y in range(RING):
            for z in range(RING):
                to_y, to_z = y, z
                if (place == 1) == (c == 0):
                    to_y = (y + step) % RING
                else:
                    to_z = (z + step) % RING
                pairs.append((c * 16 + y * 4 + z, c * 16 + to_y * 4 + to_z))
    return lax.ppermute(value, ("c", "y", "z"), pairs)


def swap(value):
    return lax.ppermute(value, "c", SWAP)


def block_at(core, d1, d2):
    y, z = lax.axis_index("y"), lax.axis_index("z")
    far_y = jnp.where(core == 0, d1, d2)
    far_z = jnp.where(core == 0, d2, d1)
    return ((y + far_y) % RING) * RING + (z + far_z) % RING


def gather_head(own):
    up = shift(own, 1, 1)
    down = shift(own, 1, -1)
    half = own.shape[0] // 2
    first = jnp.concatenate([own, up], axis=0)
    first_up = shift(first, 2, 1)
    first_down = shift(first, 2, -1)
    far_a = shift(up[:half], 1, 1)
    far_b = shift(down[half:], 1, -1)
    second = jnp.concatenate([down, far_a, far_b], axis=0)
    second_up = shift(second, 2, 1)
    second_down = shift(second, 2, -1)
    first_far = shift(first_up, 2, 1)
    second_far = shift(second_down, 2, -1)
    pieces = [first, second, first_up, first_down, second_up, second_down, first_far, second_far]
    a, b = (0, -1), (1, 2)
    places = [(a, 0), (b, 0), (a, -1), (a, 1), (b, -1), (b, 1), (a, 2), (b, 2)]
    return pieces, [(d1, d2) for d1s, d2 in places for d1 in d1s]


def project_kernel(count, last, at_ref, *refs):
    own_ref, arrived_ref = refs[:2]
    pieces = refs[2 : 2 + count]
    rest = refs[2 + count :]
    if last:
        base_ref, counts_ref, _, head_ref, pre_out, inverse_ref, emb_ref, mixing_ref, first_ref, grad_ref = rest[:10]
        held, states, loaded, stored, pre_ref = rest[10:]
    else:
        head_ref, pre_ref, held, states, loaded, stored = rest
    step = pl.program_id(0)
    half = count // 2
    blocks = 2 * half
    rows = own_ref.shape[0]
    width = 1024

    def load(i):
        return pltpu.make_async_copy(
            pieces[i], held.at[i // half, pl.ds((i % half) * 512, 512), :], loaded.at[i]
        )

    def store(k):
        row = pl.multiple_of(at_ref[0, k] * BLOCK, BLOCK)
        col = pl.multiple_of(at_ref[1, k] * width, width)
        return pltpu.make_async_copy(
            held.at[k // blocks, pl.ds((k % blocks) * BLOCK, BLOCK), :],
            head_ref.at[pl.ds(row, BLOCK), pl.ds(col, width)],
            stored.at[k],
        )

    @pl.when(step == 0)
    def _():
        for i in range(count):
            load(i).start()

    for side in range(2):

        @pl.when(step == 4 * side)
        def _(side=side):
            for k in range(blocks):
                col = pl.multiple_of(at_ref[0, side * blocks + k] * BLOCK, BLOCK)
                states[pl.ds(0, rows), pl.ds(k * BLOCK, BLOCK)] = own_ref[:, pl.ds(col, BLOCK)]
                states[pl.ds(rows, rows), pl.ds(k * BLOCK, BLOCK)] = arrived_ref[:, pl.ds(col, BLOCK)]
            for i in range(side * half, (side + 1) * half):
                load(i).wait()
            for k in range(side * blocks, (side + 1) * blocks):
                store(k).start()

    at_col = pl.multiple_of((step % 4) * BLOCK, BLOCK)
    product = jnp.dot(
        states[...], held[step // 4, :, pl.ds(at_col, BLOCK)], preferred_element_type=F32
    )
    if not last:
        pre_ref[...] = product
    else:
        out_col = pl.multiple_of(at_ref[1, (step // 4) * blocks] * width + at_col, BLOCK)
        pre_ref[:, pl.ds(out_col, BLOCK)] = base_ref[...] + product

    @pl.when(step == 7)
    def _():
        if last:
            contrast(counts_ref, pre_ref, pre_out, inverse_ref, emb_ref, mixing_ref, first_ref, grad_ref)
        for k in range(2 * blocks):
            store(k).wait()


def contrast(counts_ref, pre_ref, pre_out, inverse_ref, emb_ref, mixing_ref, first_ref, grad_ref):
    rows = counts_ref.shape[0]
    width = pre_ref.shape[1]
    scale = 16.0 / width
    chunk = 32

    def normalize(i, _):
        at = pl.ds(pl.multiple_of(i * chunk, chunk), chunk)
        values = pre_ref[at, :]
        inverse = lax.rsqrt(jnp.mean(values * values, axis=-1, keepdims=True) + EPSILON)
        emb_ref[at, :] = (values * inverse).astype(BF16)

        @pl.when(i < 2 * rows // chunk)
        def _():
            pre_out[at, :] = values
            inverse_ref[at, :] = jnp.broadcast_to(inverse, (chunk, 128))

        return 0

    lax.fori_loop(0, pre_ref.shape[0] // chunk, normalize, 0)
    query = emb_ref[pl.ds(0, rows), :]
    passage = emb_ref[pl.ds(rows, rows), :]
    fetched = emb_ref[pl.ds(2 * rows, 2 * rows), :]
    positive = (
        jnp.sum(query.astype(F32) * passage.astype(F32), axis=1, keepdims=True) * scale
    )
    table = dot(query, fetched, ((1,), (1,))) * scale
    counts = counts_ref[...]
    top = jnp.maximum(
        positive, jnp.max(jnp.where(counts > 0, table, -1e30), axis=1, keepdims=True)
    )
    raised = jnp.where(counts > 0, jnp.exp(jnp.where(counts > 0, table - top, 0.0)), 0.0)
    raised_positive = jnp.exp(positive - top)
    whole = raised_positive + jnp.sum(raised * counts, axis=1, keepdims=True)
    first = (raised_positive / whole - 1.0).astype(BF16).astype(F32)
    mixing = ((raised / whole).astype(BF16).astype(F32) * counts).astype(BF16)
    first_ref[...] = jnp.broadcast_to(first, (rows, 128))
    mixing_ref[...] = mixing
    grad_ref[...] = dot(mixing, query, ((0,), (0,))).astype(BF16)


def project_first(at, both_states, arrived, pieces):
    count = len(pieces)
    rows = arrived.shape[0]
    return pl.pallas_call(
        lambda *refs: project_kernel(count, False, *refs),
        grid_spec=pltpu.PrefetchScalarGridSpec(
            num_scalar_prefetch=1,
            grid=(8,),
            in_specs=[
                pl.BlockSpec((rows, 4096), lambda g, at: (0, 0)),
                pl.BlockSpec((rows, 4096), lambda g, at: (0, 0)),
            ]
            + [pl.BlockSpec(memory_space=pl.ANY)] * count,
            out_specs=[
                pl.BlockSpec(memory_space=pl.ANY),
                pl.BlockSpec((2 * rows, BLOCK), lambda g, at: (0, at[1, (g // 4) * count] * 4 + g % 4)),
            ],
            scratch_shapes=[
                pltpu.VMEM((2, count // 2 * 512, 1024), BF16),
                pltpu.VMEM((2 * rows, count // 2 * 512), BF16),
                pltpu.SemaphoreType.DMA((count,)),
                pltpu.SemaphoreType.DMA((2 * count,)),
            ],
        ),
        out_shape=[
            jax.ShapeDtypeStruct((4096, 2048), BF16),
            jax.ShapeDtypeStruct((2 * rows, 2048), F32),
        ],
        compiler_params=pltpu.CompilerParams(vmem_limit_bytes=48 * 1024 * 1024),
        name="project_first",
    )(at, both_states, arrived, *pieces)


def project_last(at, both_states, arrived, pieces, base, counts, head):
    count = len(pieces)
    rows = arrived.shape[0]
    half = rows // 2

    def whole(shape):
        return pl.BlockSpec(shape, lambda g, at: (0,) * len(shape))

    return pl.pallas_call(
        lambda *refs: project_kernel(count, True, *refs),
        grid_spec=pltpu.PrefetchScalarGridSpec(
            num_scalar_prefetch=1,
            grid=(8,),
            in_specs=[whole((rows, 4096)), whole((rows, 4096))]
            + [pl.BlockSpec(memory_space=pl.ANY)] * count
            + [
                pl.BlockSpec((2 * rows, BLOCK), lambda g, at: (0, at[1, (g // 4) * count] * 4 + g % 4)),
                whole((half, rows)),
                pl.BlockSpec(memory_space=pl.ANY),
            ],
            out_specs=[
                pl.BlockSpec(memory_space=pl.ANY),
                whole((rows, 2048)),
                whole((rows, 128)),
                whole((2 * rows, 2048)),
                whole((half, rows)),
                whole((half, 128)),
                whole((rows, 2048)),
            ],
            scratch_shapes=[
                pltpu.VMEM((2, count // 2 * 512, 1024), BF16),
                pltpu.VMEM((2 * rows, count // 2 * 512), BF16),
                pltpu.SemaphoreType.DMA((count,)),
                pltpu.SemaphoreType.DMA((2 * count,)),
                pltpu.VMEM((2 * rows, 2048), F32),
            ],
        ),
        out_shape=[
            jax.ShapeDtypeStruct((4096, 2048), BF16),
            jax.ShapeDtypeStruct((rows, 2048), F32),
            jax.ShapeDtypeStruct((rows, 128), F32),
            jax.ShapeDtypeStruct((2 * rows, 2048), BF16),
            jax.ShapeDtypeStruct((half, rows), BF16),
            jax.ShapeDtypeStruct((half, 128), F32),
            jax.ShapeDtypeStruct((rows, 2048), BF16),
        ],
        input_output_aliases={5 + count: 0},
        compiler_params=pltpu.CompilerParams(vmem_limit_bytes=56 * 1024 * 1024),
        name="project_last",
    )(at, both_states, arrived, *pieces, base, counts, head)


def slopes_kernel(cols_ref, pre_ref, inverse_ref, first_ref, other_ref, left_ref, right_ref, out_ref, keep_ref, send_ref, grad_ref):
    chunk = 32
    width = pre_ref.shape[1]
    grad_ref[...] = jnp.dot(left_ref[...], right_ref[...], preferred_element_type=F32)

    def some(i, _):
        at = pl.ds(pl.multiple_of(i * chunk, chunk), chunk)
        grad = first_ref[at, :1] * other_ref[at, :].astype(F32) + grad_ref[at, :]
        values = pre_ref[at, :]
        inverse = inverse_ref[at, :1]
        along = jnp.mean(grad * values, axis=-1, keepdims=True)
        out_ref[at, :] = (inverse * grad - values * (inverse * inverse * inverse * along)).astype(BF16)
        return 0

    lax.fori_loop(0, pre_ref.shape[0] // chunk, some, 0)
    for k in range(width // BLOCK // 2):
        for row, ref in ((0, keep_ref), (1, send_ref)):
            col = pl.multiple_of(cols_ref[row, k] * BLOCK, BLOCK)
            ref[:, pl.ds(k * BLOCK, BLOCK)] = out_ref[:, pl.ds(col, BLOCK)]


def slopes_of(cols, pre, part, inverse, first, emb, other, left, right):
    rows = first.shape[0]
    width = pre.shape[1]

    def whole(shape, at=0):
        return pl.BlockSpec(shape, lambda g, cols: (at, 0))

    return pl.pallas_call(
        slopes_kernel,
        grid_spec=pltpu.PrefetchScalarGridSpec(
            num_scalar_prefetch=1,
            grid=(1,),
            in_specs=[
                whole((rows, width), part),
                whole((rows, 128), part),
                whole((rows, 128)),
                whole((rows, width), other),
                whole(left.shape),
                whole((left.shape[1], width), right[1]),
            ],
            out_specs=[whole((rows, width)), whole((rows, width // 2)), whole((rows, width // 2))],
            scratch_shapes=[pltpu.VMEM((rows, width), F32)],
        ),
        out_shape=[
            jax.ShapeDtypeStruct((rows, width), BF16),
            jax.ShapeDtypeStruct((rows, width // 2), BF16),
            jax.ShapeDtypeStruct((rows, width // 2), BF16),
        ],
        compiler_params=pltpu.CompilerParams(vmem_limit_bytes=32 * 1024 * 1024),
        name="slopes_of",
    )(cols, pre, inverse, first, emb, left, right[0])


def input_grad_kernel(slopes_ref, head_ref, out_ref):
    out_ref[...] = dot(slopes_ref[...], head_ref[...], ((1,), (1,))).astype(BF16)


def input_grad(slopes, head):
    rows, width = slopes.shape
    depth = head.shape[0]
    return pl.pallas_call(
        input_grad_kernel,
        grid=(depth // 512,),
        in_specs=[
            pl.BlockSpec((rows, width), lambda k: (0, 0)),
            pl.BlockSpec((512, width), lambda k: (k, 0)),
        ],
        out_specs=pl.BlockSpec((rows, 512), lambda k: (0, k)),
        out_shape=jax.ShapeDtypeStruct((rows, depth), BF16),
        compiler_params=pltpu.CompilerParams(vmem_limit_bytes=32 * 1024 * 1024),
        name="input_grad",
    )(slopes, head)


def partial_kernel(at_ref, states_ref, slopes_ref, *refs):
    out_ref = refs[-1]
    total = lax.dot_general(
        states_ref[...], slopes_ref[...], (((0,), (0,)), ((), ())), preferred_element_type=F32
    ) * (1.0 / 128.0)
    for ref in refs[:-1]:
        total = total + ref[...].astype(F32)
    out_ref[...] = total.astype(BF16)


def head_partial(states, slopes, at, adds=()):
    count = at.shape[0]
    rows, width = slopes.shape
    return pl.pallas_call(
        partial_kernel,
        grid_spec=pltpu.PrefetchScalarGridSpec(
            num_scalar_prefetch=1,
            grid=(count,),
            in_specs=[
                pl.BlockSpec((rows, BLOCK), lambda k, at: (0, at[k])),
                pl.BlockSpec((rows, width), lambda k, at: (0, 0)),
            ]
            + [pl.BlockSpec((BLOCK, width), lambda k, at: (k, 0))] * len(adds),
            out_specs=pl.BlockSpec((BLOCK, width), lambda k, at: (k, 0)),
        ),
        out_shape=jax.ShapeDtypeStruct((count * BLOCK, width), BF16),
        compiler_params=pltpu.CompilerParams(vmem_limit_bytes=32 * 1024 * 1024),
        name="head_partial",
    )(at, states, slopes, *adds)


def add(*values):
    total = values[0].astype(F32)
    for value in values[1:]:
        total = total + value.astype(F32)
    return total.astype(BF16)


def scatter_head(states, slopes, core, beside):
    def part(d1, d2s, *adds):
        at = jnp.stack([block_at(core, d1, d2) for d2 in d2s]).astype(jnp.int32)
        return head_partial(states, slopes, at, adds)

    a, b = (2, 1), (-1, 0)
    far_a = shift(part(2, a), 1, 1)
    far_b = shift(part(2, b), 1, -1)
    up_b = shift(part(1, b), 1, 1)
    down_a = shift(part(-1, a), 1, -1)
    extra, far_a, far_b = lax.optimization_barrier((beside(), far_a, far_b))
    up_a = shift(part(1, a, far_a), 1, 1)
    down_b = shift(part(-1, b, far_b), 1, -1)
    mine_a = part(0, a, down_a, up_a)
    mine_b = part(0, b, up_b, down_b)
    far, up, down, mine = mine_a[:BLOCK], mine_a[BLOCK:], mine_b[:BLOCK], mine_b[BLOCK:]
    half = BLOCK // 2
    far_a = shift(far[:half], 2, 1)
    far_b = shift(far[half:], 2, -1)
    up_b = shift(up[half:], 2, 1)
    down_a = shift(down[:half], 2, -1)
    up_a = shift(add(up[:half], far_a), 2, 1)
    down_b = shift(add(down[half:], far_b), 2, -1)
    total = jnp.concatenate(
        [add(mine[:half], down_a, up_a), add(mine[half:], up_b, down_b)], axis=0
    )
    out = total[:, :BLOCK].astype(F32)
    for step in (1, 2, 3):
        sent = total[:, step * BLOCK : (step + 1) * BLOCK]
        out = out + lax.ppermute(
            sent, "x", [(i, (i + step) % RING) for i in range(RING)]
        ).astype(F32)
    return out, extra


def dot(a, b, contract=((1,), (0,))):
    return lax.dot_general(a, b, (contract, ((), ())), preferred_element_type=F32)


def per_device(queries, passages, head_weight, send_lists, neg_slots):
    core, x = lax.axis_index("c"), lax.axis_index("x")
    rows_dev, depth = queries.shape
    width = head_weight.shape[1]
    groups, capacity = send_lists.shape[2], send_lists.shape[3]
    slot_count = groups * capacity
    flat_lists = send_lists.reshape(slot_count)

    own_half = lax.dynamic_slice_in_dim(head_weight, core * (width // 2), width // 2, axis=1)
    pieces, places = gather_head(own_half)

    owner = (flat_lists[None, :] == jnp.arange(rows_dev, dtype=jnp.int32)[:, None]).astype(BF16)
    picked = dot(owner, passages, ((0,), (0,))).astype(BF16).reshape(groups, capacity, depth)
    arrived = lax.all_to_all(picked, ("x", "c"), split_axis=0, concat_axis=0, tiled=True)
    arrived = arrived.reshape(slot_count, depth)
    states = jnp.concatenate([queries, passages], axis=0)
    both_states = jnp.concatenate([states, swap(states)], axis=0)
    slot_ids = jnp.arange(slot_count, dtype=jnp.int32)[None, :]
    counts = jnp.zeros((rows_dev, slot_count), F32)
    for j in range(neg_slots.shape[1]):
        counts = counts + (neg_slots[:, j : j + 1] == slot_ids).astype(F32)

    def places_of(some):
        at = [block_at(core, d1, d2) for d1, d2 in some] + [block_at(1 - core, d1, d2) for d1, d2 in some]
        side = [core] * len(some) + [1 - core] * len(some)
        return jnp.stack([jnp.stack(at), jnp.stack(side)]).astype(jnp.int32)

    early, late = pieces[:6], pieces[6:]
    early = early + [swap(piece) for piece in early]
    head, base = project_first(places_of(places[:12]), both_states, arrived, early)
    late = late + [swap(piece) for piece in late]
    head, pre, inverse, emb, mixing, first, fetched_grad = project_last(
        places_of(places[12:]), both_states, arrived, late, base, counts, head
    )
    returned = lax.all_to_all(
        fetched_grad.reshape(groups, capacity, width),
        ("x", "c"),
        split_axis=0,
        concat_axis=0,
        tiled=True,
    ).reshape(slot_count, width)

    to_x = [(x + step) % RING for step in range(RING)]
    cols = jnp.stack(
        [jnp.stack([2 * to + core for to in to_x]), jnp.stack([2 * to + 1 - core for to in to_x])]
    ).astype(jnp.int32)
    query_dy, query_keep, query_send = slopes_of(cols, pre, 0, inverse, first, emb, 1, mixing, (emb, 1))
    query_other = swap(query_send)
    query_grads = input_grad(query_dy, head)
    returned, query_grads, query_other = lax.optimization_barrier((returned, query_grads, query_other))

    passage_dy, passage_keep, passage_send = slopes_of(
        cols, pre, 1, inverse, first, emb, 0, owner, (returned, 0)
    )
    passage_other = swap(passage_send)
    slopes = jnp.concatenate([query_keep, passage_keep, query_other, passage_other], axis=0)
    head_grads, passage_grads = scatter_head(
        both_states, slopes, core, lambda: input_grad(passage_dy, head)
    )
    return (query_grads, passage_grads, head_grads)


def solution(mesh):
    fine = Mesh(mesh.devices.reshape(4, 2, 4, 4), ("x", "c", "y", "z"))
    every = ("x", "c", "y", "z")
    return jax.shard_map(
        per_device,
        mesh=fine,
        in_specs=(
            P(every, None),
            P(every, None),
            P(("y", "z"), None),
            P(("x", "c"), ("y", "z"), None, None),
            P(every, None),
        ),
        out_specs=(P(every, None), P(every, None), P(("y", "z"), ("x", "c"))),
        check_vma=False,
    )
```

```python
import jax
import jax.numpy as jnp
from jax import lax
from jax.experimental import pallas as pl
from jax.experimental.pallas import tpu as pltpu
from jax.sharding import Mesh, PartitionSpec as P

EPSILON = 1e-06
BLOCK = 256
RING = 4
SWAP = [(0, 1), (1, 0)]
BF16 = jnp.bfloat16
F32 = jnp.float32


def shift(value, place, step):
    pairs = []
    for c in range(2):
        for y in range(RING):
            for z in range(RING):
                to_y, to_z = y, z
                if (place == 1) == (c == 0):
                    to_y = (y + step) % RING
                else:
                    to_z = (z + step) % RING
                pairs.append((c * 16 + y * 4 + z, c * 16 + to_y * 4 + to_z))
    return lax.ppermute(value, ("c", "y", "z"), pairs)


def swap(value):
    return lax.ppermute(value, "c", SWAP)


def block_at(core, d1, d2):
    y, z = lax.axis_index("y"), lax.axis_index("z")
    far_y = jnp.where(core == 0, d1, d2)
    far_z = jnp.where(core == 0, d2, d1)
    return ((y + far_y) % RING) * RING + (z + far_z) % RING


def together(*values):
    return lax.optimization_barrier(values)


def project_kernel(count, kind, at_ref, own_ref, arrived_ref, *refs):
    pieces, rest = refs[:count], refs[count:]
    if kind == "first":
        head_ref, pre_ref, states, stored = rest
    elif kind == "middle":
        base_ref, _, head_ref, pre_ref, states, stored = rest
    else:
        base_ref, counts_ref, _, head_ref, pre_ref, *outs, states, stored = rest
    half = count // 2
    blocks = 2 * half
    rows = arrived_ref.shape[0]
    width = 1024

    def store(k):
        row = pl.multiple_of(at_ref[0, k] * BLOCK, BLOCK)
        col = pl.multiple_of(at_ref[1, k] * width, width)
        return pltpu.make_async_copy(
            pieces[k // 2].at[pl.ds((k % 2) * BLOCK, BLOCK), :],
            head_ref.at[pl.ds(row, BLOCK), pl.ds(col, width)],
            stored.at[k],
        )

    for k in range(2 * blocks):
        store(k).start()
    for side in range(2):
        for k in range(blocks):
            col = pl.multiple_of(at_ref[0, side * blocks + k] * BLOCK, BLOCK)
            states[pl.ds(0, rows), pl.ds(k * BLOCK, BLOCK)] = own_ref[pl.ds(0, rows), pl.ds(col, BLOCK)]
            states[pl.ds(rows, rows), pl.ds(k * BLOCK, BLOCK)] = arrived_ref[:, pl.ds(col, BLOCK)]

        def strip(n, _, side=side):
            at_col = pl.multiple_of(n * BLOCK, BLOCK)
            out_col = pl.multiple_of(at_ref[1, side * blocks] * width + at_col, BLOCK)
            total = None
            for i in range(half):
                product = jnp.dot(
                    states[:, pl.ds(i * 512, 512)],
                    pieces[side * half + i][:, pl.ds(at_col, BLOCK)],
                    preferred_element_type=F32,
                )
                total = product if total is None else total + product
            if kind != "first":
                total = total + base_ref[:, pl.ds(out_col, BLOCK)]
            pre_ref[:, pl.ds(out_col, BLOCK)] = total
            return 0

        lax.fori_loop(0, width // BLOCK, strip, 0)
    if kind == "last":
        contrast(counts_ref, pre_ref, *outs)
    for k in range(2 * blocks):
        store(k).wait()


def contrast(counts_ref, pre_ref, inverse_ref, emb_ref, mixing_ref, first_ref, grad_ref):
    rows = counts_ref.shape[0]
    width = pre_ref.shape[1]
    scale = 16.0 / width
    chunk = 32

    def normalize(i, _):
        at = pl.ds(pl.multiple_of(i * chunk, chunk), chunk)
        values = pre_ref[at, :]
        inverse = lax.rsqrt(jnp.mean(values * values, axis=-1, keepdims=True) + EPSILON)
        emb_ref[at, :] = (values * inverse).astype(BF16)

        @pl.when(i < 2 * rows // chunk)
        def _():
            inverse_ref[at, :] = jnp.broadcast_to(inverse, (chunk, 128))

        return 0

    lax.fori_loop(0, pre_ref.shape[0] // chunk, normalize, 0)
    query = emb_ref[pl.ds(0, rows), :]
    passage = emb_ref[pl.ds(rows, rows), :]
    fetched = emb_ref[pl.ds(2 * rows, 2 * rows), :]
    positive = (
        jnp.sum(query.astype(F32) * passage.astype(F32), axis=1, keepdims=True) * scale
    )
    table = dot(query, fetched, ((1,), (1,))) * scale
    counts = counts_ref[...]
    top = jnp.maximum(
        positive, jnp.max(jnp.where(counts > 0, table, -1e30), axis=1, keepdims=True)
    )
    raised = jnp.where(counts > 0, jnp.exp(jnp.where(counts > 0, table - top, 0.0)), 0.0)
    raised_positive = jnp.exp(positive - top)
    whole = raised_positive + jnp.sum(raised * counts, axis=1, keepdims=True)
    first = (raised_positive / whole - 1.0).astype(BF16).astype(F32)
    mixing = ((raised / whole).astype(BF16).astype(F32) * counts).astype(BF16)
    first_ref[...] = jnp.broadcast_to(first, (rows, 128))
    mixing_ref[...] = mixing
    grad_ref[...] = dot(mixing, query, ((0,), (0,))).astype(BF16)


def vmem(count):
    return [pl.BlockSpec(memory_space=pltpu.VMEM)] * count


def project(kind, at, both_states, arrived, pieces, *more):
    count = len(pieces)
    rows = arrived.shape[0]
    half = rows // 2
    anywhere = pl.BlockSpec(memory_space=pl.ANY)
    ins = [pl.BlockSpec(memory_space=pltpu.SMEM)] + vmem(2 + count)
    outs = [anywhere] + vmem(1)
    types = [
        jax.ShapeDtypeStruct((4096, 2048), BF16),
        jax.ShapeDtypeStruct((2 * rows, 2048), F32),
    ]
    aliases = {}
    if kind != "first":
        ins += vmem(1 if kind == "middle" else 2) + [anywhere]
        aliases = {3 + count: 1, len(ins) - 1: 0}
    if kind == "last":
        outs += vmem(5)
        for shape, dtype in (
            ((rows, 128), F32),
            ((2 * rows, 2048), BF16),
            ((half, rows), BF16),
            ((half, 128), F32),
            ((rows, 2048), BF16),
        ):
            types.append(jax.ShapeDtypeStruct(shape, dtype))
    return pl.pallas_call(
        lambda *refs: project_kernel(count, kind, *refs),
        in_specs=ins,
        out_specs=outs,
        out_shape=types,
        scratch_shapes=[
            pltpu.VMEM((2 * rows, count // 2 * 512), BF16),
            pltpu.SemaphoreType.DMA((2 * count,)),
        ],
        input_output_aliases=aliases,
        compiler_params=pltpu.CompilerParams(vmem_limit_bytes=28 * 1024 * 1024),
        name="project_" + kind,
    )(at, both_states, arrived, *pieces, *more)


def slopes_kernel(part, cols_ref, pre_ref, inverse_ref, first_ref, emb_ref, left_ref, right_ref, out_ref, keep_ref, send_ref, grad_ref):
    rows, chunk = out_ref.shape[0], 32
    width = pre_ref.shape[1]
    depth = left_ref.shape[1]
    right = right_ref[pl.ds(2 * rows, depth), :] if part == 0 else right_ref[...]
    grad_ref[...] = jnp.dot(left_ref[...], right, preferred_element_type=F32)

    def some(i, _):
        at = pl.ds(pl.multiple_of(i * chunk, chunk), chunk)
        mine = pl.ds(pl.multiple_of(part * rows + i * chunk, chunk), chunk)
        other = pl.ds(pl.multiple_of((1 - part) * rows + i * chunk, chunk), chunk)
        grad = first_ref[at, :1] * emb_ref[other, :].astype(F32) + grad_ref[at, :]
        values = pre_ref[mine, :]
        inverse = inverse_ref[mine, :1]
        along = jnp.mean(grad * values, axis=-1, keepdims=True)
        out_ref[at, :] = (inverse * grad - values * (inverse * inverse * inverse * along)).astype(BF16)
        return 0

    lax.fori_loop(0, rows // chunk, some, 0)
    for k in range(width // BLOCK // 2):
        for row, ref in ((0, keep_ref), (1, send_ref)):
            col = pl.multiple_of(cols_ref[row, k] * BLOCK, BLOCK)
            ref[:, pl.ds(k * BLOCK, BLOCK)] = out_ref[:, pl.ds(col, BLOCK)]


def slopes_of(part, cols, pre, inverse, first, emb, left, right):
    rows = first.shape[0]
    width = pre.shape[1]
    return pl.pallas_call(
        lambda *refs: slopes_kernel(part, *refs),
        in_specs=[pl.BlockSpec(memory_space=pltpu.SMEM)] + vmem(6),
        out_specs=vmem(3),
        out_shape=[
            jax.ShapeDtypeStruct((rows, width), BF16),
            jax.ShapeDtypeStruct((rows, width // 2), BF16),
            jax.ShapeDtypeStruct((rows, width // 2), BF16),
        ],
        scratch_shapes=[pltpu.VMEM((rows, width), F32)],
        compiler_params=pltpu.CompilerParams(vmem_limit_bytes=16 * 1024 * 1024),
        name="slopes_of",
    )(cols, pre, inverse, first, emb, left, right)


def input_grad_kernel(slopes_ref, head_ref, out_ref):
    out_ref[...] = dot(slopes_ref[...], head_ref[...], ((1,), (1,))).astype(BF16)


def input_grad(slopes, head):
    rows, width = slopes.shape
    depth = head.shape[0]
    return pl.pallas_call(
        input_grad_kernel,
        grid=(depth // 512,),
        in_specs=[
            pl.BlockSpec((rows, width), lambda k: (0, 0)),
            pl.BlockSpec((512, width), lambda k: (k, 0)),
        ],
        out_specs=pl.BlockSpec((rows, 512), lambda k: (0, k)),
        out_shape=jax.ShapeDtypeStruct((rows, depth), BF16),
        compiler_params=pltpu.CompilerParams(vmem_limit_bytes=16 * 1024 * 1024),
        name="input_grad",
    )(slopes, pltpu.with_memory_space_constraint(head, pltpu.HBM))


def partial_kernel(outs, adds, at_ref, states_ref, slopes_ref, *refs):
    for k in range(outs * 2):
        row = pl.multiple_of(at_ref[k] * BLOCK, BLOCK)
        part = pl.ds(k % 2 * BLOCK, BLOCK)
        total = jnp.dot(
            states_ref[pl.ds(row, BLOCK), :], slopes_ref[...], preferred_element_type=F32
        ) * (1.0 / 128.0)
        for ref in refs[k // 2 * adds : (k // 2 + 1) * adds]:
            total = total + ref[part, :].astype(F32)
        refs[outs * adds + k // 2][part, :] = total.astype(BF16)


def head_partial(states, slopes, at, adds):
    outs, width = len(adds), slopes.shape[1]
    return pl.pallas_call(
        lambda *refs: partial_kernel(outs, len(adds[0]), *refs),
        in_specs=[pl.BlockSpec(memory_space=pltpu.SMEM)] + vmem(2 + outs * len(adds[0])),
        out_specs=vmem(outs),
        out_shape=[jax.ShapeDtypeStruct((2 * BLOCK, width), BF16)] * outs,
        compiler_params=pltpu.CompilerParams(vmem_limit_bytes=16 * 1024 * 1024),
        name="head_partial",
    )(at, states, slopes, *[value for some in adds for value in some])


def add(*values):
    total = values[0].astype(F32)
    for value in values[1:]:
        total = total + value.astype(F32)
    return total.astype(BF16)


def scatter_head(states, slopes, core, beside, given):
    def part(d1s, d2s, adds):
        at = [block_at(core, d1, d2) for d1, some in zip(d1s, d2s) for d2 in some]
        return head_partial(states, slopes, jnp.stack(at).astype(jnp.int32), adds)

    a, b = (2, 1), (-1, 0)
    far_a, far_b = part((2, 2), (a, b), ((), ()))
    far_a, far_b = shift(far_a, 1, 1), shift(far_b, 1, -1)
    up_b, down_a = part((1, -1), (b, a), ((), ()))
    up_b, down_a, given = together(up_b, down_a, given)
    up_b, down_a = shift(up_b, 1, 1), shift(down_a, 1, -1)
    extra = beside(given)
    far_a, far_b, extra = together(far_a, far_b, extra)
    up_a, down_b = part((1, -1), (a, b), ((far_a,), (far_b,)))
    up_a, down_b = shift(up_a, 1, 1), shift(down_b, 1, -1)
    mine_a, mine_b = part((0, 0), (a, b), ((down_a,), (up_b,)))
    up_a, down_b, mine_a, mine_b = together(up_a, down_b, mine_a, mine_b)
    half = BLOCK // 2
    far, up = mine_a[:BLOCK], mine_a[BLOCK:]
    down, mine = mine_b[:BLOCK], mine_b[BLOCK:]
    up_far, up_up = up_a[:BLOCK], up_a[BLOCK:]
    down_down, down_mine = down_b[:BLOCK], down_b[BLOCK:]
    far_a = shift(add(far[:half], up_far[:half]), 2, 1)
    far_b = shift(add(far[half:], up_far[half:]), 2, -1)
    up_b = shift(add(up[half:], up_up[half:]), 2, 1)
    down_a = shift(add(down[:half], down_down[:half]), 2, -1)
    far_a, far_b, up_b, down_a = together(far_a, far_b, up_b, down_a)
    up_a = shift(add(up[:half], up_up[:half], far_a), 2, 1)
    down_b = shift(add(down[half:], down_down[half:], far_b), 2, -1)
    up_a, down_b = together(up_a, down_b)
    total = jnp.concatenate(
        [
            add(mine[:half], down_mine[:half], down_a, up_a),
            add(mine[half:], down_mine[half:], up_b, down_b),
        ],
        axis=0,
    )
    arrived = together(
        *[
            lax.ppermute(
                total[:, step * BLOCK : (step + 1) * BLOCK],
                "x",
                [(i, (i + step) % RING) for i in range(RING)],
            )
            for step in (1, 2, 3)
        ]
    )
    out = total[:, :BLOCK].astype(F32)
    for value in arrived:
        out = out + value.astype(F32)
    return out, extra


def dot(a, b, contract=((1,), (0,))):
    return lax.dot_general(a, b, (contract, ((), ())), preferred_element_type=F32)


def per_device(queries, passages, head_weight, send_lists, neg_slots):
    core, x = lax.axis_index("c"), lax.axis_index("x")
    rows_dev, depth = queries.shape
    width = head_weight.shape[1]
    groups, capacity = send_lists.shape[2], send_lists.shape[3]
    slot_count = groups * capacity
    flat_lists = send_lists.reshape(slot_count)

    def places_of(*pieces):
        places = [(d1, d2) for d1s, d2 in pieces for d1 in d1s]
        at = [block_at(core, d1, d2) for d1, d2 in places] + [block_at(1 - core, d1, d2) for d1, d2 in places]
        side = [core] * len(places) + [1 - core] * len(places)
        return jnp.stack([jnp.stack(at), jnp.stack(side)]).astype(jnp.int32)

    a, b = (0, -1), (1, 2)
    states = jnp.concatenate([queries, passages], axis=0)
    owner = (flat_lists[None, :] == jnp.arange(rows_dev, dtype=jnp.int32)[:, None]).astype(BF16)
    own = lax.dynamic_slice_in_dim(head_weight, core * (width // 2), width // 2, axis=1)

    up, down = shift(own, 1, 1), shift(own, 1, -1)
    picked = dot(owner, passages, ((0,), (0,))).astype(BF16).reshape(groups, capacity, depth)
    up, down, picked = together(up, down, picked)
    arrived = lax.all_to_all(picked, ("x", "c"), split_axis=0, concat_axis=0, tiled=True)
    arrived = arrived.reshape(slot_count, depth)

    first = jnp.concatenate([own, up], axis=0)
    first_up, first_down = shift(first, 2, 1), shift(first, 2, -1)
    half = BLOCK // 2
    far_a, far_b = shift(up[:half], 1, 1), shift(down[half:], 1, -1)
    first_up, first_down, far_a, far_b = together(first_up, first_down, far_a, far_b)

    second = jnp.concatenate([down, far_a, far_b], axis=0)
    second_up, second_down = shift(second, 2, 1), shift(second, 2, -1)
    early = [first, second, first_up, first_down]
    early = early + [swap(piece) for piece in early]
    both_states = jnp.concatenate([states, swap(states)], axis=0)
    turned = both_states.T
    slot_ids = jnp.arange(slot_count, dtype=jnp.int32)[None, :]
    counts = jnp.zeros((rows_dev, slot_count), F32)
    for j in range(neg_slots.shape[1]):
        counts = counts + (neg_slots[:, j : j + 1] == slot_ids).astype(F32)
    second_up, second_down, arrived, first_up = together(second_up, second_down, arrived, first_up)

    first_far, second_far = shift(first_up, 2, 1), shift(second_down, 2, -1)
    head, pre = project(
        "first", places_of((a, 0), (b, 0), (a, -1), (a, 1)), both_states, arrived, early
    )
    middle = [second_up, second_down, swap(second_up), swap(second_down)]
    head, pre = project("middle", places_of((b, -1), (b, 1)), both_states, arrived, middle, pre, head)
    first_far, second_far, pre, counts, turned = together(first_far, second_far, pre, counts, turned)
    late = [first_far, second_far, swap(first_far), swap(second_far)]
    head, pre, inverse, emb, mixing, first, fetched_grad = project(
        "last", places_of((a, 2), (b, 2)), both_states, arrived, late, pre, counts, head
    )
    returned = lax.all_to_all(
        fetched_grad.reshape(groups, capacity, width),
        ("x", "c"),
        split_axis=0,
        concat_axis=0,
        tiled=True,
    ).reshape(slot_count, width)

    to_x = [(x + step) % RING for step in range(RING)]
    cols = jnp.stack(
        [jnp.stack([2 * to + core for to in to_x]), jnp.stack([2 * to + 1 - core for to in to_x])]
    ).astype(jnp.int32)
    query_dy, query_keep, query_send = slopes_of(0, cols, pre, inverse, first, emb, mixing, emb)
    query_other = swap(query_send)
    query_grads = input_grad(query_dy, head)
    returned, query_grads, query_other = lax.optimization_barrier((returned, query_grads, query_other))

    passage_dy, passage_keep, passage_send = slopes_of(
        1, cols, pre, inverse, first, emb, owner, returned
    )
    passage_other = swap(passage_send)
    slopes = jnp.concatenate([query_keep, passage_keep, query_other, passage_other], axis=0)
    head_grads, passage_grads = scatter_head(
        turned, slopes, core, lambda slopes: input_grad(slopes, head), passage_dy
    )
    return (query_grads, passage_grads, head_grads)


def solution(mesh):
    fine = Mesh(mesh.devices.reshape(4, 2, 4, 4), ("x", "c", "y", "z"))
    every = ("x", "c", "y", "z")
    return jax.shard_map(
        per_device,
        mesh=fine,
        in_specs=(
            P(every, None),
            P(every, None),
            P(("y", "z"), None),
            P(("x", "c"), ("y", "z"), None, None),
            P(every, None),
        ),
        out_specs=(P(every, None), P(every, None), P(("y", "z"), ("x", "c"))),
        check_vma=False,
    )
```

```python
import jax
import jax.numpy as jnp
from jax import lax
from jax.experimental import pallas as pl
from jax.experimental.pallas import tpu as pltpu
from jax.sharding import Mesh, PartitionSpec as P

EPSILON = 1e-06
BLOCK = 256
RING = 4
SWAP = [(0, 1), (1, 0)]
BF16 = jnp.bfloat16
F32 = jnp.float32


def shift(value, place, step):
    pairs = []
    for c in range(2):
        for y in range(RING):
            for z in range(RING):
                to_y, to_z = y, z
                if (place == 1) == (c == 0):
                    to_y = (y + step) % RING
                else:
                    to_z = (z + step) % RING
                pairs.append((c * 16 + y * 4 + z, c * 16 + to_y * 4 + to_z))
    return lax.ppermute(value, ("c", "y", "z"), pairs)


def swap(value):
    return lax.ppermute(value, "c", SWAP)


def block_at(core, d1, d2):
    y, z = lax.axis_index("y"), lax.axis_index("z")
    far_y = jnp.where(core == 0, d1, d2)
    far_z = jnp.where(core == 0, d2, d1)
    return ((y + far_y) % RING) * RING + (z + far_z) % RING


def together(*values):
    return lax.optimization_barrier(values)


def turn_kernel(*refs):
    turned_ref = refs[-1]
    rows = refs[0].shape[0]

    def block(k, _):
        at = pl.ds(pl.multiple_of(k * BLOCK, BLOCK), BLOCK)
        part = jnp.concatenate([ref[:, at] for ref in refs[:-1]], axis=0)
        turned_ref[at, :] = part.T
        return 0

    lax.fori_loop(0, refs[0].shape[1] // BLOCK, block, 0)


def turn(*states):
    rows, depth = states[0].shape
    return pl.pallas_call(
        turn_kernel,
        in_specs=vmem(len(states)),
        out_specs=vmem(1)[0],
        out_shape=jax.ShapeDtypeStruct((depth, rows * len(states)), BF16),
        compiler_params=pltpu.CompilerParams(vmem_limit_bytes=20 * 1024 * 1024),
        name="turn",
    )(*states)


def project_kernel(xs, count, store_all, bases, finish, at_ref, *refs):
    x_refs, refs = refs[:xs], refs[xs:]
    pieces, refs = refs[:count], refs[count:]
    base_refs, refs = refs[:bases], refs[bases:]
    if finish:
        counts_ref, refs = refs[0], refs[1:]
    if store_all:
        if bases:
            refs = refs[1:]
        head_ref, refs = refs[0], refs[1:]
    outs = max(bases, 1)
    pre_refs, refs = refs[:outs], refs[outs:]
    states, stored = refs[-2:]
    half = count // 2
    blocks = 2 * half
    width = 1024

    def store(k):
        row = pl.multiple_of(at_ref[0, k] * BLOCK, BLOCK)
        col = pl.multiple_of(at_ref[1, k] * width, width)
        return pltpu.make_async_copy(
            pieces[k // 2].at[pl.ds((k % 2) * BLOCK, BLOCK), :],
            head_ref.at[pl.ds(row, BLOCK), pl.ds(col, width)],
            stored.at[k],
        )

    if store_all:
        for k in range(2 * blocks):
            store(k).start()
    for side in range(2):
        for k in range(blocks):
            col = pl.multiple_of(at_ref[0, side * blocks + k] * BLOCK, BLOCK)
            row = 0
            for ref in x_refs:
                states[pl.ds(row, ref.shape[0]), pl.ds(k * BLOCK, BLOCK)] = ref[:, pl.ds(col, BLOCK)]
                row += ref.shape[0]

        def strip(n, _, side=side):
            at_col = pl.multiple_of(n * BLOCK, BLOCK)
            out_col = pl.multiple_of(at_ref[1, side * blocks] * width + at_col, BLOCK)
            total = None
            for i in range(half):
                product = jnp.dot(
                    states[:, pl.ds(i * 512, 512)],
                    pieces[side * half + i][:, pl.ds(at_col, BLOCK)],
                    preferred_element_type=F32,
                )
                total = product if total is None else total + product
            row = 0
            for i, pre_ref in enumerate(pre_refs):
                rows = pre_ref.shape[0]
                part = total[row : row + rows]
                if bases:
                    part = part + base_refs[i][:, pl.ds(out_col, BLOCK)]
                pre_ref[:, pl.ds(out_col, BLOCK)] = part
                row += rows
            return 0

        lax.fori_loop(0, width // BLOCK, strip, 0)
    if finish:
        contrast(counts_ref, *pre_refs, *refs[:-2])
    if store_all:
        for k in range(2 * blocks):
            store(k).wait()


def contrast(counts_ref, pre_ref, arrived_ref, inverse_ref, emb_ref, mixing_ref, first_ref, grad_ref):
    rows = counts_ref.shape[0]
    width = pre_ref.shape[1]
    scale = 16.0 / width
    chunk = 32

    def normalize(i, _):
        at = pl.ds(pl.multiple_of(i * chunk, chunk), chunk)
        after = pl.ds(pl.multiple_of(2 * rows + i * chunk, chunk), chunk)
        values = pre_ref[at, :]
        inverse = lax.rsqrt(jnp.mean(values * values, axis=-1, keepdims=True) + EPSILON)
        emb_ref[at, :] = (values * inverse).astype(BF16)
        inverse_ref[at, :] = jnp.broadcast_to(inverse, (chunk, 128))
        values = arrived_ref[at, :]
        inverse = lax.rsqrt(jnp.mean(values * values, axis=-1, keepdims=True) + EPSILON)
        emb_ref[after, :] = (values * inverse).astype(BF16)
        return 0

    lax.fori_loop(0, 2 * rows // chunk, normalize, 0)
    query = emb_ref[pl.ds(0, rows), :]
    passage = emb_ref[pl.ds(rows, rows), :]
    fetched = emb_ref[pl.ds(2 * rows, 2 * rows), :]
    positive = (
        jnp.sum(query.astype(F32) * passage.astype(F32), axis=1, keepdims=True) * scale
    )
    table = dot(query, fetched, ((1,), (1,))) * scale
    counts = counts_ref[...]
    top = jnp.maximum(
        positive, jnp.max(jnp.where(counts > 0, table, -1e30), axis=1, keepdims=True)
    )
    raised = jnp.where(counts > 0, jnp.exp(jnp.where(counts > 0, table - top, 0.0)), 0.0)
    raised_positive = jnp.exp(positive - top)
    whole = raised_positive + jnp.sum(raised * counts, axis=1, keepdims=True)
    first = (raised_positive / whole - 1.0).astype(BF16).astype(F32)
    mixing = ((raised / whole).astype(BF16).astype(F32) * counts).astype(BF16)
    first_ref[...] = jnp.broadcast_to(first, (rows, 128))
    mixing_ref[...] = mixing
    grad_ref[...] = dot(mixing, query, ((0,), (0,))).astype(BF16)


def vmem(count):
    return [pl.BlockSpec(memory_space=pltpu.VMEM)] * count


def near(shape, dtype):
    return pltpu.VMEM(shape, dtype)


def keep_near(*values):
    return [pltpu.with_memory_space_constraint(value, pltpu.VMEM) for value in values]


def project(at, xs, pieces, bases=(), head=None, store=True, counts=None):
    count = len(pieces)
    sizes = [base.shape[0] for base in bases] or [sum(x.shape[0] for x in xs)]
    finish = counts is not None
    anywhere = pl.BlockSpec(memory_space=pl.ANY)
    ins = [pl.BlockSpec(memory_space=pltpu.SMEM)] + vmem(len(xs) + count + len(bases) + finish)
    args = [at, *xs, *pieces, *keep_near(*bases)] + ([counts] if finish else [])
    aliases = {1 + len(xs) + count + i: int(store) + i for i in range(len(bases))}
    outs, types = vmem(len(sizes)), [near((size, 2048), F32) for size in sizes]
    if store:
        outs, types = [anywhere] + outs, [jax.ShapeDtypeStruct((4096, 2048), BF16)] + types
        if bases:
            aliases[len(args)] = 0
            args.append(head)
            ins.append(anywhere)
    if finish:
        rows = sizes[0]
        outs += vmem(5)
        types += [
            near((rows, 128), F32),
            near((2 * rows, 2048), BF16),
            near((rows // 2, rows), BF16),
            near((rows // 2, 128), F32),
            jax.ShapeDtypeStruct((rows, 2048), BF16),
        ]
    return pl.pallas_call(
        lambda *refs: project_kernel(len(xs), count, store, len(bases), finish, *refs),
        in_specs=ins,
        out_specs=outs,
        out_shape=types,
        scratch_shapes=[
            pltpu.VMEM((sum(sizes), count // 2 * 512), BF16),
            pltpu.SemaphoreType.DMA((2 * count,)),
        ],
        input_output_aliases=aliases,
        compiler_params=pltpu.CompilerParams(vmem_limit_bytes=24 * 1024 * 1024),
        name="project",
    )(*args)


def slopes_kernel(part, cols_ref, pre_ref, inverse_ref, first_ref, emb_ref, left_ref, right_ref, out_ref, keep_ref, send_ref, grad_ref):
    rows, chunk = out_ref.shape[0], 32
    width = pre_ref.shape[1]
    depth = left_ref.shape[1]
    right = right_ref[pl.ds(2 * rows, depth), :] if part == 0 else right_ref[...]
    grad_ref[...] = jnp.dot(left_ref[...], right, preferred_element_type=F32)

    def some(i, _):
        at = pl.ds(pl.multiple_of(i * chunk, chunk), chunk)
        mine = pl.ds(pl.multiple_of(part * rows + i * chunk, chunk), chunk)
        other = pl.ds(pl.multiple_of((1 - part) * rows + i * chunk, chunk), chunk)
        grad = first_ref[at, :1] * emb_ref[other, :].astype(F32) + grad_ref[at, :]
        values = pre_ref[mine, :]
        inverse = inverse_ref[mine, :1]
        along = jnp.mean(grad * values, axis=-1, keepdims=True)
        out_ref[at, :] = (inverse * grad - values * (inverse * inverse * inverse * along)).astype(BF16)
        return 0

    lax.fori_loop(0, rows // chunk, some, 0)
    for k in range(width // BLOCK // 2):
        for row, ref in ((0, keep_ref), (1, send_ref)):
            col = pl.multiple_of(cols_ref[row, k] * BLOCK, BLOCK)
            ref[:, pl.ds(k * BLOCK, BLOCK)] = out_ref[:, pl.ds(col, BLOCK)]


def slopes_of(part, cols, pre, inverse, first, emb, left, right):
    rows = first.shape[0]
    width = pre.shape[1]
    return pl.pallas_call(
        lambda *refs: slopes_kernel(part, *refs),
        in_specs=[pl.BlockSpec(memory_space=pltpu.SMEM)] + vmem(6),
        out_specs=vmem(3),
        out_shape=[
            jax.ShapeDtypeStruct((rows, width), BF16),
            jax.ShapeDtypeStruct((rows, width // 2), BF16),
            jax.ShapeDtypeStruct((rows, width // 2), BF16),
        ],
        scratch_shapes=[pltpu.VMEM((rows, width), F32)],
        compiler_params=pltpu.CompilerParams(vmem_limit_bytes=16 * 1024 * 1024),
        name="slopes_of",
    )(cols, *keep_near(pre, inverse, first, emb), left, right)


def input_grad_kernel(slopes_ref, head_ref, *refs):
    refs[-1][...] = dot(slopes_ref[...], head_ref[...], ((1,), (1,))).astype(BF16)


def input_grad(slopes, head, part, filled=None):
    rows, width = slopes.shape
    depth = head.shape[0]
    steps = depth // 512 // 2
    more = [] if filled is None else [filled]
    return pl.pallas_call(
        input_grad_kernel,
        grid=(steps,),
        in_specs=[
            pl.BlockSpec((rows, width), lambda k: (0, 0)),
            pl.BlockSpec((512, width), lambda k: (k + part * steps, 0)),
        ]
        + [pl.BlockSpec(memory_space=pl.ANY)] * len(more),
        out_specs=pl.BlockSpec((rows, 512), lambda k: (0, k + part * steps)),
        out_shape=jax.ShapeDtypeStruct((rows, depth), BF16),
        input_output_aliases={2: 0} if more else {},
        compiler_params=pltpu.CompilerParams(vmem_limit_bytes=16 * 1024 * 1024),
        name="input_grad",
    )(slopes, pltpu.with_memory_space_constraint(head, pltpu.HBM), *more)


def partial_kernel(outs, adds, at_ref, states_ref, slopes_ref, *refs):
    for k in range(outs * 2):
        row = pl.multiple_of(at_ref[k] * BLOCK, BLOCK)
        part = pl.ds(k % 2 * BLOCK, BLOCK)
        total = jnp.dot(
            states_ref[pl.ds(row, BLOCK), :], slopes_ref[...], preferred_element_type=F32
        ) * (1.0 / 128.0)
        for ref in refs[k // 2 * adds : (k // 2 + 1) * adds]:
            total = total + ref[part, :].astype(F32)
        refs[outs * adds + k // 2][part, :] = total.astype(BF16)


def head_partial(states, slopes, at, adds):
    outs, width = len(adds), slopes.shape[1]
    return pl.pallas_call(
        lambda *refs: partial_kernel(outs, len(adds[0]), *refs),
        in_specs=[pl.BlockSpec(memory_space=pltpu.SMEM)] + vmem(2 + outs * len(adds[0])),
        out_specs=vmem(outs),
        out_shape=[jax.ShapeDtypeStruct((2 * BLOCK, width), BF16)] * outs,
        compiler_params=pltpu.CompilerParams(vmem_limit_bytes=16 * 1024 * 1024),
        name="head_partial",
    )(at, states, slopes, *[value for some in adds for value in some])


def add(*values):
    total = values[0].astype(F32)
    for value in values[1:]:
        total = total + value.astype(F32)
    return total.astype(BF16)


def scatter_head(states, slopes, core, head, passage_dy):
    def part(d1s, d2s, adds):
        at = [block_at(core, d1, d2) for d1, some in zip(d1s, d2s) for d2 in some]
        return head_partial(states, slopes, jnp.stack(at).astype(jnp.int32), adds)

    a, b = (2, 1), (-1, 0)
    far_a, far_b = part((2, 2), (a, b), ((), ()))
    far_a, far_b = shift(far_a, 1, 1), shift(far_b, 1, -1)
    up_b, down_a = part((1, -1), (b, a), ((), ()))
    up_b, down_a, passage_dy = together(up_b, down_a, passage_dy)
    up_b, down_a = shift(up_b, 1, 1), shift(down_a, 1, -1)
    extra = input_grad(passage_dy, head, 0)
    far_a, far_b, extra = together(far_a, far_b, extra)
    up_a, down_b = part((1, -1), (a, b), ((far_a,), (far_b,)))
    up_a, down_b = shift(up_a, 1, 1), shift(down_b, 1, -1)
    mine_a, mine_b = part((0, 0), (a, b), ((down_a,), (up_b,)))
    mine_a, mine_b, passage_dy = together(mine_a, mine_b, passage_dy)
    extra = input_grad(passage_dy, head, 1, extra)
    up_a, down_b, mine_a, mine_b, extra = together(up_a, down_b, mine_a, mine_b, extra)
    half = BLOCK // 2
    far, up = mine_a[:BLOCK], mine_a[BLOCK:]
    down, mine = mine_b[:BLOCK], mine_b[BLOCK:]
    up_far, up_up = up_a[:BLOCK], up_a[BLOCK:]
    down_down, down_mine = down_b[:BLOCK], down_b[BLOCK:]
    far_a = shift(add(far[:half], up_far[:half]), 2, 1)
    far_b = shift(add(far[half:], up_far[half:]), 2, -1)
    up_b = shift(add(up[half:], up_up[half:]), 2, 1)
    down_a = shift(add(down[:half], down_down[:half]), 2, -1)
    far_a, far_b, up_b, down_a = together(far_a, far_b, up_b, down_a)
    up_a = shift(add(up[:half], up_up[:half], far_a), 2, 1)
    down_b = shift(add(down[half:], down_down[half:], far_b), 2, -1)
    up_a, down_b = together(up_a, down_b)
    total = jnp.concatenate(
        [
            add(mine[:half], down_mine[:half], down_a, up_a),
            add(mine[half:], down_mine[half:], up_b, down_b),
        ],
        axis=0,
    )
    arrived = together(
        *[
            lax.ppermute(
                total[:, step * BLOCK : (step + 1) * BLOCK],
                "x",
                [(i, (i + step) % RING) for i in range(RING)],
            )
            for step in (1, 2, 3)
        ]
    )
    out = total[:, :BLOCK].astype(F32)
    for value in arrived:
        out = out + value.astype(F32)
    return out, extra


def dot(a, b, contract=((1,), (0,))):
    return lax.dot_general(a, b, (contract, ((), ())), preferred_element_type=F32)


def per_device(queries, passages, head_weight, send_lists, neg_slots):
    core, x = lax.axis_index("c"), lax.axis_index("x")
    rows_dev, depth = queries.shape
    width = head_weight.shape[1]
    groups, capacity = send_lists.shape[2], send_lists.shape[3]
    slot_count = groups * capacity
    flat_lists = send_lists.reshape(slot_count)

    def places_of(*pieces):
        places = [(d1, d2) for d1s, d2 in pieces for d1 in d1s]
        at = [block_at(core, d1, d2) for d1, d2 in places] + [block_at(1 - core, d1, d2) for d1, d2 in places]
        side = [core] * len(places) + [1 - core] * len(places)
        return jnp.stack([jnp.stack(at), jnp.stack(side)]).astype(jnp.int32)

    a, b = (0, -1), (1, 2)
    owner = (flat_lists[None, :] == jnp.arange(rows_dev, dtype=jnp.int32)[:, None]).astype(BF16)
    own = lax.dynamic_slice_in_dim(head_weight, core * (width // 2), width // 2, axis=1)

    up, down = shift(own, 1, 1), shift(own, 1, -1)
    picked = dot(owner, passages, ((0,), (0,))).astype(BF16).reshape(groups, capacity, depth)
    up, down, picked = together(up, down, picked)
    arrived = lax.all_to_all(picked, ("x", "c"), split_axis=0, concat_axis=0, tiled=True)
    arrived = arrived.reshape(slot_count, depth)

    first = jnp.concatenate([own, up], axis=0)
    first_up, first_down = shift(first, 2, 1), shift(first, 2, -1)
    half = BLOCK // 2
    far_a, far_b = shift(up[:half], 1, 1), shift(down[half:], 1, -1)
    slot_ids = jnp.arange(slot_count, dtype=jnp.int32)[None, :]
    counts = jnp.zeros((rows_dev, slot_count), F32)
    for j in range(neg_slots.shape[1]):
        counts = counts + (neg_slots[:, j : j + 1] == slot_ids).astype(F32)
    first_up, first_down, far_a, far_b, counts = together(first_up, first_down, far_a, far_b, counts)

    second = jnp.concatenate([down, far_a, far_b], axis=0)
    second_up, second_down = shift(second, 2, 1), shift(second, 2, -1)
    early = [first, second, first_up, first_down]
    early = early + [swap(piece) for piece in early]
    early_at = places_of((a, 0), (b, 0), (a, -1), (a, 1))
    head, pre = project(early_at, (queries, passages), early)
    second_up, second_down, first_up, pre = together(second_up, second_down, first_up, pre)

    first_far, second_far = shift(first_up, 2, 1), shift(second_down, 2, -1)
    turned = turn(queries, passages, swap(queries), swap(passages))
    middle = [second_up, second_down, swap(second_up), swap(second_down)]
    middle_at = places_of((b, -1), (b, 1))
    head, pre = project(middle_at, (queries, passages), middle, (pre,), head)
    pre, arrived = together(pre, arrived)
    joined = early[:4] + middle[:2] + early[4:] + middle[2:]
    joined_at = places_of((a, 0), (b, 0), (a, -1), (a, 1), (b, -1), (b, 1))
    (arrived_pre,) = project(joined_at, (arrived,), joined, store=False)
    late = [first_far, second_far, swap(first_far), swap(second_far)]
    head, pre, _, inverse, emb, mixing, first, fetched_grad = project(
        places_of((a, 2), (b, 2)),
        (queries, passages, arrived),
        late,
        (pre, arrived_pre),
        head,
        counts=counts,
    )
    returned = lax.all_to_all(
        fetched_grad.reshape(groups, capacity, width),
        ("x", "c"),
        split_axis=0,
        concat_axis=0,
        tiled=True,
    ).reshape(slot_count, width)

    to_x = [(x + step) % RING for step in range(RING)]
    cols = jnp.stack(
        [jnp.stack([2 * to + core for to in to_x]), jnp.stack([2 * to + 1 - core for to in to_x])]
    ).astype(jnp.int32)
    query_dy, query_keep, query_send = slopes_of(0, cols, pre, inverse, first, emb, mixing, emb)
    query_other = swap(query_send)
    query_grads = input_grad(query_dy, head, 1, input_grad(query_dy, head, 0))
    returned, query_grads, query_other = lax.optimization_barrier((returned, query_grads, query_other))

    passage_dy, passage_keep, passage_send = slopes_of(
        1, cols, pre, inverse, first, emb, owner, returned
    )
    passage_other = swap(passage_send)
    slopes = jnp.concatenate([query_keep, passage_keep, query_other, passage_other], axis=0)
    head_grads, passage_grads = scatter_head(
        turned, slopes, core, head, passage_dy
    )
    return (query_grads, passage_grads, head_grads)


def solution(mesh):
    fine = Mesh(mesh.devices.reshape(4, 2, 4, 4), ("x", "c", "y", "z"))
    every = ("x", "c", "y", "z")
    return jax.shard_map(
        per_device,
        mesh=fine,
        in_specs=(
            P(every, None),
            P(every, None),
            P(("y", "z"), None),
            P(("x", "c"), ("y", "z"), None, None),
            P(every, None),
        ),
        out_specs=(P(every, None), P(every, None), P(("y", "z"), ("x", "c"))),
        check_vma=False,
    )
```

```python
import jax
import jax.numpy as jnp
from jax import lax
from jax.experimental import pallas as pl
from jax.experimental.pallas import tpu as pltpu
from jax.sharding import Mesh, PartitionSpec as P

EPSILON = 1e-06
BLOCK = 256
RING = 4
SWAP = [(0, 1), (1, 0)]
BF16 = jnp.bfloat16
F32 = jnp.float32


def shift(value, place, step):
    pairs = []
    for c in range(2):
        for y in range(RING):
            for z in range(RING):
                to_y, to_z = y, z
                if (place == 1) == (c == 0):
                    to_y = (y + step) % RING
                else:
                    to_z = (z + step) % RING
                pairs.append((c * 16 + y * 4 + z, c * 16 + to_y * 4 + to_z))
    return lax.ppermute(value, ("c", "y", "z"), pairs)


def swap(value):
    return lax.ppermute(value, "c", SWAP)


def block_at(core, d1, d2):
    y, z = lax.axis_index("y"), lax.axis_index("z")
    far_y = jnp.where(core == 0, d1, d2)
    far_z = jnp.where(core == 0, d2, d1)
    return ((y + far_y) % RING) * RING + (z + far_z) % RING


def together(*values):
    return lax.optimization_barrier(values)


def turn_kernel(*refs):
    parts = 4
    x_refs, turned_ref, held, turned, loaded, stored = refs[:4], *refs[4:]
    rows, depth = x_refs[0].shape
    size = depth // parts
    loads, stores = [], []
    for i in range(parts):
        at = pl.ds(i * size, size)
        loads.append(
            [
                pltpu.make_async_copy(ref.at[:, at], held.at[pl.ds(j * rows, rows), at], loaded.at[i, j])
                for j, ref in enumerate(x_refs)
            ]
        )
        stores.append(pltpu.make_async_copy(turned.at[at, :], turned_ref.at[at, :], stored.at[i]))
    for load in loads:
        start(load)
    for i in range(parts):
        wait(loads[i])
        for k in range(size // BLOCK):
            at = pl.ds(i * size + k * BLOCK, BLOCK)
            turned[at, :] = held[:, at].T
        stores[i].start()
    wait(stores)


def turn(*states):
    rows, depth = states[0].shape
    whole = rows * len(states)
    anywhere = pl.BlockSpec(memory_space=pl.ANY)
    return pl.pallas_call(
        turn_kernel,
        in_specs=[anywhere] * len(states),
        out_specs=anywhere,
        out_shape=pltpu.HBM((depth, whole), BF16),
        scratch_shapes=[
            pltpu.VMEM((whole, depth), BF16),
            pltpu.VMEM((depth, whole), BF16),
            pltpu.SemaphoreType.DMA((4, len(states))),
            pltpu.SemaphoreType.DMA((4,)),
        ],
        compiler_params=pltpu.CompilerParams(vmem_limit_bytes=20 * 1024 * 1024),
        cost_estimate=pl.CostEstimate(flops=1, transcendentals=0, bytes_accessed=1),
        name="turn",
    )(*keep_far(*states[:2]), *states[2:])


def copies_of(pairs, sems):
    return [pltpu.make_async_copy(*pair, sems.at[i]) for i, pair in enumerate(pairs)]


def start(copies):
    for copy in copies:
        copy.start()


def wait(copies):
    for copy in copies:
        copy.wait()


def head_copies(at_ref, held, head_ref, side, blocks, sems):
    col = pl.multiple_of(at_ref[1, side] * 1024, 1024)
    pairs = []
    for k in blocks:
        row = pl.multiple_of(at_ref[0, 16 * side + k] * BLOCK, BLOCK)
        pairs.append(
            (
                held.at[side, pl.ds((k - blocks[0]) * BLOCK, BLOCK), :],
                head_ref.at[pl.ds(row, BLOCK), pl.ds(col, 1024)],
            )
        )
    return copies_of(pairs, sems)


def piece_copies(pieces, held, side, sems):
    row, pairs = 0, []
    for piece in pieces:
        pairs.append((piece, held.at[side, pl.ds(row, piece.shape[0]), :]))
        row += piece.shape[0]
    return copies_of(pairs, sems)


def column_copies(at_ref, side, blocks, sources, states, sems):
    pairs = []
    for i, k in enumerate(blocks):
        col, row = pl.multiple_of(at_ref[0, 16 * side + k] * BLOCK, BLOCK), 0
        for ref in sources:
            to = states.at[side, pl.ds(row, ref.shape[0]), pl.ds(i * BLOCK, BLOCK)]
            pairs.append((ref.at[:, pl.ds(col, BLOCK)], to))
            row += ref.shape[0]
    return copies_of(pairs, sems)


def strips(at_ref, side, body):
    def one(n, _):
        at_col = pl.multiple_of(n * BLOCK, BLOCK)
        body(pl.ds(at_col, BLOCK), pl.ds(pl.multiple_of(at_ref[1, side] * 1024 + at_col, BLOCK), BLOCK))
        return 0

    for n in range(1024 // BLOCK):
        one(n, 0)


def project_early_kernel(count, at_ref, *refs):
    x_refs, pieces = refs[:2], refs[2 : 2 + 2 * count]
    head_ref, part_out, states, held, part_ref, fetched, loaded, stored, parted = refs[2 + 2 * count :]
    blocks = list(range(held.shape[1] // BLOCK))
    loads = [
        column_copies(at_ref, i, blocks, x_refs, states, fetched.at[i])
        + piece_copies(pieces[i * count : (i + 1) * count], held, i, loaded.at[i])
        for i in range(2)
    ]
    stores = [head_copies(at_ref, held, head_ref, i, blocks, stored.at[i]) for i in range(2)]
    outs = []
    start(loads[0])
    for side in range(2):
        wait(loads[side])
        start(loads[1] if side == 0 else stores[0] + stores[1])

        def multiply(near_at, whole_at, side=side):
            part_ref[:, whole_at] = jnp.dot(
                states[side], held[side, :, near_at], preferred_element_type=F32
            ).astype(BF16)

        strips(at_ref, side, multiply)
        whole = pl.ds(pl.multiple_of(at_ref[1, side] * 1024, 1024), 1024)
        outs.append(pltpu.make_async_copy(part_ref.at[:, whole], part_out.at[:, whole], parted.at[side]))
        start(outs[side:])
    wait(outs + stores[0] + stores[1])


def project_early(at, xs, pieces):
    count, depth = len(pieces) // 2, sum(piece.shape[0] for piece in pieces) // 2
    rows = sum(x.shape[0] for x in xs)
    anywhere = pl.BlockSpec(memory_space=pl.ANY)
    return pl.pallas_call(
        lambda *refs: project_early_kernel(count, *refs),
        in_specs=[pl.BlockSpec(memory_space=pltpu.SMEM)] + [anywhere] * (2 + 2 * count),
        out_specs=[anywhere] * 2,
        out_shape=[pltpu.HBM((4096, 2048), BF16), pltpu.HBM((rows, 2048), BF16)],
        scratch_shapes=[
            pltpu.VMEM((2, rows, depth), BF16),
            pltpu.VMEM((2, depth, 1024), BF16),
            pltpu.VMEM((rows, 2048), BF16),
            pltpu.SemaphoreType.DMA((2, 2 * depth // BLOCK)),
            pltpu.SemaphoreType.DMA((2, count)),
            pltpu.SemaphoreType.DMA((2, depth // BLOCK)),
            pltpu.SemaphoreType.DMA((2,)),
        ],
        compiler_params=pltpu.CompilerParams(vmem_limit_bytes=24 * 1024 * 1024),
        name="project_early",
    )(at, *keep_far(*xs, *pieces))


def project_middle_kernel(count, early, at_ref, *refs):
    x_refs, pieces = refs[:3], refs[3 : 3 + 2 * count]
    part_in, _, head_ref, part_out = refs[3 + 2 * count : 7 + 2 * count]
    own_states, far_states, held, part_ref, fetched, loaded, stored, parted = refs[7 + 2 * count :]
    rows, depth = far_states.shape[1], held.shape[1]
    blocks = list(range(depth // BLOCK))
    late = early * BLOCK
    base = copies_of([(part_in, part_ref.at[pl.ds(0, rows), :])], parted.at[2])
    loads = [
        column_copies(at_ref, i, blocks, x_refs[2:], far_states, fetched.at[2 * i])
        + piece_copies(pieces[i * count : (i + 1) * count], held, i, loaded.at[i])
        + column_copies(at_ref, i, blocks[early:], x_refs[:2], own_states, fetched.at[2 * i + 1])
        for i in range(2)
    ]
    stores = [head_copies(at_ref, held, head_ref, i, blocks, stored.at[i])[early:] for i in range(2)]
    outs = []
    start(loads[0] + base)
    for side in range(2):
        wait(loads[side])
        start(loads[1] if side == 0 else stores[0] + stores[1])
        if side == 0:
            wait(base)

        def multiply(near_at, whole_at, side=side):
            own_at = pl.ds(0, rows)
            part_ref[own_at, whole_at] = (
                part_ref[own_at, whole_at].astype(F32)
                + jnp.dot(
                    own_states[side],
                    held[side, pl.ds(late, depth - late), near_at],
                    preferred_element_type=F32,
                )
            ).astype(BF16)
            part_ref[pl.ds(rows, rows), whole_at] = jnp.dot(
                far_states[side], held[side, :, near_at], preferred_element_type=F32
            ).astype(BF16)

        strips(at_ref, side, multiply)
        whole = pl.ds(pl.multiple_of(at_ref[1, side] * 1024, 1024), 1024)
        outs.append(
            pltpu.make_async_copy(part_ref.at[:, whole], part_out.at[:, whole], parted.at[side, 0])
        )
        start(outs[side:])
    wait(outs + stores[0] + stores[1])


def project_middle(at, early, xs, pieces, part, head):
    count, depth = len(pieces) // 2, sum(piece.shape[0] for piece in pieces) // 2
    rows = xs[2].shape[0]
    anywhere = pl.BlockSpec(memory_space=pl.ANY)
    ins = [anywhere] * (5 + 2 * count)
    return pl.pallas_call(
        lambda *refs: project_middle_kernel(count, early, *refs),
        in_specs=[pl.BlockSpec(memory_space=pltpu.SMEM)] + ins,
        out_specs=[anywhere] * 2,
        out_shape=[pltpu.HBM((4096, 2048), BF16), pltpu.HBM((2 * rows, 2048), BF16)],
        scratch_shapes=[
            pltpu.VMEM((2, rows, depth - early * BLOCK), BF16),
            pltpu.VMEM((2, rows, depth), BF16),
            pltpu.VMEM((2, depth, 1024), BF16),
            pltpu.VMEM((2 * rows, 2048), BF16),
            pltpu.SemaphoreType.DMA((4, 16)),
            pltpu.SemaphoreType.DMA((2, count)),
            pltpu.SemaphoreType.DMA((2, depth // BLOCK)),
            pltpu.SemaphoreType.DMA((3, 1)),
        ],
        input_output_aliases={len(ins): 0},
        compiler_params=pltpu.CompilerParams(vmem_limit_bytes=36 * 1024 * 1024),
        name="project_middle",
    )(at, *keep_far(*xs, *pieces, part, head))


def project_last_kernel(count, at_ref, *refs):
    x_refs, pieces = refs[:3], refs[3 : 3 + 2 * count]
    part_in, counts_ref, _, head_ref, emb_out, inverse_ref, mixing_ref, first_ref, grad_ref = refs[
        3 + 2 * count : 12 + 2 * count
    ]
    states, held, part_ref, pre_ref, emb_ref, parted, fetched, loaded, stored, sent = refs[12 + 2 * count :]
    late = held.shape[1] // BLOCK
    blocks = list(range(16 - late, 16))
    loads, stores = [], []
    for side in range(2):
        copies = column_copies(at_ref, side, blocks, x_refs, states, fetched.at[side])
        copies += piece_copies(pieces[side * count : (side + 1) * count], held, side, loaded.at[side])
        loads.append(copies)
        stores.append(head_copies(at_ref, held, head_ref, side, blocks, stored.at[side]))
    halves = [pl.ds(pl.multiple_of(at_ref[1, side] * 1024, 1024), 1024) for side in range(2)]
    base = copies_of([(part_in.at[:, at], part_ref.at[:, at]) for at in halves], parted)
    start(loads[0] + base[:1] + loads[1] + base[1:])
    inverse_ref[...] = jnp.zeros(inverse_ref.shape, F32)
    for side in range(2):
        wait(loads[side] + base[side : side + 1])
        if side == 1:
            start(stores[0] + stores[1])

        def multiply(near_at, whole_at, side=side):
            values = part_ref[:, whole_at].astype(F32) + jnp.dot(
                states[side], held[side, :, near_at], preferred_element_type=F32
            )
            pre_ref[:, whole_at] = values
            squares = values * values
            inverse_ref[...] += squares[:, :128] + squares[:, 128:]

        strips(at_ref, side, multiply)
    normalize(pre_ref, emb_ref, inverse_ref)
    sending = copies_of([(emb_ref, emb_out)], sent)
    start(sending)
    contrast(counts_ref, emb_ref, mixing_ref, first_ref, grad_ref)
    wait(sending + stores[0] + stores[1])


def project_last(at, xs, pieces, part, counts, head):
    count, depth = len(pieces) // 2, sum(piece.shape[0] for piece in pieces) // 2
    rows = sum(x.shape[0] for x in xs)
    half = rows // 4
    anywhere = pl.BlockSpec(memory_space=pl.ANY)
    ins = [anywhere] * (4 + 2 * count) + vmem(1) + [anywhere]
    return pl.pallas_call(
        lambda *refs: project_last_kernel(count, *refs),
        in_specs=[pl.BlockSpec(memory_space=pltpu.SMEM)] + ins,
        out_specs=[anywhere] * 2 + vmem(4),
        out_shape=[
            pltpu.HBM((4096, 2048), BF16),
            pltpu.HBM((rows, 2048), BF16),
            pltpu.HBM((rows, 128), F32),
            pltpu.HBM((half, 2 * half), BF16),
            pltpu.HBM((half, 128), F32),
            pltpu.HBM((2 * half, 2048), BF16),
        ],
        scratch_shapes=[
            pltpu.VMEM((2, rows, depth), BF16),
            pltpu.VMEM((2, depth, 1024), BF16),
            pltpu.VMEM((rows, 2048), BF16),
            pltpu.VMEM((rows, 2048), F32),
            pltpu.VMEM((rows, 2048), BF16),
            pltpu.SemaphoreType.DMA((2,)),
            pltpu.SemaphoreType.DMA((2, 3 * depth // BLOCK)),
            pltpu.SemaphoreType.DMA((2, count)),
            pltpu.SemaphoreType.DMA((2, depth // BLOCK)),
            pltpu.SemaphoreType.DMA((1,)),
        ],
        input_output_aliases={len(ins): 0},
        compiler_params=pltpu.CompilerParams(vmem_limit_bytes=30 * 1024 * 1024),
        name="project_last",
    )(at, *keep_far(*xs, *pieces, part), counts, *keep_far(head))


def normalize(pre_ref, emb_ref, inverse_ref):
    chunk = 128
    width = pre_ref.shape[1]

    def some(i, _):
        at = pl.ds(pl.multiple_of(i * chunk, chunk), chunk)
        mean = jnp.sum(inverse_ref[at, :], axis=-1, keepdims=True) * (1.0 / width)
        inverse = jnp.broadcast_to(lax.rsqrt(mean + EPSILON), (chunk, 128))
        inverse_ref[at, :] = inverse
        emb_ref[at, :] = (pre_ref[at, :] * inverse[:, :1]).astype(BF16)
        return 0

    lax.fori_loop(0, pre_ref.shape[0] // chunk, some, 0)


def contrast(counts_ref, emb_ref, mixing_ref, first_ref, grad_ref):
    rows = counts_ref.shape[0]
    scale = 16.0 / emb_ref.shape[1]
    query = emb_ref[pl.ds(0, rows), :]
    passage = emb_ref[pl.ds(rows, rows), :]
    fetched = emb_ref[pl.ds(2 * rows, 2 * rows), :]
    positive = (
        jnp.sum(query.astype(F32) * passage.astype(F32), axis=1, keepdims=True) * scale
    )
    table = dot(query, fetched, ((1,), (1,))) * scale
    counts = counts_ref[...]
    top = jnp.maximum(
        positive, jnp.max(jnp.where(counts > 0, table, -1e30), axis=1, keepdims=True)
    )
    raised = jnp.where(counts > 0, jnp.exp(jnp.where(counts > 0, table - top, 0.0)), 0.0)
    raised_positive = jnp.exp(positive - top)
    whole = raised_positive + jnp.sum(raised * counts, axis=1, keepdims=True)
    first = (raised_positive / whole - 1.0).astype(BF16).astype(F32)
    mixing = ((raised / whole).astype(BF16).astype(F32) * counts).astype(BF16)
    first_ref[...] = jnp.broadcast_to(first, (rows, 128))
    mixing_ref[...] = mixing
    grad_ref[...] = dot(mixing, query, ((0,), (0,))).astype(BF16)


def vmem(count):
    return [pl.BlockSpec(memory_space=pltpu.VMEM)] * count


def near(shape, dtype):
    return pltpu.VMEM(shape, dtype)


def keep_near(*values):
    return [pltpu.with_memory_space_constraint(value, pltpu.VMEM) for value in values]


def keep_far(*values):
    return [pltpu.with_memory_space_constraint(value, pltpu.HBM) for value in values]


def slopes_kernel(part, cols_ref, inverse_hbm, first_hbm, emb_hbm, left_hbm, right_hbm, out_ref, keep_ref, send_ref, grad_ref, inverse_ref, first_ref, emb_ref, own_ref, left_ref, right_ref, sems):
    rows, chunk = out_ref.shape[0], 96
    width = out_ref.shape[1]
    depth = left_ref.shape[1]
    loads = [
        (left_hbm, left_ref),
        (right_hbm.at[pl.ds(2 * rows if part == 0 else 0, depth), :], right_ref),
        (emb_hbm.at[pl.ds((1 - part) * rows, rows), :], emb_ref),
        (first_hbm, first_ref),
        (inverse_hbm.at[pl.ds(part * rows, rows), :], inverse_ref),
        (emb_hbm.at[pl.ds(part * rows, rows), :], own_ref),
    ]
    loads = [pltpu.make_async_copy(*load, sems.at[i]) for i, load in enumerate(loads)]
    for load in loads:
        load.start()
    for load in loads[:2]:
        load.wait()
    grad_ref[...] = jnp.dot(left_ref[...], right_ref[...], preferred_element_type=F32)
    for load in loads[2:]:
        load.wait()

    def some(i, _):
        at = pl.ds(pl.multiple_of(i * chunk, chunk), chunk)
        grad = first_ref[at, :1] * emb_ref[at, :].astype(F32) + grad_ref[at, :]
        values = own_ref[at, :].astype(F32)
        along = jnp.mean(grad * values, axis=-1, keepdims=True)
        out_ref[at, :] = (inverse_ref[at, :1] * (grad - values * along)).astype(BF16)
        return 0

    lax.fori_loop(0, rows // chunk, some, 0)
    for k in range(width // BLOCK // 2):
        for row, ref in ((0, keep_ref), (1, send_ref)):
            col = pl.multiple_of(cols_ref[row, k] * BLOCK, BLOCK)
            ref[:, pl.ds(k * BLOCK, BLOCK)] = out_ref[:, pl.ds(col, BLOCK)]


def slopes_of(part, cols, inverse, first, emb, left, right):
    rows = first.shape[0]
    width = emb.shape[1]
    anywhere = pl.BlockSpec(memory_space=pl.ANY)
    return pl.pallas_call(
        lambda *refs: slopes_kernel(part, *refs),
        in_specs=[pl.BlockSpec(memory_space=pltpu.SMEM)] + [anywhere] * 5,
        out_specs=vmem(3),
        out_shape=[
            jax.ShapeDtypeStruct((rows, width), BF16),
            jax.ShapeDtypeStruct((rows, width // 2), BF16),
            jax.ShapeDtypeStruct((rows, width // 2), BF16),
        ],
        scratch_shapes=[
            pltpu.VMEM((rows, width), F32),
            pltpu.VMEM(first.shape, F32),
            pltpu.VMEM(first.shape, F32),
            pltpu.VMEM((rows, width), BF16),
            pltpu.VMEM((rows, width), BF16),
            pltpu.VMEM(left.shape, BF16),
            pltpu.VMEM((left.shape[1], width), BF16),
            pltpu.SemaphoreType.DMA((6,)),
        ],
        compiler_params=pltpu.CompilerParams(vmem_limit_bytes=16 * 1024 * 1024),
        name="slopes_of",
    )(cols, *keep_far(inverse, first, emb, left), right)


def input_grad_kernel(count, *refs):
    slopes_refs, head_ref, out_refs = refs[:count], refs[count], refs[-count:]
    rows = slopes_refs[0].shape[0]
    slopes = jnp.concatenate([ref[...] for ref in slopes_refs], axis=0)
    grads = dot(slopes, head_ref[...], ((1,), (1,))).astype(BF16)
    for i, ref in enumerate(out_refs):
        ref[...] = grads[i * rows : (i + 1) * rows]


def input_grad(slopes, head, part, filled=()):
    count = len(slopes)
    rows, width = slopes[0].shape
    depth = head.shape[0]
    steps = depth // 512 // 2
    return pl.pallas_call(
        lambda *refs: input_grad_kernel(count, *refs),
        grid=(steps,),
        in_specs=[pl.BlockSpec((rows, width), lambda k: (0, 0))] * count
        + [pl.BlockSpec((512, width), lambda k: (k + part * steps, 0))]
        + [pl.BlockSpec(memory_space=pl.ANY)] * len(filled),
        out_specs=[pl.BlockSpec((rows, 512), lambda k: (0, k + part * steps))] * count,
        out_shape=[jax.ShapeDtypeStruct((rows, depth), BF16)] * count,
        input_output_aliases={count + 1 + i: i for i in range(len(filled))},
        compiler_params=pltpu.CompilerParams(vmem_limit_bytes=20 * 1024 * 1024),
        cost_estimate=pl.CostEstimate(flops=1, transcendentals=0, bytes_accessed=1),
        name="input_grad",
    )(*slopes, *keep_far(head), *filled)


def partial_kernel(outs, adds, at_ref, states_ref, slopes_ref, *refs):
    for k in range(outs * 2):
        row = pl.multiple_of(at_ref[k] * BLOCK, BLOCK)
        part = pl.ds(k % 2 * BLOCK, BLOCK)
        total = jnp.dot(
            states_ref[pl.ds(row, BLOCK), :], slopes_ref[...], preferred_element_type=F32
        ) * (1.0 / 128.0)
        for ref in refs[k // 2 * adds : (k // 2 + 1) * adds]:
            total = total + ref[part, :].astype(F32)
        refs[outs * adds + k // 2][part, :] = total.astype(BF16)


def head_partial(states, slopes, at, adds):
    outs, width = len(adds), slopes.shape[1]
    return pl.pallas_call(
        lambda *refs: partial_kernel(outs, len(adds[0]), *refs),
        in_specs=[pl.BlockSpec(memory_space=pltpu.SMEM)] + vmem(2 + outs * len(adds[0])),
        out_specs=vmem(outs),
        out_shape=[jax.ShapeDtypeStruct((2 * BLOCK, width), BF16)] * outs,
        compiler_params=pltpu.CompilerParams(vmem_limit_bytes=20 * 1024 * 1024),
        name="head_partial",
    )(at, *keep_near(states), slopes, *[value for some in adds for value in some])


def add(*values):
    total = values[0].astype(F32)
    for value in values[1:]:
        total = total + value.astype(F32)
    return total.astype(BF16)


def scatter_head(states, slopes, core, head, query_dy, passage_dy, query_grads):
    def part(d1s, d2s, adds):
        at = [block_at(core, d1, d2) for d1, some in zip(d1s, d2s) for d2 in some]
        return head_partial(states, slopes, jnp.stack(at).astype(jnp.int32), adds)

    a, b = (2, 1), (-1, 0)
    far_a, far_b = part((2, 2), (a, b), ((), ()))
    far_a, far_b = shift(far_a, 1, 1), shift(far_b, 1, -1)
    up_b, down_a = part((1, -1), (b, a), ((), ()))
    up_b, down_a, passage_dy = together(up_b, down_a, passage_dy)
    up_b, down_a = shift(up_b, 1, 1), shift(down_a, 1, -1)
    (passage_grads,) = input_grad([passage_dy], head, 0)
    far_a, far_b, passage_grads = together(far_a, far_b, passage_grads)
    up_a, down_b = part((1, -1), (a, b), ((far_a,), (far_b,)))
    up_a, down_b = shift(up_a, 1, 1), shift(down_b, 1, -1)
    mine_a, mine_b = part((0, 0), (a, b), ((down_a,), (up_b,)))
    mine_a, mine_b, passage_dy = together(mine_a, mine_b, passage_dy)
    grads = input_grad([query_dy, passage_dy], head, 1, [query_grads, passage_grads])
    up_a, down_b, mine_a, mine_b, *grads = together(up_a, down_b, mine_a, mine_b, *grads)
    half = BLOCK // 2
    far, up = mine_a[:BLOCK], mine_a[BLOCK:]
    down, mine = mine_b[:BLOCK], mine_b[BLOCK:]
    up_far, up_up = up_a[:BLOCK], up_a[BLOCK:]
    down_down, down_mine = down_b[:BLOCK], down_b[BLOCK:]
    far_a = shift(add(far[:half], up_far[:half]), 2, 1)
    far_b = shift(add(far[half:], up_far[half:]), 2, -1)
    up_b = shift(add(up[half:], up_up[half:]), 2, 1)
    down_a = shift(add(down[:half], down_down[:half]), 2, -1)
    far_a, far_b, up_b, down_a = together(far_a, far_b, up_b, down_a)
    up_a = shift(add(up[:half], up_up[:half], far_a), 2, 1)
    down_b = shift(add(down[half:], down_down[half:], far_b), 2, -1)
    up_a, down_b = together(up_a, down_b)
    total = jnp.concatenate(
        [
            add(mine[:half], down_mine[:half], down_a, up_a),
            add(mine[half:], down_mine[half:], up_b, down_b),
        ],
        axis=0,
    )
    arrived = together(
        *[
            lax.ppermute(
                total[:, step * BLOCK : (step + 1) * BLOCK],
                "x",
                [(i, (i + step) % RING) for i in range(RING)],
            )
            for step in (1, 2, 3)
        ]
    )
    out = total[:, :BLOCK].astype(F32)
    for value in arrived:
        out = out + value.astype(F32)
    return out, *grads


def dot(a, b, contract=((1,), (0,))):
    return lax.dot_general(a, b, (contract, ((), ())), preferred_element_type=F32)


def per_device(queries, passages, head_weight, send_lists, neg_slots):
    core, x = lax.axis_index("c"), lax.axis_index("x")
    rows_dev, depth = queries.shape
    width = head_weight.shape[1]
    groups, capacity = send_lists.shape[2], send_lists.shape[3]
    slot_count = groups * capacity
    flat_lists = send_lists.reshape(slot_count)

    owner = (flat_lists[None, :] == jnp.arange(rows_dev, dtype=jnp.int32)[:, None]).astype(BF16)
    own = lax.dynamic_slice_in_dim(head_weight, core * (width // 2), width // 2, axis=1)

    up, down = shift(own, 1, 1), shift(own, 1, -1)
    picked = dot(owner, passages, ((0,), (0,))).astype(BF16).reshape(groups, capacity, depth)
    own, picked = together(own, picked)
    own_up, own_down = shift(own, 2, 1), shift(own, 2, -1)
    arrived = lax.all_to_all(picked, ("x", "c"), split_axis=0, concat_axis=0, tiled=True)
    arrived = arrived.reshape(slot_count, depth)

    far = shift(up, 1, 1)
    up_up, up_down = shift(up, 2, 1), shift(up, 2, -1)
    slot_ids = jnp.arange(slot_count, dtype=jnp.int32)[None, :]
    counts = jnp.zeros((rows_dev, slot_count), F32)
    for j in range(neg_slots.shape[1]):
        counts = counts + (neg_slots[:, j : j + 1] == slot_ids).astype(F32)
    far, up_up, up_down, own_up, own_down, counts = together(far, up_up, up_down, own_up, own_down, counts)

    second = jnp.concatenate([down, far], axis=0)
    second_up, second_down = shift(second, 2, 1), shift(second, 2, -1)
    first_up = jnp.concatenate([own_up, up_up], axis=0)
    early = [own, up, second, first_up, own_down, up_down]
    early = early, [swap(piece) for piece in early]
    places = [(0, 0), (-1, 0), (1, 0), (2, 0), (0, -1), (-1, -1), (0, 1), (-1, 1)]
    places += [(1, -1), (2, -1), (1, 1), (2, 1), (0, 2), (-1, 2), (1, 2), (2, 2)]
    at = [block_at(core, *place) for place in places] + [block_at(1 - core, *place) for place in places]
    side = [core, 1 - core] + [core] * 30
    at = jnp.stack([jnp.stack(at), jnp.stack(side)]).astype(jnp.int32)
    xs = queries, passages, arrived
    head, part = project_early(at, xs[:2], early[0] + early[1])
    second_up, second_down, first_up, part = together(second_up, second_down, first_up, part)

    first_far, second_far = shift(first_up, 2, 1), shift(second_down, 2, -1)
    middle = [second_up, second_down]
    other_middle = [swap(piece) for piece in middle]
    head, part = project_middle(at, 8, xs, early[0] + middle + early[1] + other_middle, part, head)
    first_far, second_far, part = together(first_far, second_far, part)
    late = [first_far, second_far, swap(first_far), swap(second_far)]
    head, emb, inverse, mixing, first, fetched_grad = project_last(at, xs, late, part, counts, head)
    returned = lax.all_to_all(
        fetched_grad.reshape(groups, capacity, width),
        ("x", "c"),
        split_axis=0,
        concat_axis=0,
        tiled=True,
    ).reshape(slot_count, width)

    to_x = [(x + step) % RING for step in range(RING)]
    cols = jnp.stack(
        [jnp.stack([2 * to + core for to in to_x]), jnp.stack([2 * to + 1 - core for to in to_x])]
    ).astype(jnp.int32)
    query_states, passage_states, first = together(queries, passages, first)
    query_dy, query_keep, query_send = slopes_of(0, cols, inverse, first, emb, mixing, emb)
    turned = turn(query_states, passage_states, swap(query_states), swap(passage_states))
    (query_grads,) = input_grad([query_dy], head, 0)
    returned, query_grads, query_send, turned = together(returned, query_grads, query_send, turned)
    query_other = swap(query_send)

    passage_dy, passage_keep, passage_send = slopes_of(
        1, cols, inverse, first, emb, owner, returned
    )
    passage_other = swap(passage_send)
    slopes = jnp.concatenate([query_keep, passage_keep, query_other, passage_other], axis=0)
    head_grads, query_grads, passage_grads = scatter_head(
        turned, slopes, core, head, query_dy, passage_dy, query_grads
    )
    return (query_grads, passage_grads, head_grads)


def solution(mesh):
    fine = Mesh(mesh.devices.reshape(4, 2, 4, 4), ("x", "c", "y", "z"))
    every = ("x", "c", "y", "z")
    return jax.shard_map(
        per_device,
        mesh=fine,
        in_specs=(
            P(every, None),
            P(every, None),
            P(("y", "z"), None),
            P(("x", "c"), ("y", "z"), None, None),
            P(every, None),
        ),
        out_specs=(P(every, None), P(every, None), P(("y", "z"), ("x", "c"))),
        check_vma=False,
    )
```

```python
import jax
import jax.numpy as jnp
from jax import lax
from jax.experimental import pallas as pl
from jax.experimental.pallas import tpu as pltpu
from jax.sharding import Mesh, PartitionSpec as P

EPSILON = 1e-06
BLOCK = 256
RING = 4
SWAP = [(0, 1), (1, 0)]
BF16 = jnp.bfloat16
F32 = jnp.float32


def shift(value, place, step):
    pairs = []
    for c in range(2):
        for y in range(RING):
            for z in range(RING):
                to_y, to_z = y, z
                if (place == 1) == (c == 0):
                    to_y = (y + step) % RING
                else:
                    to_z = (z + step) % RING
                pairs.append((c * 16 + y * 4 + z, c * 16 + to_y * 4 + to_z))
    return lax.ppermute(value, ("c", "y", "z"), pairs)


def swap(value):
    return lax.ppermute(value, "c", SWAP)


def block_at(core, d1, d2):
    y, z = lax.axis_index("y"), lax.axis_index("z")
    far_y = jnp.where(core == 0, d1, d2)
    far_z = jnp.where(core == 0, d2, d1)
    return ((y + far_y) % RING) * RING + (z + far_z) % RING


def together(*values):
    return lax.optimization_barrier(values)


def turn_kernel(*refs):
    parts = 4
    x_refs, turned_ref, held, turned, loaded, stored = refs[:4], *refs[4:]
    rows, depth = x_refs[0].shape
    size = depth // parts
    loads, stores = [], []
    for i in range(parts):
        at = pl.ds(i * size, size)
        loads.append(
            [
                pltpu.make_async_copy(ref.at[:, at], held.at[pl.ds(j * rows, rows), at], loaded.at[i, j])
                for j, ref in enumerate(x_refs)
            ]
        )
        stores.append(pltpu.make_async_copy(turned.at[at, :], turned_ref.at[at, :], stored.at[i]))
    for load in loads:
        start(load)
    for i in range(parts):
        wait(loads[i])
        for k in range(size // BLOCK):
            at = pl.ds(i * size + k * BLOCK, BLOCK)
            turned[at, :] = held[:, at].T
        stores[i].start()
    wait(stores)


def turn(*states):
    rows, depth = states[0].shape
    whole = rows * len(states)
    anywhere = pl.BlockSpec(memory_space=pl.ANY)
    return pl.pallas_call(
        turn_kernel,
        in_specs=[anywhere] * len(states),
        out_specs=anywhere,
        out_shape=pltpu.HBM((depth, whole), BF16),
        scratch_shapes=[
            pltpu.VMEM((whole, depth), BF16),
            pltpu.VMEM((depth, whole), BF16),
            pltpu.SemaphoreType.DMA((4, len(states))),
            pltpu.SemaphoreType.DMA((4,)),
        ],
        compiler_params=pltpu.CompilerParams(vmem_limit_bytes=20 * 1024 * 1024),
        cost_estimate=pl.CostEstimate(flops=1, transcendentals=0, bytes_accessed=1),
        name="turn",
    )(*keep_far(*states[:2]), *states[2:])


def copies_of(pairs, sems):
    return [pltpu.make_async_copy(*pair, sems.at[i]) for i, pair in enumerate(pairs)]


def start(copies):
    for copy in copies:
        copy.start()


def wait(copies):
    for copy in copies:
        copy.wait()


def head_copies(at_ref, held, head_ref, side, blocks, sems):
    col = pl.multiple_of(at_ref[1, side] * 1024, 1024)
    pairs = []
    for k in blocks:
        row = pl.multiple_of(at_ref[0, 16 * side + k] * BLOCK, BLOCK)
        pairs.append(
            (
                held.at[side, pl.ds((k - blocks[0]) * BLOCK, BLOCK), :],
                head_ref.at[pl.ds(row, BLOCK), pl.ds(col, 1024)],
            )
        )
    return copies_of(pairs, sems)


def piece_copies(pieces, held, side, sems):
    row, pairs = 0, []
    for piece in pieces:
        pairs.append((piece, held.at[side, pl.ds(row, piece.shape[0]), :]))
        row += piece.shape[0]
    return copies_of(pairs, sems)


def column_copies(at_ref, side, blocks, sources, states, sems):
    pairs = []
    for i, k in enumerate(blocks):
        col, row = pl.multiple_of(at_ref[0, 16 * side + k] * BLOCK, BLOCK), 0
        for ref in sources:
            to = states.at[side, pl.ds(row, ref.shape[0]), pl.ds(i * BLOCK, BLOCK)]
            pairs.append((ref.at[:, pl.ds(col, BLOCK)], to))
            row += ref.shape[0]
    return copies_of(pairs, sems)


def strips(at_ref, side, body, unroll=1):
    def one(n, _):
        at_col = pl.multiple_of(n * BLOCK, BLOCK)
        body(pl.ds(at_col, BLOCK), pl.ds(pl.multiple_of(at_ref[1, side] * 1024 + at_col, BLOCK), BLOCK))
        return 0

    lax.fori_loop(0, 1024 // BLOCK, one, 0, unroll=unroll)


def project_early_kernel(count, at_ref, *refs):
    x_refs, pieces = refs[:2], refs[2 : 2 + 2 * count]
    head_ref, part_out, states, held, part_ref, fetched, loaded, stored, parted = refs[2 + 2 * count :]
    blocks = list(range(held.shape[1] // BLOCK))
    loads = [
        column_copies(at_ref, i, blocks, x_refs, states, fetched.at[i])
        + piece_copies(pieces[i * count : (i + 1) * count], held, i, loaded.at[i])
        for i in range(2)
    ]
    stores = [head_copies(at_ref, held, head_ref, i, blocks, stored.at[i]) for i in range(2)]
    outs = []
    start(loads[0])
    for side in range(2):
        wait(loads[side])
        start(loads[1] if side == 0 else stores[0] + stores[1])

        def multiply(near_at, whole_at, side=side):
            part_ref[:, whole_at] = jnp.dot(
                states[side], held[side, :, near_at], preferred_element_type=F32
            ).astype(BF16)

        strips(at_ref, side, multiply)
        whole = pl.ds(pl.multiple_of(at_ref[1, side] * 1024, 1024), 1024)
        outs.append(pltpu.make_async_copy(part_ref.at[:, whole], part_out.at[:, whole], parted.at[side]))
        start(outs[side:])
    wait(outs + stores[0] + stores[1])


def project_early(at, xs, pieces):
    count, depth = len(pieces) // 2, sum(piece.shape[0] for piece in pieces) // 2
    rows = sum(x.shape[0] for x in xs)
    anywhere = pl.BlockSpec(memory_space=pl.ANY)
    return pl.pallas_call(
        lambda *refs: project_early_kernel(count, *refs),
        in_specs=[pl.BlockSpec(memory_space=pltpu.SMEM)] + [anywhere] * (2 + 2 * count),
        out_specs=[anywhere] * 2,
        out_shape=[pltpu.HBM((4096, 2048), BF16), pltpu.HBM((rows, 2048), BF16)],
        scratch_shapes=[
            pltpu.VMEM((2, rows, depth), BF16),
            pltpu.VMEM((2, depth, 1024), BF16),
            pltpu.VMEM((rows, 2048), BF16),
            pltpu.SemaphoreType.DMA((2, 2 * depth // BLOCK)),
            pltpu.SemaphoreType.DMA((2, count)),
            pltpu.SemaphoreType.DMA((2, depth // BLOCK)),
            pltpu.SemaphoreType.DMA((2,)),
        ],
        compiler_params=pltpu.CompilerParams(vmem_limit_bytes=24 * 1024 * 1024),
        name="project_early",
    )(at, *keep_far(*xs, *pieces))


def project_middle_kernel(count, early, at_ref, *refs):
    x_refs, pieces = refs[:3], refs[3 : 3 + 2 * count]
    part_in, _, head_ref, part_out = refs[3 + 2 * count : 7 + 2 * count]
    own_states, far_states, held, part_ref, fetched, loaded, stored, parted = refs[7 + 2 * count :]
    rows, depth = far_states.shape[1], held.shape[1]
    blocks = list(range(depth // BLOCK))
    late = early * BLOCK
    base = copies_of([(part_in, part_ref.at[pl.ds(0, rows), :])], parted.at[2])
    loads = [
        column_copies(at_ref, i, blocks, x_refs[2:], far_states, fetched.at[2 * i])
        + piece_copies(pieces[i * count : (i + 1) * count], held, i, loaded.at[i])
        + column_copies(at_ref, i, blocks[early:], x_refs[:2], own_states, fetched.at[2 * i + 1])
        for i in range(2)
    ]
    stores = [head_copies(at_ref, held, head_ref, i, blocks, stored.at[i])[early:] for i in range(2)]
    outs = []
    start(loads[0] + base)
    for side in range(2):
        wait(loads[side])
        start(loads[1] if side == 0 else stores[0] + stores[1])
        if side == 0:
            wait(base)

        def multiply(near_at, whole_at, side=side):
            own_at = pl.ds(0, rows)
            part_ref[own_at, whole_at] = (
                part_ref[own_at, whole_at].astype(F32)
                + jnp.dot(
                    own_states[side],
                    held[side, pl.ds(late, depth - late), near_at],
                    preferred_element_type=F32,
                )
            ).astype(BF16)
            part_ref[pl.ds(rows, rows), whole_at] = jnp.dot(
                far_states[side], held[side, :, near_at], preferred_element_type=F32
            ).astype(BF16)

        strips(at_ref, side, multiply)
        whole = pl.ds(pl.multiple_of(at_ref[1, side] * 1024, 1024), 1024)
        outs.append(
            pltpu.make_async_copy(part_ref.at[:, whole], part_out.at[:, whole], parted.at[side, 0])
        )
        start(outs[side:])
    wait(outs + stores[0] + stores[1])


def project_middle(at, early, xs, pieces, part, head):
    count, depth = len(pieces) // 2, sum(piece.shape[0] for piece in pieces) // 2
    rows = xs[2].shape[0]
    anywhere = pl.BlockSpec(memory_space=pl.ANY)
    ins = [anywhere] * (5 + 2 * count)
    return pl.pallas_call(
        lambda *refs: project_middle_kernel(count, early, *refs),
        in_specs=[pl.BlockSpec(memory_space=pltpu.SMEM)] + ins,
        out_specs=[anywhere] * 2,
        out_shape=[pltpu.HBM((4096, 2048), BF16), pltpu.HBM((2 * rows, 2048), BF16)],
        scratch_shapes=[
            pltpu.VMEM((2, rows, depth - early * BLOCK), BF16),
            pltpu.VMEM((2, rows, depth), BF16),
            pltpu.VMEM((2, depth, 1024), BF16),
            pltpu.VMEM((2 * rows, 2048), BF16),
            pltpu.SemaphoreType.DMA((4, 16)),
            pltpu.SemaphoreType.DMA((2, count)),
            pltpu.SemaphoreType.DMA((2, depth // BLOCK)),
            pltpu.SemaphoreType.DMA((3, 1)),
        ],
        input_output_aliases={len(ins): 0},
        compiler_params=pltpu.CompilerParams(vmem_limit_bytes=36 * 1024 * 1024),
        name="project_middle",
    )(at, *keep_far(*xs, *pieces, part, head))


def project_last_kernel(count, at_ref, *refs):
    x_refs, pieces = refs[:3], refs[3 : 3 + 2 * count]
    part_in, counts_ref, _, head_ref, emb_out, inverse_ref, mixing_ref, first_ref, grad_ref = refs[
        3 + 2 * count : 12 + 2 * count
    ]
    states, held, part_ref, pre_ref, emb_ref, parted, fetched, loaded, stored, sent = refs[12 + 2 * count :]
    late = held.shape[1] // BLOCK
    blocks = list(range(16 - late, 16))
    loads, stores = [], []
    for side in range(2):
        copies = column_copies(at_ref, side, blocks, x_refs, states, fetched.at[side])
        copies += piece_copies(pieces[side * count : (side + 1) * count], held, side, loaded.at[side])
        loads.append(copies)
        stores.append(head_copies(at_ref, held, head_ref, side, blocks, stored.at[side]))
    halves = [pl.ds(pl.multiple_of(at_ref[1, side] * 1024, 1024), 1024) for side in range(2)]
    base = copies_of([(part_in.at[:, at], part_ref.at[:, at]) for at in halves], parted)
    start(loads[0] + base[:1] + loads[1] + base[1:])
    inverse_ref[...] = jnp.zeros(inverse_ref.shape, F32)
    for side in range(2):
        wait(loads[side] + base[side : side + 1])
        if side == 1:
            start(stores[0] + stores[1])

        def multiply(near_at, whole_at, side=side):
            values = part_ref[:, whole_at].astype(F32) + jnp.dot(
                states[side], held[side, :, near_at], preferred_element_type=F32
            )
            pre_ref[:, whole_at] = values
            squares = values * values
            inverse_ref[...] += squares[:, :128] + squares[:, 128:]

        strips(at_ref, side, multiply, 4)
    normalize(pre_ref, emb_ref, inverse_ref)
    sending = copies_of([(emb_ref, emb_out)], sent)
    start(sending)
    contrast(counts_ref, emb_ref, mixing_ref, first_ref, grad_ref)
    wait(sending + stores[0] + stores[1])


def project_last(at, xs, pieces, part, counts, head):
    count, depth = len(pieces) // 2, sum(piece.shape[0] for piece in pieces) // 2
    rows = sum(x.shape[0] for x in xs)
    half = rows // 4
    anywhere = pl.BlockSpec(memory_space=pl.ANY)
    ins = [anywhere] * (4 + 2 * count) + vmem(1) + [anywhere]
    return pl.pallas_call(
        lambda *refs: project_last_kernel(count, *refs),
        in_specs=[pl.BlockSpec(memory_space=pltpu.SMEM)] + ins,
        out_specs=[anywhere] * 2 + vmem(4),
        out_shape=[
            pltpu.HBM((4096, 2048), BF16),
            pltpu.HBM((rows, 2048), BF16),
            pltpu.HBM((rows, 128), F32),
            pltpu.HBM((half, 2 * half), BF16),
            pltpu.HBM((half, 128), F32),
            pltpu.HBM((2 * half, 2048), BF16),
        ],
        scratch_shapes=[
            pltpu.VMEM((2, rows, depth), BF16),
            pltpu.VMEM((2, depth, 1024), BF16),
            pltpu.VMEM((rows, 2048), BF16),
            pltpu.VMEM((rows, 2048), F32),
            pltpu.VMEM((rows, 2048), BF16),
            pltpu.SemaphoreType.DMA((2,)),
            pltpu.SemaphoreType.DMA((2, 3 * depth // BLOCK)),
            pltpu.SemaphoreType.DMA((2, count)),
            pltpu.SemaphoreType.DMA((2, depth // BLOCK)),
            pltpu.SemaphoreType.DMA((1,)),
        ],
        input_output_aliases={len(ins): 0},
        compiler_params=pltpu.CompilerParams(vmem_limit_bytes=30 * 1024 * 1024),
        name="project_last",
    )(at, *keep_far(*xs, *pieces, part), counts, *keep_far(head))


def normalize(pre_ref, emb_ref, inverse_ref):
    chunk = 128
    width = pre_ref.shape[1]

    def some(i, _):
        at = pl.ds(pl.multiple_of(i * chunk, chunk), chunk)
        mean = jnp.sum(inverse_ref[at, :], axis=-1, keepdims=True) * (1.0 / width)
        inverse = jnp.broadcast_to(lax.rsqrt(mean + EPSILON), (chunk, 128))
        inverse_ref[at, :] = inverse
        emb_ref[at, :] = (pre_ref[at, :] * inverse[:, :1]).astype(BF16)
        return 0

    lax.fori_loop(0, pre_ref.shape[0] // chunk, some, 0)


def contrast(counts_ref, emb_ref, mixing_ref, first_ref, grad_ref):
    rows = counts_ref.shape[0]
    scale = 16.0 / emb_ref.shape[1]
    query = emb_ref[pl.ds(0, rows), :]
    passage = emb_ref[pl.ds(rows, rows), :]
    fetched = emb_ref[pl.ds(2 * rows, 2 * rows), :]
    positive = (
        jnp.sum(query.astype(F32) * passage.astype(F32), axis=1, keepdims=True) * scale
    )
    table = dot(query, fetched, ((1,), (1,))) * scale
    counts = counts_ref[...]
    top = jnp.maximum(
        positive, jnp.max(jnp.where(counts > 0, table, -1e30), axis=1, keepdims=True)
    )
    raised = jnp.where(counts > 0, jnp.exp(jnp.where(counts > 0, table - top, 0.0)), 0.0)
    raised_positive = jnp.exp(positive - top)
    whole = raised_positive + jnp.sum(raised * counts, axis=1, keepdims=True)
    first = (raised_positive / whole - 1.0).astype(BF16).astype(F32)
    mixing = ((raised / whole).astype(BF16).astype(F32) * counts).astype(BF16)
    first_ref[...] = jnp.broadcast_to(first, (rows, 128))
    mixing_ref[...] = mixing
    grad_ref[...] = dot(mixing, query, ((0,), (0,))).astype(BF16)


def vmem(count):
    return [pl.BlockSpec(memory_space=pltpu.VMEM)] * count


def near(shape, dtype):
    return pltpu.VMEM(shape, dtype)


def keep_near(*values):
    return [pltpu.with_memory_space_constraint(value, pltpu.VMEM) for value in values]


def keep_far(*values):
    return [pltpu.with_memory_space_constraint(value, pltpu.HBM) for value in values]


def slopes_kernel(part, cols_ref, inverse_hbm, first_hbm, emb_hbm, left_hbm, right_hbm, out_ref, keep_ref, send_ref, grad_ref, inverse_ref, first_ref, emb_ref, own_ref, left_ref, right_ref, sems):
    rows, chunk = out_ref.shape[0], 96
    width = out_ref.shape[1]
    depth = left_ref.shape[1]
    loads = [
        (left_hbm, left_ref),
        (right_hbm.at[pl.ds(2 * rows if part == 0 else 0, depth), :], right_ref),
        (emb_hbm.at[pl.ds((1 - part) * rows, rows), :], emb_ref),
        (first_hbm, first_ref),
        (inverse_hbm.at[pl.ds(part * rows, rows), :], inverse_ref),
        (emb_hbm.at[pl.ds(part * rows, rows), :], own_ref),
    ]
    loads = [pltpu.make_async_copy(*load, sems.at[i]) for i, load in enumerate(loads)]
    for load in loads:
        load.start()
    for load in loads[:2]:
        load.wait()
    grad_ref[...] = jnp.dot(left_ref[...], right_ref[...], preferred_element_type=F32)
    for load in loads[2:]:
        load.wait()

    def some(i, _):
        at = pl.ds(pl.multiple_of(i * chunk, chunk), chunk)
        grad = first_ref[at, :1] * emb_ref[at, :].astype(F32) + grad_ref[at, :]
        values = own_ref[at, :].astype(F32)
        along = jnp.mean(grad * values, axis=-1, keepdims=True)
        out_ref[at, :] = (inverse_ref[at, :1] * (grad - values * along)).astype(BF16)
        return 0

    lax.fori_loop(0, rows // chunk, some, 0)
    for k in range(width // BLOCK // 2):
        for row, ref in ((0, keep_ref), (1, send_ref)):
            col = pl.multiple_of(cols_ref[row, k] * BLOCK, BLOCK)
            ref[:, pl.ds(k * BLOCK, BLOCK)] = out_ref[:, pl.ds(col, BLOCK)]


def slopes_of(part, cols, inverse, first, emb, left, right):
    rows = first.shape[0]
    width = emb.shape[1]
    anywhere = pl.BlockSpec(memory_space=pl.ANY)
    return pl.pallas_call(
        lambda *refs: slopes_kernel(part, *refs),
        in_specs=[pl.BlockSpec(memory_space=pltpu.SMEM)] + [anywhere] * 5,
        out_specs=vmem(3),
        out_shape=[
            jax.ShapeDtypeStruct((rows, width), BF16),
            jax.ShapeDtypeStruct((rows, width // 2), BF16),
            jax.ShapeDtypeStruct((rows, width // 2), BF16),
        ],
        scratch_shapes=[
            pltpu.VMEM((rows, width), F32),
            pltpu.VMEM(first.shape, F32),
            pltpu.VMEM(first.shape, F32),
            pltpu.VMEM((rows, width), BF16),
            pltpu.VMEM((rows, width), BF16),
            pltpu.VMEM(left.shape, BF16),
            pltpu.VMEM((left.shape[1], width), BF16),
            pltpu.SemaphoreType.DMA((6,)),
        ],
        compiler_params=pltpu.CompilerParams(vmem_limit_bytes=16 * 1024 * 1024),
        name="slopes_of",
    )(cols, *keep_far(inverse, first, emb, left), right)


def input_grad_kernel(count, *refs):
    slopes_refs, head_ref, out_refs = refs[:count], refs[count], refs[-count:]
    rows = slopes_refs[0].shape[0]
    slopes = jnp.concatenate([ref[...] for ref in slopes_refs], axis=0)
    grads = dot(slopes, head_ref[...], ((1,), (1,))).astype(BF16)
    for i, ref in enumerate(out_refs):
        ref[...] = grads[i * rows : (i + 1) * rows]


def input_grad(slopes, head, part, filled=()):
    count = len(slopes)
    rows, width = slopes[0].shape
    depth = head.shape[0]
    steps = depth // 512 // 2
    return pl.pallas_call(
        lambda *refs: input_grad_kernel(count, *refs),
        grid=(steps,),
        in_specs=[pl.BlockSpec((rows, width), lambda k: (0, 0))] * count
        + [pl.BlockSpec((512, width), lambda k: (k + part * steps, 0))]
        + [pl.BlockSpec(memory_space=pl.ANY)] * len(filled),
        out_specs=[pl.BlockSpec((rows, 512), lambda k: (0, k + part * steps))] * count,
        out_shape=[jax.ShapeDtypeStruct((rows, depth), BF16)] * count,
        input_output_aliases={count + 1 + i: i for i in range(len(filled))},
        compiler_params=pltpu.CompilerParams(vmem_limit_bytes=20 * 1024 * 1024),
        cost_estimate=pl.CostEstimate(flops=1, transcendentals=0, bytes_accessed=1),
        name="input_grad",
    )(*slopes, *keep_far(head), *filled)


def partial_kernel(outs, adds, at_ref, states_ref, slopes_ref, *refs):
    for i in range(outs):

        def block(k, _, i=i):
            row = pl.multiple_of(at_ref[2 * i + k] * BLOCK, BLOCK)
            part = pl.ds(pl.multiple_of(k * BLOCK, BLOCK), BLOCK)
            total = jnp.dot(
                states_ref[pl.ds(row, BLOCK), :], slopes_ref[...], preferred_element_type=F32
            ) * (1.0 / 128.0)
            for ref in refs[i * adds : (i + 1) * adds]:
                total = total + ref[part, :].astype(F32)
            refs[outs * adds + i][part, :] = total.astype(BF16)
            return 0

        lax.fori_loop(0, 2, block, 0)


def head_partial(states, slopes, at, adds):
    outs, width = len(adds), slopes.shape[1]
    return pl.pallas_call(
        lambda *refs: partial_kernel(outs, len(adds[0]), *refs),
        in_specs=[pl.BlockSpec(memory_space=pltpu.SMEM)] + vmem(2 + outs * len(adds[0])),
        out_specs=vmem(outs),
        out_shape=[jax.ShapeDtypeStruct((2 * BLOCK, width), BF16)] * outs,
        compiler_params=pltpu.CompilerParams(vmem_limit_bytes=20 * 1024 * 1024),
        name="head_partial",
    )(at, *keep_near(states), slopes, *[value for some in adds for value in some])


def add(*values):
    total = values[0].astype(F32)
    for value in values[1:]:
        total = total + value.astype(F32)
    return total.astype(BF16)


def scatter_head(states, slopes, core, head, query_dy, passage_dy, query_grads):
    def part(d1s, d2s, adds):
        at = [block_at(core, d1, d2) for d1, some in zip(d1s, d2s) for d2 in some]
        return head_partial(states, slopes, jnp.stack(at).astype(jnp.int32), adds)

    a, b = (2, 1), (-1, 0)
    far_a, far_b = part((2, 2), (a, b), ((), ()))
    far_a, far_b = shift(far_a, 1, 1), shift(far_b, 1, -1)
    up_b, down_a = part((1, -1), (b, a), ((), ()))
    up_b, down_a, passage_dy = together(up_b, down_a, passage_dy)
    up_b, down_a = shift(up_b, 1, 1), shift(down_a, 1, -1)
    (passage_grads,) = input_grad([passage_dy], head, 0)
    far_a, far_b, passage_grads = together(far_a, far_b, passage_grads)
    up_a, down_b = part((1, -1), (a, b), ((far_a,), (far_b,)))
    up_a, down_b = shift(up_a, 1, 1), shift(down_b, 1, -1)
    mine_a, mine_b = part((0, 0), (a, b), ((down_a,), (up_b,)))
    mine_a, mine_b, passage_dy = together(mine_a, mine_b, passage_dy)
    grads = input_grad([query_dy, passage_dy], head, 1, [query_grads, passage_grads])
    up_a, down_b, mine_a, mine_b, *grads = together(up_a, down_b, mine_a, mine_b, *grads)
    half = BLOCK // 2
    far, up = mine_a[:BLOCK], mine_a[BLOCK:]
    down, mine = mine_b[:BLOCK], mine_b[BLOCK:]
    up_far, up_up = up_a[:BLOCK], up_a[BLOCK:]
    down_down, down_mine = down_b[:BLOCK], down_b[BLOCK:]
    far_a = shift(add(far[:half], up_far[:half]), 2, 1)
    far_b = shift(add(far[half:], up_far[half:]), 2, -1)
    up_b = shift(add(up[half:], up_up[half:]), 2, 1)
    down_a = shift(add(down[:half], down_down[:half]), 2, -1)
    far_a, far_b, up_b, down_a = together(far_a, far_b, up_b, down_a)
    up_a = shift(add(up[:half], up_up[:half], far_a), 2, 1)
    down_b = shift(add(down[half:], down_down[half:], far_b), 2, -1)
    up_a, down_b = together(up_a, down_b)
    total = jnp.concatenate(
        [
            add(mine[:half], down_mine[:half], down_a, up_a),
            add(mine[half:], down_mine[half:], up_b, down_b),
        ],
        axis=0,
    )
    arrived = together(
        *[
            lax.ppermute(
                total[:, step * BLOCK : (step + 1) * BLOCK],
                "x",
                [(i, (i + step) % RING) for i in range(RING)],
            )
            for step in (2, 1, 3)
        ]
    )
    out = total[:, :BLOCK].astype(F32)
    for value in arrived:
        out = out + value.astype(F32)
    return out, *grads


def dot(a, b, contract=((1,), (0,))):
    return lax.dot_general(a, b, (contract, ((), ())), preferred_element_type=F32)


def per_device(queries, passages, head_weight, send_lists, neg_slots):
    core, x = lax.axis_index("c"), lax.axis_index("x")
    rows_dev, depth = queries.shape
    width = head_weight.shape[1]
    groups, capacity = send_lists.shape[2], send_lists.shape[3]
    slot_count = groups * capacity
    flat_lists = send_lists.reshape(slot_count)

    owner = (flat_lists[None, :] == jnp.arange(rows_dev, dtype=jnp.int32)[:, None]).astype(BF16)
    own = lax.dynamic_slice_in_dim(head_weight, core * (width // 2), width // 2, axis=1)

    up, down = shift(own, 1, 1), shift(own, 1, -1)
    picked = dot(owner, passages, ((0,), (0,))).astype(BF16).reshape(groups, capacity, depth)
    own, picked = together(own, picked)
    own_up, own_down = shift(own, 2, 1), shift(own, 2, -1)
    arrived = lax.all_to_all(picked, ("x", "c"), split_axis=0, concat_axis=0, tiled=True)
    arrived = arrived.reshape(slot_count, depth)

    far = shift(up, 1, 1)
    up_up, up_down = shift(up, 2, 1), shift(up, 2, -1)
    slot_ids = jnp.arange(slot_count, dtype=jnp.int32)[None, :]
    counts = jnp.zeros((rows_dev, slot_count), F32)
    for j in range(neg_slots.shape[1]):
        counts = counts + (neg_slots[:, j : j + 1] == slot_ids).astype(F32)
    far, up_up, up_down, own_up, own_down, counts, owner = together(
        far, up_up, up_down, own_up, own_down, counts, owner
    )

    second = jnp.concatenate([down, far], axis=0)
    second_up, second_down = shift(second, 2, 1), shift(second, 2, -1)
    first_up = jnp.concatenate([own_up, up_up], axis=0)
    early = [own, up, second, first_up, own_down, up_down]
    early = early, [swap(piece) for piece in early]
    places = [(0, 0), (-1, 0), (1, 0), (2, 0), (0, -1), (-1, -1), (0, 1), (-1, 1)]
    places += [(1, -1), (2, -1), (1, 1), (2, 1), (0, 2), (-1, 2), (1, 2), (2, 2)]
    at = [block_at(core, *place) for place in places] + [block_at(1 - core, *place) for place in places]
    side = [core, 1 - core] + [core] * 30
    at = jnp.stack([jnp.stack(at), jnp.stack(side)]).astype(jnp.int32)
    xs = queries, passages, arrived
    head, part = project_early(at, xs[:2], early[0] + early[1])
    second_up, second_down, first_up, part = together(second_up, second_down, first_up, part)

    first_far, second_far = shift(first_up, 2, 1), shift(second_down, 2, -1)
    middle = [second_up, second_down]
    other_middle = [swap(piece) for piece in middle]
    head, part = project_middle(at, 8, xs, early[0] + middle + early[1] + other_middle, part, head)
    first_far, second_far, part = together(first_far, second_far, part)
    late = [first_far, second_far, swap(first_far), swap(second_far)]
    head, emb, inverse, mixing, first, fetched_grad = project_last(at, xs, late, part, counts, head)
    returned = lax.all_to_all(
        fetched_grad.reshape(groups, capacity, width),
        ("x", "c"),
        split_axis=0,
        concat_axis=0,
        tiled=True,
    ).reshape(slot_count, width)

    to_x = [(x + step) % RING for step in range(RING)]
    cols = jnp.stack(
        [jnp.stack([2 * to + core for to in to_x]), jnp.stack([2 * to + 1 - core for to in to_x])]
    ).astype(jnp.int32)
    query_states, passage_states, first = together(queries, passages, first)
    query_dy, query_keep, query_send = slopes_of(0, cols, inverse, first, emb, mixing, emb)
    turned = turn(query_states, passage_states, swap(query_states), swap(passage_states))
    (query_grads,) = input_grad([query_dy], head, 0)
    returned, query_grads, query_send, turned = together(returned, query_grads, query_send, turned)
    query_other = swap(query_send)

    passage_dy, passage_keep, passage_send = slopes_of(
        1, cols, inverse, first, emb, owner, returned
    )
    passage_other = swap(passage_send)
    slopes = jnp.concatenate([query_keep, passage_keep, query_other, passage_other], axis=0)
    head_grads, query_grads, passage_grads = scatter_head(
        turned, slopes, core, head, query_dy, passage_dy, query_grads
    )
    return (query_grads, passage_grads, head_grads)


def solution(mesh):
    fine = Mesh(mesh.devices.reshape(4, 2, 4, 4), ("x", "c", "y", "z"))
    every = ("x", "c", "y", "z")
    return jax.shard_map(
        per_device,
        mesh=fine,
        in_specs=(
            P(every, None),
            P(every, None),
            P(("y", "z"), None),
            P(("x", "c"), ("y", "z"), None, None),
            P(every, None),
        ),
        out_specs=(P(every, None), P(every, None), P(("y", "z"), ("x", "c"))),
        check_vma=False,
    )
```

```python
import jax
import jax.numpy as jnp
from jax import lax
from jax.experimental import pallas as pl
from jax.experimental.pallas import tpu as pltpu
from jax.sharding import Mesh, PartitionSpec as P

EPSILON = 1e-06
BLOCK = 256
RING = 4
SWAP = [(0, 1), (1, 0)]
BF16 = jnp.bfloat16
F32 = jnp.float32


def shift(value, place, step):
    pairs = []
    for c in range(2):
        for y in range(RING):
            for z in range(RING):
                to_y, to_z = y, z
                if (place == 1) == (c == 0):
                    to_y = (y + step) % RING
                else:
                    to_z = (z + step) % RING
                pairs.append((c * 16 + y * 4 + z, c * 16 + to_y * 4 + to_z))
    return lax.ppermute(value, ("c", "y", "z"), pairs)


def swap(value):
    return lax.ppermute(value, "c", SWAP)


def block_at(core, d1, d2):
    y, z = lax.axis_index("y"), lax.axis_index("z")
    far_y = jnp.where(core == 0, d1, d2)
    far_z = jnp.where(core == 0, d2, d1)
    return ((y + far_y) % RING) * RING + (z + far_z) % RING


def together(*values):
    return lax.optimization_barrier(values)


def turn_kernel(*refs):
    parts = 4
    x_refs, turned_ref, held, turned, loaded, stored = refs[:4], *refs[4:]
    rows, depth = x_refs[0].shape
    size = depth // parts
    loads, stores = [], []
    for i in range(parts):
        at = pl.ds(i * size, size)
        loads.append(
            [
                pltpu.make_async_copy(ref.at[:, at], held.at[pl.ds(j * rows, rows), at], loaded.at[i, j])
                for j, ref in enumerate(x_refs)
            ]
        )
        stores.append(pltpu.make_async_copy(turned.at[at, :], turned_ref.at[at, :], stored.at[i]))
    for load in loads:
        start(load)
    for i in range(parts):
        wait(loads[i])
        for k in range(size // BLOCK):
            at = pl.ds(i * size + k * BLOCK, BLOCK)
            turned[at, :] = held[:, at].T
        stores[i].start()
    wait(stores)


def turn(*states):
    rows, depth = states[0].shape
    whole = rows * len(states)
    anywhere = pl.BlockSpec(memory_space=pl.ANY)
    return pl.pallas_call(
        turn_kernel,
        in_specs=[anywhere] * len(states),
        out_specs=anywhere,
        out_shape=pltpu.HBM((depth, whole), BF16),
        scratch_shapes=[
            pltpu.VMEM((whole, depth), BF16),
            pltpu.VMEM((depth, whole), BF16),
            pltpu.SemaphoreType.DMA((4, len(states))),
            pltpu.SemaphoreType.DMA((4,)),
        ],
        compiler_params=pltpu.CompilerParams(vmem_limit_bytes=20 * 1024 * 1024),
        cost_estimate=pl.CostEstimate(flops=1, transcendentals=0, bytes_accessed=1),
        name="turn",
    )(*keep_far(*states[:2]), *states[2:])


def copies_of(pairs, sems):
    return [pltpu.make_async_copy(*pair, sems.at[i]) for i, pair in enumerate(pairs)]


def start(copies):
    for copy in copies:
        copy.start()


def wait(copies):
    for copy in copies:
        copy.wait()


def head_copies(at_ref, held, head_ref, side, blocks, sems):
    col = pl.multiple_of(at_ref[1, side] * 1024, 1024)
    pairs = []
    for k in blocks:
        row = pl.multiple_of(at_ref[0, 16 * side + k] * BLOCK, BLOCK)
        pairs.append(
            (
                held.at[side, pl.ds((k - blocks[0]) * BLOCK, BLOCK), :],
                head_ref.at[pl.ds(row, BLOCK), pl.ds(col, 1024)],
            )
        )
    return copies_of(pairs, sems)


def piece_copies(pieces, held, side, sems):
    row, pairs = 0, []
    for piece in pieces:
        pairs.append((piece, held.at[side, pl.ds(row, piece.shape[0]), :]))
        row += piece.shape[0]
    return copies_of(pairs, sems)


def column_copies(at_ref, side, blocks, sources, states, sems):
    pairs = []
    for i, k in enumerate(blocks):
        col, row = pl.multiple_of(at_ref[0, 16 * side + k] * BLOCK, BLOCK), 0
        for ref in sources:
            to = states.at[side, pl.ds(row, ref.shape[0]), pl.ds(i * BLOCK, BLOCK)]
            pairs.append((ref.at[:, pl.ds(col, BLOCK)], to))
            row += ref.shape[0]
    return copies_of(pairs, sems)


def strips(at_ref, side, body, unroll=1):
    def one(n, _):
        at_col = pl.multiple_of(n * BLOCK, BLOCK)
        body(pl.ds(at_col, BLOCK), pl.ds(pl.multiple_of(at_ref[1, side] * 1024 + at_col, BLOCK), BLOCK))
        return 0

    lax.fori_loop(0, 1024 // BLOCK, one, 0, unroll=unroll)


def project_early_kernel(count, at_ref, *refs):
    x_refs, pieces = refs[:2], refs[2 : 2 + 2 * count]
    head_ref, part_out, states, held, part_ref, fetched, loaded, stored, parted = refs[2 + 2 * count :]
    blocks = list(range(held.shape[1] // BLOCK))
    loads = [
        column_copies(at_ref, i, blocks, x_refs, states, fetched.at[i])
        + piece_copies(pieces[i * count : (i + 1) * count], held, i, loaded.at[i])
        for i in range(2)
    ]
    stores = [head_copies(at_ref, held, head_ref, i, blocks, stored.at[i]) for i in range(2)]
    outs = []
    start(loads[0])
    for side in range(2):
        wait(loads[side])
        start(loads[1] if side == 0 else stores[0] + stores[1])

        def multiply(near_at, whole_at, side=side):
            part_ref[:, whole_at] = jnp.dot(
                states[side], held[side, :, near_at], preferred_element_type=F32
            ).astype(BF16)

        strips(at_ref, side, multiply)
        whole = pl.ds(pl.multiple_of(at_ref[1, side] * 1024, 1024), 1024)
        outs.append(pltpu.make_async_copy(part_ref.at[:, whole], part_out.at[:, whole], parted.at[side]))
        start(outs[side:])
    wait(outs + stores[0] + stores[1])


def project_early(at, xs, pieces):
    count, depth = len(pieces) // 2, sum(piece.shape[0] for piece in pieces) // 2
    rows = sum(x.shape[0] for x in xs)
    anywhere = pl.BlockSpec(memory_space=pl.ANY)
    return pl.pallas_call(
        lambda *refs: project_early_kernel(count, *refs),
        in_specs=[pl.BlockSpec(memory_space=pltpu.SMEM)] + [anywhere] * (2 + 2 * count),
        out_specs=[anywhere] * 2,
        out_shape=[pltpu.HBM((4096, 2048), BF16), pltpu.HBM((rows, 2048), BF16)],
        scratch_shapes=[
            pltpu.VMEM((2, rows, depth), BF16),
            pltpu.VMEM((2, depth, 1024), BF16),
            pltpu.VMEM((rows, 2048), BF16),
            pltpu.SemaphoreType.DMA((2, 2 * depth // BLOCK)),
            pltpu.SemaphoreType.DMA((2, count)),
            pltpu.SemaphoreType.DMA((2, depth // BLOCK)),
            pltpu.SemaphoreType.DMA((2,)),
        ],
        compiler_params=pltpu.CompilerParams(vmem_limit_bytes=24 * 1024 * 1024),
        name="project_early",
    )(at, *keep_far(*xs, *pieces))


def project_middle_kernel(count, early, at_ref, *refs):
    x_refs, pieces = refs[:3], refs[3 : 3 + 2 * count]
    part_in, _, head_ref, part_out = refs[3 + 2 * count : 7 + 2 * count]
    own_states, far_states, held, part_ref, fetched, loaded, stored, parted = refs[7 + 2 * count :]
    rows, depth = far_states.shape[1], held.shape[1]
    blocks = list(range(depth // BLOCK))
    late = early * BLOCK
    base = copies_of([(part_in, part_ref.at[pl.ds(0, rows), :])], parted.at[2])
    loads = [
        column_copies(at_ref, i, blocks, x_refs[2:], far_states, fetched.at[2 * i])
        + piece_copies(pieces[i * count : (i + 1) * count], held, i, loaded.at[i])
        + column_copies(at_ref, i, blocks[early:], x_refs[:2], own_states, fetched.at[2 * i + 1])
        for i in range(2)
    ]
    stores = [head_copies(at_ref, held, head_ref, i, blocks, stored.at[i])[early:] for i in range(2)]
    outs = []
    start(loads[0] + base)
    for side in range(2):
        wait(loads[side])
        start(loads[1] if side == 0 else stores[0] + stores[1])
        if side == 0:
            wait(base)

        def multiply(near_at, whole_at, side=side):
            own_at = pl.ds(0, rows)
            part_ref[own_at, whole_at] = (
                part_ref[own_at, whole_at].astype(F32)
                + jnp.dot(
                    own_states[side],
                    held[side, pl.ds(late, depth - late), near_at],
                    preferred_element_type=F32,
                )
            ).astype(BF16)
            part_ref[pl.ds(rows, rows), whole_at] = jnp.dot(
                far_states[side], held[side, :, near_at], preferred_element_type=F32
            ).astype(BF16)

        strips(at_ref, side, multiply)
        whole = pl.ds(pl.multiple_of(at_ref[1, side] * 1024, 1024), 1024)
        outs.append(
            pltpu.make_async_copy(part_ref.at[:, whole], part_out.at[:, whole], parted.at[side, 0])
        )
        start(outs[side:])
    wait(outs + stores[0] + stores[1])


def project_middle(at, early, xs, pieces, part, head):
    count, depth = len(pieces) // 2, sum(piece.shape[0] for piece in pieces) // 2
    rows = xs[2].shape[0]
    anywhere = pl.BlockSpec(memory_space=pl.ANY)
    ins = [anywhere] * (5 + 2 * count)
    return pl.pallas_call(
        lambda *refs: project_middle_kernel(count, early, *refs),
        in_specs=[pl.BlockSpec(memory_space=pltpu.SMEM)] + ins,
        out_specs=[anywhere] * 2,
        out_shape=[pltpu.HBM((4096, 2048), BF16), pltpu.HBM((2 * rows, 2048), BF16)],
        scratch_shapes=[
            pltpu.VMEM((2, rows, depth - early * BLOCK), BF16),
            pltpu.VMEM((2, rows, depth), BF16),
            pltpu.VMEM((2, depth, 1024), BF16),
            pltpu.VMEM((2 * rows, 2048), BF16),
            pltpu.SemaphoreType.DMA((4, 16)),
            pltpu.SemaphoreType.DMA((2, count)),
            pltpu.SemaphoreType.DMA((2, depth // BLOCK)),
            pltpu.SemaphoreType.DMA((3, 1)),
        ],
        input_output_aliases={len(ins): 0},
        compiler_params=pltpu.CompilerParams(vmem_limit_bytes=36 * 1024 * 1024),
        name="project_middle",
    )(at, *keep_far(*xs), *pieces, *keep_far(part, head))


def project_last_kernel(count, at_ref, *refs):
    x_refs, pieces = refs[:3], refs[3 : 3 + 2 * count]
    part_in, counts_ref, _, head_ref, emb_out, inverse_ref, mixing_ref, first_ref, grad_ref = refs[
        3 + 2 * count : 12 + 2 * count
    ]
    states, held, part_ref, pre_ref, emb_ref, parted, fetched, loaded, stored, sent = refs[12 + 2 * count :]
    late = held.shape[1] // BLOCK
    blocks = list(range(16 - late, 16))
    loads, stores = [], []
    for side in range(2):
        copies = column_copies(at_ref, side, blocks, x_refs, states, fetched.at[side])
        copies += piece_copies(pieces[side * count : (side + 1) * count], held, side, loaded.at[side])
        loads.append(copies)
        stores.append(head_copies(at_ref, held, head_ref, side, blocks, stored.at[side]))
    halves = [pl.ds(pl.multiple_of(at_ref[1, side] * 1024, 1024), 1024) for side in range(2)]
    base = copies_of([(part_in.at[:, at], part_ref.at[:, at]) for at in halves], parted)
    start(loads[0] + base[:1] + loads[1] + base[1:])
    inverse_ref[...] = jnp.zeros(inverse_ref.shape, F32)
    for side in range(2):
        wait(loads[side] + base[side : side + 1])
        if side == 1:
            start(stores[0] + stores[1])

        def multiply(near_at, whole_at, side=side):
            values = part_ref[:, whole_at].astype(F32) + jnp.dot(
                states[side], held[side, :, near_at], preferred_element_type=F32
            )
            pre_ref[:, whole_at] = values
            squares = values * values
            inverse_ref[...] += squares[:, :128] + squares[:, 128:]

        strips(at_ref, side, multiply, 4)
    normalize(pre_ref, emb_ref, inverse_ref)
    sending = copies_of([(emb_ref, emb_out)], sent)
    start(sending)
    contrast(counts_ref, emb_ref, mixing_ref, first_ref, grad_ref)
    wait(sending + stores[0] + stores[1])


def project_last(at, xs, pieces, part, counts, head):
    count, depth = len(pieces) // 2, sum(piece.shape[0] for piece in pieces) // 2
    rows = sum(x.shape[0] for x in xs)
    half = rows // 4
    anywhere = pl.BlockSpec(memory_space=pl.ANY)
    ins = [anywhere] * (4 + 2 * count) + vmem(1) + [anywhere]
    return pl.pallas_call(
        lambda *refs: project_last_kernel(count, *refs),
        in_specs=[pl.BlockSpec(memory_space=pltpu.SMEM)] + ins,
        out_specs=[anywhere] * 2 + vmem(4),
        out_shape=[
            pltpu.HBM((4096, 2048), BF16),
            pltpu.HBM((rows, 2048), BF16),
            pltpu.HBM((rows, 128), F32),
            pltpu.HBM((half, 2 * half), BF16),
            pltpu.HBM((half, 128), F32),
            pltpu.HBM((2 * half, 2048), BF16),
        ],
        scratch_shapes=[
            pltpu.VMEM((2, rows, depth), BF16),
            pltpu.VMEM((2, depth, 1024), BF16),
            pltpu.VMEM((rows, 2048), BF16),
            pltpu.VMEM((rows, 2048), F32),
            pltpu.VMEM((rows, 2048), BF16),
            pltpu.SemaphoreType.DMA((2,)),
            pltpu.SemaphoreType.DMA((2, 3 * depth // BLOCK)),
            pltpu.SemaphoreType.DMA((2, count)),
            pltpu.SemaphoreType.DMA((2, depth // BLOCK)),
            pltpu.SemaphoreType.DMA((1,)),
        ],
        input_output_aliases={len(ins): 0},
        compiler_params=pltpu.CompilerParams(vmem_limit_bytes=30 * 1024 * 1024),
        name="project_last",
    )(at, *keep_far(*xs), *pieces, *keep_far(part), counts, *keep_far(head))


def normalize(pre_ref, emb_ref, inverse_ref):
    chunk = 128
    width = pre_ref.shape[1]

    def some(i, _):
        at = pl.ds(pl.multiple_of(i * chunk, chunk), chunk)
        mean = jnp.sum(inverse_ref[at, :], axis=-1, keepdims=True) * (1.0 / width)
        inverse = jnp.broadcast_to(lax.rsqrt(mean + EPSILON), (chunk, 128))
        inverse_ref[at, :] = inverse
        emb_ref[at, :] = (pre_ref[at, :] * inverse[:, :1]).astype(BF16)
        return 0

    lax.fori_loop(0, pre_ref.shape[0] // chunk, some, 0)


def contrast(counts_ref, emb_ref, mixing_ref, first_ref, grad_ref):
    rows = counts_ref.shape[0]
    scale = 16.0 / emb_ref.shape[1]
    query = emb_ref[pl.ds(0, rows), :]
    passage = emb_ref[pl.ds(rows, rows), :]
    fetched = emb_ref[pl.ds(2 * rows, 2 * rows), :]
    positive = (
        jnp.sum(query.astype(F32) * passage.astype(F32), axis=1, keepdims=True) * scale
    )
    table = dot(query, fetched, ((1,), (1,))) * scale
    counts = counts_ref[...]
    top = jnp.maximum(
        positive, jnp.max(jnp.where(counts > 0, table, -1e30), axis=1, keepdims=True)
    )
    raised = jnp.where(counts > 0, jnp.exp(jnp.where(counts > 0, table - top, 0.0)), 0.0)
    raised_positive = jnp.exp(positive - top)
    whole = raised_positive + jnp.sum(raised * counts, axis=1, keepdims=True)
    first = (raised_positive / whole - 1.0).astype(BF16).astype(F32)
    mixing = ((raised / whole).astype(BF16).astype(F32) * counts).astype(BF16)
    first_ref[...] = jnp.broadcast_to(first, (rows, 128))
    mixing_ref[...] = mixing
    grad_ref[...] = dot(mixing, query, ((0,), (0,))).astype(BF16)


def vmem(count):
    return [pl.BlockSpec(memory_space=pltpu.VMEM)] * count


def near(shape, dtype):
    return pltpu.VMEM(shape, dtype)


def keep_near(*values):
    return [pltpu.with_memory_space_constraint(value, pltpu.VMEM) for value in values]


def keep_far(*values):
    return [pltpu.with_memory_space_constraint(value, pltpu.HBM) for value in values]


def slopes_kernel(part, cols_ref, inverse_hbm, first_hbm, emb_hbm, left_hbm, right_hbm, out_ref, keep_ref, send_ref, grad_ref, inverse_ref, first_ref, emb_ref, own_ref, left_ref, right_ref, sems):
    rows, chunk = out_ref.shape[0], 96
    width = out_ref.shape[1]
    depth = left_ref.shape[1]
    loads = [
        (left_hbm, left_ref),
        (right_hbm.at[pl.ds(2 * rows if part == 0 else 0, depth), :], right_ref),
        (emb_hbm.at[pl.ds((1 - part) * rows, rows), :], emb_ref),
        (first_hbm, first_ref),
        (inverse_hbm.at[pl.ds(part * rows, rows), :], inverse_ref),
        (emb_hbm.at[pl.ds(part * rows, rows), :], own_ref),
    ]
    loads = [pltpu.make_async_copy(*load, sems.at[i]) for i, load in enumerate(loads)]
    for load in loads:
        load.start()
    for load in loads[:2]:
        load.wait()
    grad_ref[...] = jnp.dot(left_ref[...], right_ref[...], preferred_element_type=F32)
    for load in loads[2:]:
        load.wait()

    def some(i, _):
        at = pl.ds(pl.multiple_of(i * chunk, chunk), chunk)
        grad = first_ref[at, :1] * emb_ref[at, :].astype(F32) + grad_ref[at, :]
        values = own_ref[at, :].astype(F32)
        along = jnp.mean(grad * values, axis=-1, keepdims=True)
        out_ref[at, :] = (inverse_ref[at, :1] * (grad - values * along)).astype(BF16)
        return 0

    lax.fori_loop(0, rows // chunk, some, 0)
    for k in range(width // BLOCK // 2):
        for row, ref in ((0, keep_ref), (1, send_ref)):
            col = pl.multiple_of(cols_ref[row, k] * BLOCK, BLOCK)
            ref[:, pl.ds(k * BLOCK, BLOCK)] = out_ref[:, pl.ds(col, BLOCK)]


def slopes_of(part, cols, inverse, first, emb, left, right):
    rows = first.shape[0]
    width = emb.shape[1]
    anywhere = pl.BlockSpec(memory_space=pl.ANY)
    return pl.pallas_call(
        lambda *refs: slopes_kernel(part, *refs),
        in_specs=[pl.BlockSpec(memory_space=pltpu.SMEM)] + [anywhere] * 5,
        out_specs=vmem(3),
        out_shape=[
            jax.ShapeDtypeStruct((rows, width), BF16),
            jax.ShapeDtypeStruct((rows, width // 2), BF16),
            jax.ShapeDtypeStruct((rows, width // 2), BF16),
        ],
        scratch_shapes=[
            pltpu.VMEM((rows, width), F32),
            pltpu.VMEM(first.shape, F32),
            pltpu.VMEM(first.shape, F32),
            pltpu.VMEM((rows, width), BF16),
            pltpu.VMEM((rows, width), BF16),
            pltpu.VMEM(left.shape, BF16),
            pltpu.VMEM((left.shape[1], width), BF16),
            pltpu.SemaphoreType.DMA((6,)),
        ],
        compiler_params=pltpu.CompilerParams(vmem_limit_bytes=16 * 1024 * 1024),
        name="slopes_of",
    )(cols, *keep_far(inverse, first, emb, left), right)


def input_grad_kernel(count, *refs):
    slopes_refs, head_ref, out_refs = refs[:count], refs[count], refs[-count:]
    rows = slopes_refs[0].shape[0]
    slopes = jnp.concatenate([ref[...] for ref in slopes_refs], axis=0)
    grads = dot(slopes, head_ref[...], ((1,), (1,))).astype(BF16)
    for i, ref in enumerate(out_refs):
        ref[...] = grads[i * rows : (i + 1) * rows]


def input_grad(slopes, head, part, filled=()):
    count = len(slopes)
    rows, width = slopes[0].shape
    depth = head.shape[0]
    steps = depth // 512 // 2
    return pl.pallas_call(
        lambda *refs: input_grad_kernel(count, *refs),
        grid=(steps,),
        in_specs=[pl.BlockSpec((rows, width), lambda k: (0, 0))] * count
        + [pl.BlockSpec((512, width), lambda k: (k + part * steps, 0))]
        + [pl.BlockSpec(memory_space=pl.ANY)] * len(filled),
        out_specs=[pl.BlockSpec((rows, 512), lambda k: (0, k + part * steps))] * count,
        out_shape=[jax.ShapeDtypeStruct((rows, depth), BF16)] * count,
        input_output_aliases={count + 1 + i: i for i in range(len(filled))},
        compiler_params=pltpu.CompilerParams(vmem_limit_bytes=20 * 1024 * 1024),
        cost_estimate=pl.CostEstimate(flops=1, transcendentals=0, bytes_accessed=1),
        name="input_grad",
    )(*slopes, *keep_far(head), *filled)


def partial_kernel(outs, adds, at_ref, states_ref, slopes_ref, *refs):
    for i in range(outs):

        def block(k, _, i=i):
            row = pl.multiple_of(at_ref[2 * i + k] * BLOCK, BLOCK)
            part = pl.ds(pl.multiple_of(k * BLOCK, BLOCK), BLOCK)
            total = jnp.dot(
                states_ref[pl.ds(row, BLOCK), :], slopes_ref[...], preferred_element_type=F32
            ) * (1.0 / 128.0)
            for ref in refs[i * adds : (i + 1) * adds]:
                total = total + ref[part, :].astype(F32)
            refs[outs * adds + i][part, :] = total.astype(BF16)
            return 0

        lax.fori_loop(0, 2, block, 0)


def head_partial(states, slopes, at, adds):
    outs, width = len(adds), slopes.shape[1]
    return pl.pallas_call(
        lambda *refs: partial_kernel(outs, len(adds[0]), *refs),
        in_specs=[pl.BlockSpec(memory_space=pltpu.SMEM)] + vmem(2 + outs * len(adds[0])),
        out_specs=vmem(outs),
        out_shape=[jax.ShapeDtypeStruct((2 * BLOCK, width), BF16)] * outs,
        compiler_params=pltpu.CompilerParams(vmem_limit_bytes=20 * 1024 * 1024),
        name="head_partial",
    )(at, *keep_near(states), slopes, *[value for some in adds for value in some])


def add(*values):
    total = values[0].astype(F32)
    for value in values[1:]:
        total = total + value.astype(F32)
    return total.astype(BF16)


def scatter_head(states, slopes, core, head, query_dy, passage_dy, query_grads):
    def part(d1s, d2s, adds):
        at = [block_at(core, d1, d2) for d1, some in zip(d1s, d2s) for d2 in some]
        return head_partial(states, slopes, jnp.stack(at).astype(jnp.int32), adds)

    a, b = (2, 1), (-1, 0)
    far_a, far_b = part((2, 2), (a, b), ((), ()))
    far_a, far_b = shift(far_a, 1, 1), shift(far_b, 1, -1)
    up_b, down_a = part((1, -1), (b, a), ((), ()))
    up_b, down_a, passage_dy = together(up_b, down_a, passage_dy)
    up_b, down_a = shift(up_b, 1, 1), shift(down_a, 1, -1)
    (passage_grads,) = input_grad([passage_dy], head, 0)
    far_a, far_b, passage_grads = together(far_a, far_b, passage_grads)
    up_a, down_b = part((1, -1), (a, b), ((far_a,), (far_b,)))
    up_a, down_b = shift(up_a, 1, 1), shift(down_b, 1, -1)
    mine_a, mine_b = part((0, 0), (a, b), ((down_a,), (up_b,)))
    mine_a, mine_b, passage_dy = together(mine_a, mine_b, passage_dy)
    grads = input_grad([query_dy, passage_dy], head, 1, [query_grads, passage_grads])
    up_a, down_b, mine_a, mine_b, *grads = together(up_a, down_b, mine_a, mine_b, *grads)
    half = BLOCK // 2
    far, up = mine_a[:BLOCK], mine_a[BLOCK:]
    down, mine = mine_b[:BLOCK], mine_b[BLOCK:]
    up_far, up_up = up_a[:BLOCK], up_a[BLOCK:]
    down_down, down_mine = down_b[:BLOCK], down_b[BLOCK:]
    far_a = shift(add(far[:half], up_far[:half]), 2, 1)
    far_b = shift(add(far[half:], up_far[half:]), 2, -1)
    up_b = shift(add(up[half:], up_up[half:]), 2, 1)
    down_a = shift(add(down[:half], down_down[:half]), 2, -1)
    far_a, far_b, up_b, down_a = together(far_a, far_b, up_b, down_a)
    up_a = shift(add(up[:half], up_up[:half], far_a), 2, 1)
    down_b = shift(add(down[half:], down_down[half:], far_b), 2, -1)
    up_a, down_b = together(up_a, down_b)
    total = jnp.concatenate(
        [
            add(mine[:half], down_mine[:half], down_a, up_a),
            add(mine[half:], down_mine[half:], up_b, down_b),
        ],
        axis=0,
    )
    arrived = together(
        *[
            lax.ppermute(
                total[:, step * BLOCK : (step + 1) * BLOCK],
                "x",
                [(i, (i + step) % RING) for i in range(RING)],
            )
            for step in (2, 1, 3)
        ]
    )
    out = total[:, :BLOCK].astype(F32)
    for value in arrived:
        out = out + value.astype(F32)
    return out, *grads


def dot(a, b, contract=((1,), (0,))):
    return lax.dot_general(a, b, (contract, ((), ())), preferred_element_type=F32)


def per_device(queries, passages, head_weight, send_lists, neg_slots):
    core, x = lax.axis_index("c"), lax.axis_index("x")
    rows_dev, depth = queries.shape
    width = head_weight.shape[1]
    groups, capacity = send_lists.shape[2], send_lists.shape[3]
    slot_count = groups * capacity
    flat_lists = send_lists.reshape(slot_count)

    owner = (flat_lists[None, :] == jnp.arange(rows_dev, dtype=jnp.int32)[:, None]).astype(BF16)
    own = lax.dynamic_slice_in_dim(head_weight, core * (width // 2), width // 2, axis=1)

    up, down = shift(own, 1, 1), shift(own, 1, -1)
    picked = dot(owner, passages, ((0,), (0,))).astype(BF16).reshape(groups, capacity, depth)
    own, picked = together(own, picked)
    own_up, own_down = shift(own, 2, 1), shift(own, 2, -1)
    arrived = lax.all_to_all(picked, ("x", "c"), split_axis=0, concat_axis=0, tiled=True)
    arrived = arrived.reshape(slot_count, depth)

    far = shift(up, 1, 1)
    up_up, up_down = shift(up, 2, 1), shift(up, 2, -1)
    slot_ids = jnp.arange(slot_count, dtype=jnp.int32)[None, :]
    counts = jnp.zeros((rows_dev, slot_count), F32)
    for j in range(neg_slots.shape[1]):
        counts = counts + (neg_slots[:, j : j + 1] == slot_ids).astype(F32)
    far, up_up, up_down, own_up, own_down, counts, owner = together(
        far, up_up, up_down, own_up, own_down, counts, owner
    )

    second = jnp.concatenate([down, far], axis=0)
    second_up, second_down = shift(second, 2, 1), shift(second, 2, -1)
    first_up = jnp.concatenate([own_up, up_up], axis=0)
    early = [own, up, second, first_up, own_down, up_down]
    early = early, [swap(piece) for piece in early]
    places = [(0, 0), (-1, 0), (1, 0), (2, 0), (0, -1), (-1, -1), (0, 1), (-1, 1)]
    places += [(1, -1), (2, -1), (1, 1), (2, 1), (0, 2), (-1, 2), (1, 2), (2, 2)]
    at = [block_at(core, *place) for place in places] + [block_at(1 - core, *place) for place in places]
    side = [core, 1 - core] + [core] * 30
    at = jnp.stack([jnp.stack(at), jnp.stack(side)]).astype(jnp.int32)
    xs = queries, passages, arrived
    head, part = project_early(at, xs[:2], early[0] + early[1])
    second_up, second_down, first_up, part = together(second_up, second_down, first_up, part)

    first_far, second_far = shift(first_up, 2, 1), shift(second_down, 2, -1)
    middle = [second_up, second_down]
    other_middle = [swap(piece) for piece in middle]
    early = [keep_far(*some) for some in early]
    head, part = project_middle(at, 8, xs, early[0] + middle + early[1] + other_middle, part, head)
    first_far, second_far, part = together(first_far, second_far, part)
    late = [first_far, second_far, swap(first_far), swap(second_far)]
    head, emb, inverse, mixing, first, fetched_grad = project_last(at, xs, late, part, counts, head)
    returned = lax.all_to_all(
        fetched_grad.reshape(groups, capacity, width),
        ("x", "c"),
        split_axis=0,
        concat_axis=0,
        tiled=True,
    ).reshape(slot_count, width)

    to_x = [(x + step) % RING for step in range(RING)]
    cols = jnp.stack(
        [jnp.stack([2 * to + core for to in to_x]), jnp.stack([2 * to + 1 - core for to in to_x])]
    ).astype(jnp.int32)
    query_states, passage_states, first = together(queries, passages, first)
    query_dy, query_keep, query_send = slopes_of(0, cols, inverse, first, emb, mixing, emb)
    turned = turn(query_states, passage_states, swap(query_states), swap(passage_states))
    (query_grads,) = input_grad([query_dy], head, 0)
    returned, query_grads, query_send, turned = together(returned, query_grads, query_send, turned)
    query_other = swap(query_send)

    passage_dy, passage_keep, passage_send = slopes_of(
        1, cols, inverse, first, emb, owner, returned
    )
    passage_other = swap(passage_send)
    slopes = jnp.concatenate([query_keep, passage_keep, query_other, passage_other], axis=0)
    head_grads, query_grads, passage_grads = scatter_head(
        turned, slopes, core, head, query_dy, passage_dy, query_grads
    )
    return (query_grads, passage_grads, head_grads)


def solution(mesh):
    fine = Mesh(mesh.devices.reshape(4, 2, 4, 4), ("x", "c", "y", "z"))
    every = ("x", "c", "y", "z")
    return jax.shard_map(
        per_device,
        mesh=fine,
        in_specs=(
            P(every, None),
            P(every, None),
            P(("y", "z"), None),
            P(("x", "c"), ("y", "z"), None, None),
            P(every, None),
        ),
        out_specs=(P(every, None), P(every, None), P(("y", "z"), ("x", "c"))),
        check_vma=False,
    )
```

```python
import jax
import jax.numpy as jnp
from jax import lax
from jax.experimental import pallas as pl
from jax.experimental.pallas import tpu as pltpu
from jax.sharding import Mesh, PartitionSpec as P

EPSILON = 1e-06
BLOCK = 256
RING = 4
SWAP = [(0, 1), (1, 0)]
BF16 = jnp.bfloat16
F32 = jnp.float32


def shift(value, place, step):
    pairs = []
    for c in range(2):
        for y in range(RING):
            for z in range(RING):
                to_y, to_z = y, z
                if (place == 1) == (c == 0):
                    to_y = (y + step) % RING
                else:
                    to_z = (z + step) % RING
                pairs.append((c * 16 + y * 4 + z, c * 16 + to_y * 4 + to_z))
    return lax.ppermute(value, ("c", "y", "z"), pairs)


def swap(value):
    return lax.ppermute(value, "c", SWAP)


def block_at(core, d1, d2):
    y, z = lax.axis_index("y"), lax.axis_index("z")
    far_y = jnp.where(core == 0, d1, d2)
    far_z = jnp.where(core == 0, d2, d1)
    return ((y + far_y) % RING) * RING + (z + far_z) % RING


def together(*values):
    return lax.optimization_barrier(values)


def turn_kernel(*refs):
    parts = 4
    x_refs, turned_ref, held, turned, loaded, stored = refs[:4], *refs[4:]
    rows, depth = x_refs[0].shape
    size = depth // parts
    loads, stores = [], []
    for i in range(parts):
        at = pl.ds(i * size, size)
        loads.append(
            [
                pltpu.make_async_copy(ref.at[:, at], held.at[pl.ds(j * rows, rows), at], loaded.at[i, j])
                for j, ref in enumerate(x_refs)
            ]
        )
        stores.append(pltpu.make_async_copy(turned.at[at, :], turned_ref.at[at, :], stored.at[i]))
    for load in loads:
        start(load)
    for i in range(parts):
        wait(loads[i])
        for k in range(size // BLOCK):
            at = pl.ds(i * size + k * BLOCK, BLOCK)
            turned[at, :] = held[:, at].T
        stores[i].start()
    wait(stores)


def turn(*states):
    rows, depth = states[0].shape
    whole = rows * len(states)
    anywhere = pl.BlockSpec(memory_space=pl.ANY)
    return pl.pallas_call(
        turn_kernel,
        in_specs=[anywhere] * len(states),
        out_specs=anywhere,
        out_shape=pltpu.HBM((depth, whole), BF16),
        scratch_shapes=[
            pltpu.VMEM((whole, depth), BF16),
            pltpu.VMEM((depth, whole), BF16),
            pltpu.SemaphoreType.DMA((4, len(states))),
            pltpu.SemaphoreType.DMA((4,)),
        ],
        compiler_params=pltpu.CompilerParams(vmem_limit_bytes=20 * 1024 * 1024),
        cost_estimate=pl.CostEstimate(flops=1, transcendentals=0, bytes_accessed=1),
        name="turn",
    )(*keep_far(*states[:2]), *states[2:])


def copies_of(pairs, sems):
    return [pltpu.make_async_copy(*pair, sems.at[i]) for i, pair in enumerate(pairs)]


def start(copies):
    for copy in copies:
        copy.start()


def wait(copies):
    for copy in copies:
        copy.wait()


def head_copies(at_ref, held, head_ref, side, blocks, sems):
    col = pl.multiple_of(at_ref[1, side] * 1024, 1024)
    pairs = []
    for k in blocks:
        row = pl.multiple_of(at_ref[0, 16 * side + k] * BLOCK, BLOCK)
        pairs.append(
            (
                held.at[side, pl.ds((k - blocks[0]) * BLOCK, BLOCK), :],
                head_ref.at[pl.ds(row, BLOCK), pl.ds(col, 1024)],
            )
        )
    return copies_of(pairs, sems)


def piece_copies(pieces, held, side, sems):
    row, pairs = 0, []
    for piece in pieces:
        pairs.append((piece, held.at[side, pl.ds(row, piece.shape[0]), :]))
        row += piece.shape[0]
    return copies_of(pairs, sems)


def column_copies(at_ref, side, blocks, sources, states, sems):
    pairs = []
    for i, k in enumerate(blocks):
        col, row = pl.multiple_of(at_ref[0, 16 * side + k] * BLOCK, BLOCK), 0
        for ref in sources:
            to = states.at[side, pl.ds(row, ref.shape[0]), pl.ds(i * BLOCK, BLOCK)]
            pairs.append((ref.at[:, pl.ds(col, BLOCK)], to))
            row += ref.shape[0]
    return copies_of(pairs, sems)


def strips(at_ref, side, body, unroll=1):
    def one(n, _):
        at_col = pl.multiple_of(n * BLOCK, BLOCK)
        body(pl.ds(at_col, BLOCK), pl.ds(pl.multiple_of(at_ref[1, side] * 1024 + at_col, BLOCK), BLOCK))
        return 0

    lax.fori_loop(0, 1024 // BLOCK, one, 0, unroll=unroll)


def project_early_kernel(count, at_ref, *refs):
    x_refs, pieces = refs[:2], refs[2 : 2 + 2 * count]
    head_ref, part_out, states, held, part_ref, fetched, loaded, stored, parted = refs[2 + 2 * count :]
    blocks = list(range(held.shape[1] // BLOCK))
    loads = [
        column_copies(at_ref, i, blocks, x_refs, states, fetched.at[i])
        + piece_copies(pieces[i * count : (i + 1) * count], held, i, loaded.at[i])
        for i in range(2)
    ]
    stores = [head_copies(at_ref, held, head_ref, i, blocks, stored.at[i]) for i in range(2)]
    outs = []
    start(loads[0])
    for side in range(2):
        wait(loads[side])
        start(loads[1] if side == 0 else stores[0] + stores[1])

        def multiply(near_at, whole_at, side=side):
            part_ref[:, whole_at] = jnp.dot(
                states[side], held[side, :, near_at], preferred_element_type=F32
            ).astype(BF16)

        strips(at_ref, side, multiply)
        whole = pl.ds(pl.multiple_of(at_ref[1, side] * 1024, 1024), 1024)
        outs.append(pltpu.make_async_copy(part_ref.at[:, whole], part_out.at[:, whole], parted.at[side]))
        start(outs[side:])
    wait(outs + stores[0] + stores[1])


def project_early(at, xs, pieces):
    count, depth = len(pieces) // 2, sum(piece.shape[0] for piece in pieces) // 2
    rows = sum(x.shape[0] for x in xs)
    anywhere = pl.BlockSpec(memory_space=pl.ANY)
    return pl.pallas_call(
        lambda *refs: project_early_kernel(count, *refs),
        in_specs=[pl.BlockSpec(memory_space=pltpu.SMEM)] + [anywhere] * (2 + 2 * count),
        out_specs=[anywhere] * 2,
        out_shape=[pltpu.HBM((4096, 2048), BF16), pltpu.HBM((rows, 2048), BF16)],
        scratch_shapes=[
            pltpu.VMEM((2, rows, depth), BF16),
            pltpu.VMEM((2, depth, 1024), BF16),
            pltpu.VMEM((rows, 2048), BF16),
            pltpu.SemaphoreType.DMA((2, 2 * depth // BLOCK)),
            pltpu.SemaphoreType.DMA((2, count)),
            pltpu.SemaphoreType.DMA((2, depth // BLOCK)),
            pltpu.SemaphoreType.DMA((2,)),
        ],
        compiler_params=pltpu.CompilerParams(vmem_limit_bytes=24 * 1024 * 1024),
        name="project_early",
    )(at, *keep_far(*xs, *pieces))


def project_middle_kernel(count, early, at_ref, *refs):
    x_refs, pieces = refs[:3], refs[3 : 3 + 2 * count]
    part_in, _, head_ref, part_out = refs[3 + 2 * count : 7 + 2 * count]
    own_states, far_states, held, part_ref, fetched, loaded, stored, parted = refs[7 + 2 * count :]
    rows, depth = far_states.shape[1], held.shape[1]
    blocks = list(range(depth // BLOCK))
    late = early * BLOCK
    base = copies_of([(part_in, part_ref.at[pl.ds(0, rows), :])], parted.at[2])
    loads = [
        column_copies(at_ref, i, blocks, x_refs[2:], far_states, fetched.at[2 * i])
        + piece_copies(pieces[i * count : (i + 1) * count], held, i, loaded.at[i])
        + column_copies(at_ref, i, blocks[early:], x_refs[:2], own_states, fetched.at[2 * i + 1])
        for i in range(2)
    ]
    stores = [head_copies(at_ref, held, head_ref, i, blocks, stored.at[i])[early:] for i in range(2)]
    outs = []
    start(loads[0] + base)
    for side in range(2):
        wait(loads[side])
        start(loads[1] if side == 0 else stores[0] + stores[1])
        if side == 0:
            wait(base)

        def multiply(near_at, whole_at, side=side):
            own_at = pl.ds(0, rows)
            part_ref[own_at, whole_at] = (
                part_ref[own_at, whole_at].astype(F32)
                + jnp.dot(
                    own_states[side],
                    held[side, pl.ds(late, depth - late), near_at],
                    preferred_element_type=F32,
                )
            ).astype(BF16)
            part_ref[pl.ds(rows, rows), whole_at] = jnp.dot(
                far_states[side], held[side, :, near_at], preferred_element_type=F32
            ).astype(BF16)

        strips(at_ref, side, multiply)
        whole = pl.ds(pl.multiple_of(at_ref[1, side] * 1024, 1024), 1024)
        outs.append(
            pltpu.make_async_copy(part_ref.at[:, whole], part_out.at[:, whole], parted.at[side, 0])
        )
        start(outs[side:])
    wait(outs + stores[0] + stores[1])


def project_middle(at, early, xs, pieces, part, head):
    count, depth = len(pieces) // 2, sum(piece.shape[0] for piece in pieces) // 2
    rows = xs[2].shape[0]
    anywhere = pl.BlockSpec(memory_space=pl.ANY)
    ins = [anywhere] * (5 + 2 * count)
    return pl.pallas_call(
        lambda *refs: project_middle_kernel(count, early, *refs),
        in_specs=[pl.BlockSpec(memory_space=pltpu.SMEM)] + ins,
        out_specs=[anywhere] * 2,
        out_shape=[pltpu.HBM((4096, 2048), BF16), pltpu.HBM((2 * rows, 2048), BF16)],
        scratch_shapes=[
            pltpu.VMEM((2, rows, depth - early * BLOCK), BF16),
            pltpu.VMEM((2, rows, depth), BF16),
            pltpu.VMEM((2, depth, 1024), BF16),
            pltpu.VMEM((2 * rows, 2048), BF16),
            pltpu.SemaphoreType.DMA((4, 16)),
            pltpu.SemaphoreType.DMA((2, count)),
            pltpu.SemaphoreType.DMA((2, depth // BLOCK)),
            pltpu.SemaphoreType.DMA((3, 1)),
        ],
        input_output_aliases={len(ins): 0},
        compiler_params=pltpu.CompilerParams(vmem_limit_bytes=36 * 1024 * 1024),
        name="project_middle",
    )(at, *keep_far(*xs), *pieces, *keep_far(part, head))


def project_last_kernel(count, at_ref, *refs):
    x_refs, pieces = refs[:3], refs[3 : 3 + 2 * count]
    part_in, counts_ref, _, head_ref, emb_out, inverse_ref, mixing_ref, first_ref, grad_ref = refs[
        3 + 2 * count : 12 + 2 * count
    ]
    states, held, part_ref, pre_ref, emb_ref, parted, fetched, loaded, stored, sent = refs[12 + 2 * count :]
    late = held.shape[1] // BLOCK
    blocks = list(range(16 - late, 16))
    loads, stores = [], []
    for side in range(2):
        copies = column_copies(at_ref, side, blocks, x_refs, states, fetched.at[side])
        copies += piece_copies(pieces[side * count : (side + 1) * count], held, side, loaded.at[side])
        loads.append(copies)
        stores.append(head_copies(at_ref, held, head_ref, side, blocks, stored.at[side]))
    halves = [pl.ds(pl.multiple_of(at_ref[1, side] * 1024, 1024), 1024) for side in range(2)]
    base = copies_of([(part_in.at[:, at], part_ref.at[:, at]) for at in halves], parted)
    start(loads[0] + base[:1] + loads[1] + base[1:])
    inverse_ref[...] = jnp.zeros(inverse_ref.shape, F32)
    for side in range(2):
        wait(loads[side] + base[side : side + 1])
        if side == 1:
            start(stores[0] + stores[1])

        def multiply(near_at, whole_at, side=side):
            values = part_ref[:, whole_at].astype(F32) + jnp.dot(
                states[side], held[side, :, near_at], preferred_element_type=F32
            )
            pre_ref[:, whole_at] = values
            squares = values * values
            inverse_ref[...] += squares[:, :128] + squares[:, 128:]

        strips(at_ref, side, multiply, 4)
    normalize(pre_ref, emb_ref, inverse_ref)
    sending = copies_of([(emb_ref, emb_out)], sent)
    start(sending)
    contrast(counts_ref, emb_ref, mixing_ref, first_ref, grad_ref)
    wait(sending + stores[0] + stores[1])


def project_last(at, xs, pieces, part, counts, head):
    count, depth = len(pieces) // 2, sum(piece.shape[0] for piece in pieces) // 2
    rows = sum(x.shape[0] for x in xs)
    half = rows // 4
    anywhere = pl.BlockSpec(memory_space=pl.ANY)
    ins = [anywhere] * (4 + 2 * count) + vmem(1) + [anywhere]
    return pl.pallas_call(
        lambda *refs: project_last_kernel(count, *refs),
        in_specs=[pl.BlockSpec(memory_space=pltpu.SMEM)] + ins,
        out_specs=[anywhere] * 2 + vmem(4),
        out_shape=[
            pltpu.HBM((4096, 2048), BF16),
            pltpu.HBM((rows, 2048), BF16),
            pltpu.HBM((rows, 128), F32),
            pltpu.HBM((half, 2 * half), BF16),
            pltpu.HBM((half, 128), F32),
            pltpu.HBM((2 * half, 2048), BF16),
        ],
        scratch_shapes=[
            pltpu.VMEM((2, rows, depth), BF16),
            pltpu.VMEM((2, depth, 1024), BF16),
            pltpu.VMEM((rows, 2048), BF16),
            pltpu.VMEM((rows, 2048), F32),
            pltpu.VMEM((rows, 2048), BF16),
            pltpu.SemaphoreType.DMA((2,)),
            pltpu.SemaphoreType.DMA((2, 3 * depth // BLOCK)),
            pltpu.SemaphoreType.DMA((2, count)),
            pltpu.SemaphoreType.DMA((2, depth // BLOCK)),
            pltpu.SemaphoreType.DMA((1,)),
        ],
        input_output_aliases={len(ins): 0},
        compiler_params=pltpu.CompilerParams(vmem_limit_bytes=30 * 1024 * 1024),
        name="project_last",
    )(at, *keep_far(*xs), *pieces, *keep_far(part), counts, *keep_far(head))


def normalize(pre_ref, emb_ref, inverse_ref):
    chunk = 128
    width = pre_ref.shape[1]

    def some(i, _):
        at = pl.ds(pl.multiple_of(i * chunk, chunk), chunk)
        mean = jnp.sum(inverse_ref[at, :], axis=-1, keepdims=True) * (1.0 / width)
        inverse = jnp.broadcast_to(lax.rsqrt(mean + EPSILON), (chunk, 128))
        inverse_ref[at, :] = inverse
        emb_ref[at, :] = (pre_ref[at, :] * inverse[:, :1]).astype(BF16)
        return 0

    lax.fori_loop(0, pre_ref.shape[0] // chunk, some, 0)


def contrast(counts_ref, emb_ref, mixing_ref, first_ref, grad_ref):
    rows = counts_ref.shape[0]
    scale = 16.0 / emb_ref.shape[1]
    query = emb_ref[pl.ds(0, rows), :]
    passage = emb_ref[pl.ds(rows, rows), :]
    fetched = emb_ref[pl.ds(2 * rows, 2 * rows), :]
    positive = (
        jnp.sum(query.astype(F32) * passage.astype(F32), axis=1, keepdims=True) * scale
    )
    table = dot(query, fetched, ((1,), (1,))) * scale
    counts = counts_ref[...]
    top = jnp.maximum(
        positive, jnp.max(jnp.where(counts > 0, table, -1e30), axis=1, keepdims=True)
    )
    raised = jnp.where(counts > 0, jnp.exp(jnp.where(counts > 0, table - top, 0.0)), 0.0)
    raised_positive = jnp.exp(positive - top)
    whole = raised_positive + jnp.sum(raised * counts, axis=1, keepdims=True)
    first = (raised_positive / whole - 1.0).astype(BF16).astype(F32)
    mixing = ((raised / whole).astype(BF16).astype(F32) * counts).astype(BF16)
    first_ref[...] = jnp.broadcast_to(first, (rows, 128))
    mixing_ref[...] = mixing
    grad_ref[...] = dot(mixing, query, ((0,), (0,))).astype(BF16)


def vmem(count):
    return [pl.BlockSpec(memory_space=pltpu.VMEM)] * count


def near(shape, dtype):
    return pltpu.VMEM(shape, dtype)


def keep_near(*values):
    return [pltpu.with_memory_space_constraint(value, pltpu.VMEM) for value in values]


def keep_far(*values):
    return [pltpu.with_memory_space_constraint(value, pltpu.HBM) for value in values]


def slopes_kernel(part, cols_ref, inverse_hbm, first_hbm, emb_hbm, left_hbm, right_hbm, out_ref, keep_ref, send_ref, grad_ref, inverse_ref, first_ref, emb_ref, own_ref, left_ref, right_ref, sems):
    rows, chunk = out_ref.shape[0], 96
    width = out_ref.shape[1]
    depth = left_ref.shape[1]
    loads = [
        (left_hbm, left_ref),
        (right_hbm.at[pl.ds(2 * rows if part == 0 else 0, depth), :], right_ref),
        (emb_hbm.at[pl.ds((1 - part) * rows, rows), :], emb_ref),
        (first_hbm, first_ref),
        (inverse_hbm.at[pl.ds(part * rows, rows), :], inverse_ref),
        (emb_hbm.at[pl.ds(part * rows, rows), :], own_ref),
    ]
    loads = [pltpu.make_async_copy(*load, sems.at[i]) for i, load in enumerate(loads)]
    for load in loads:
        load.start()
    for load in loads[:2]:
        load.wait()
    grad_ref[...] = jnp.dot(left_ref[...], right_ref[...], preferred_element_type=F32)
    for load in loads[2:]:
        load.wait()

    def some(i, _):
        at = pl.ds(pl.multiple_of(i * chunk, chunk), chunk)
        grad = first_ref[at, :1] * emb_ref[at, :].astype(F32) + grad_ref[at, :]
        values = own_ref[at, :].astype(F32)
        along = jnp.mean(grad * values, axis=-1, keepdims=True)
        out_ref[at, :] = (inverse_ref[at, :1] * (grad - values * along)).astype(BF16)
        return 0

    lax.fori_loop(0, rows // chunk, some, 0)
    for k in range(width // BLOCK // 2):
        for row, ref in ((0, keep_ref), (1, send_ref)):
            col = pl.multiple_of(cols_ref[row, k] * BLOCK, BLOCK)
            ref[:, pl.ds(k * BLOCK, BLOCK)] = out_ref[:, pl.ds(col, BLOCK)]


def slopes_of(part, cols, inverse, first, emb, left, right):
    rows = first.shape[0]
    width = emb.shape[1]
    anywhere = pl.BlockSpec(memory_space=pl.ANY)
    return pl.pallas_call(
        lambda *refs: slopes_kernel(part, *refs),
        in_specs=[pl.BlockSpec(memory_space=pltpu.SMEM)] + [anywhere] * 5,
        out_specs=vmem(3),
        out_shape=[
            jax.ShapeDtypeStruct((rows, width), BF16),
            jax.ShapeDtypeStruct((rows, width // 2), BF16),
            jax.ShapeDtypeStruct((rows, width // 2), BF16),
        ],
        scratch_shapes=[
            pltpu.VMEM((rows, width), F32),
            pltpu.VMEM(first.shape, F32),
            pltpu.VMEM(first.shape, F32),
            pltpu.VMEM((rows, width), BF16),
            pltpu.VMEM((rows, width), BF16),
            pltpu.VMEM(left.shape, BF16),
            pltpu.VMEM((left.shape[1], width), BF16),
            pltpu.SemaphoreType.DMA((6,)),
        ],
        compiler_params=pltpu.CompilerParams(vmem_limit_bytes=16 * 1024 * 1024),
        name="slopes_of",
    )(cols, *keep_far(inverse, first, emb, left), right)


def input_grad_kernel(count, *refs):
    slopes_refs, head_ref, out_refs = refs[:count], refs[count], refs[-count:]
    rows = slopes_refs[0].shape[0]
    slopes = jnp.concatenate([ref[...] for ref in slopes_refs], axis=0)
    grads = dot(slopes, head_ref[...], ((1,), (1,))).astype(BF16)
    for i, ref in enumerate(out_refs):
        ref[...] = grads[i * rows : (i + 1) * rows]


def input_grad(slopes, head, part, filled=()):
    count = len(slopes)
    rows, width = slopes[0].shape
    depth = head.shape[0]
    steps = depth // 512 // 2
    return pl.pallas_call(
        lambda *refs: input_grad_kernel(count, *refs),
        grid=(steps,),
        in_specs=[pl.BlockSpec((rows, width), lambda k: (0, 0))] * count
        + [pl.BlockSpec((512, width), lambda k: (k + part * steps, 0))]
        + [pl.BlockSpec(memory_space=pl.ANY)] * len(filled),
        out_specs=[pl.BlockSpec((rows, 512), lambda k: (0, k + part * steps))] * count,
        out_shape=[jax.ShapeDtypeStruct((rows, depth), BF16)] * count,
        input_output_aliases={count + 1 + i: i for i in range(len(filled))},
        compiler_params=pltpu.CompilerParams(vmem_limit_bytes=20 * 1024 * 1024),
        cost_estimate=pl.CostEstimate(flops=1, transcendentals=0, bytes_accessed=1),
        name="input_grad",
    )(*slopes, *keep_far(head), *filled)


def partial_kernel(outs, adds, at_ref, states_ref, slopes_ref, *refs):
    for i in range(outs):

        def block(k, _, i=i):
            row = pl.multiple_of(at_ref[2 * i + k] * BLOCK, BLOCK)
            part = pl.ds(pl.multiple_of(k * BLOCK, BLOCK), BLOCK)
            total = jnp.dot(
                states_ref[pl.ds(row, BLOCK), :], slopes_ref[...], preferred_element_type=F32
            ) * (1.0 / 128.0)
            for ref in refs[i * adds : (i + 1) * adds]:
                total = total + ref[part, :].astype(F32)
            refs[outs * adds + i][part, :] = total.astype(BF16)
            return 0

        lax.fori_loop(0, 2, block, 0, unroll=adds == 0)


def head_partial(states, slopes, at, adds):
    outs, width = len(adds), slopes.shape[1]
    return pl.pallas_call(
        lambda *refs: partial_kernel(outs, len(adds[0]), *refs),
        in_specs=[pl.BlockSpec(memory_space=pltpu.SMEM)] + vmem(2 + outs * len(adds[0])),
        out_specs=vmem(outs),
        out_shape=[jax.ShapeDtypeStruct((2 * BLOCK, width), BF16)] * outs,
        compiler_params=pltpu.CompilerParams(vmem_limit_bytes=20 * 1024 * 1024),
        name="head_partial",
    )(at, *keep_near(states), slopes, *[value for some in adds for value in some])


def add(*values):
    total = values[0].astype(F32)
    for value in values[1:]:
        total = total + value.astype(F32)
    return total.astype(BF16)


def scatter_head(states, slopes, core, head, query_dy, passage_dy, query_grads):
    def part(d1s, d2s, adds):
        at = [block_at(core, d1, d2) for d1, some in zip(d1s, d2s) for d2 in some]
        return head_partial(states, slopes, jnp.stack(at).astype(jnp.int32), adds)

    a, b = (2, 1), (-1, 0)
    far_a, far_b = part((2, 2), (a, b), ((), ()))
    far_a, far_b = shift(far_a, 1, 1), shift(far_b, 1, -1)
    up_b, down_a = part((1, -1), (b, a), ((), ()))
    up_b, down_a, passage_dy = together(up_b, down_a, passage_dy)
    up_b, down_a = shift(up_b, 1, 1), shift(down_a, 1, -1)
    (passage_grads,) = input_grad([passage_dy], head, 0)
    far_a, far_b, passage_grads = together(far_a, far_b, passage_grads)
    up_a, down_b = part((1, -1), (a, b), ((far_a,), (far_b,)))
    up_a, down_b = shift(up_a, 1, 1), shift(down_b, 1, -1)
    mine_a, mine_b = part((0, 0), (a, b), ((down_a,), (up_b,)))
    mine_a, mine_b, passage_dy = together(mine_a, mine_b, passage_dy)
    grads = input_grad([query_dy, passage_dy], head, 1, [query_grads, passage_grads])
    up_a, down_b, mine_a, mine_b, *grads = together(up_a, down_b, mine_a, mine_b, *grads)
    half = BLOCK // 2
    far, up = mine_a[:BLOCK], mine_a[BLOCK:]
    down, mine = mine_b[:BLOCK], mine_b[BLOCK:]
    up_far, up_up = up_a[:BLOCK], up_a[BLOCK:]
    down_down, down_mine = down_b[:BLOCK], down_b[BLOCK:]
    far_a = shift(add(far[:half], up_far[:half]), 2, 1)
    far_b = shift(add(far[half:], up_far[half:]), 2, -1)
    up_b = shift(add(up[half:], up_up[half:]), 2, 1)
    down_a = shift(add(down[:half], down_down[:half]), 2, -1)
    far_a, far_b, up_b, down_a = together(far_a, far_b, up_b, down_a)
    up_a = shift(add(up[:half], up_up[:half], far_a), 2, 1)
    down_b = shift(add(down[half:], down_down[half:], far_b), 2, -1)
    up_a, down_b = together(up_a, down_b)
    total = jnp.concatenate(
        [
            add(mine[:half], down_mine[:half], down_a, up_a),
            add(mine[half:], down_mine[half:], up_b, down_b),
        ],
        axis=0,
    )
    arrived = together(
        *[
            lax.ppermute(
                total[:, step * BLOCK : (step + 1) * BLOCK],
                "x",
                [(i, (i + step) % RING) for i in range(RING)],
            )
            for step in (2, 1, 3)
        ]
    )
    out = total[:, :BLOCK].astype(F32)
    for value in arrived:
        out = out + value.astype(F32)
    return out, *grads


def dot(a, b, contract=((1,), (0,))):
    return lax.dot_general(a, b, (contract, ((), ())), preferred_element_type=F32)


def per_device(queries, passages, head_weight, send_lists, neg_slots):
    core, x = lax.axis_index("c"), lax.axis_index("x")
    rows_dev, depth = queries.shape
    width = head_weight.shape[1]
    groups, capacity = send_lists.shape[2], send_lists.shape[3]
    slot_count = groups * capacity
    flat_lists = send_lists.reshape(slot_count)

    owner = (flat_lists[None, :] == jnp.arange(rows_dev, dtype=jnp.int32)[:, None]).astype(BF16)
    own = lax.dynamic_slice_in_dim(head_weight, core * (width // 2), width // 2, axis=1)

    up, down = shift(own, 1, 1), shift(own, 1, -1)
    picked = dot(owner, passages, ((0,), (0,))).astype(BF16).reshape(groups, capacity, depth)
    own, picked = together(own, picked)
    own_up, own_down = shift(own, 2, 1), shift(own, 2, -1)
    arrived = lax.all_to_all(picked, ("x", "c"), split_axis=0, concat_axis=0, tiled=True)
    arrived = arrived.reshape(slot_count, depth)

    far = shift(up, 1, 1)
    up_up, up_down = shift(up, 2, 1), shift(up, 2, -1)
    slot_ids = jnp.arange(slot_count, dtype=jnp.int32)[None, :]
    counts = jnp.zeros((rows_dev, slot_count), F32)
    for j in range(neg_slots.shape[1]):
        counts = counts + (neg_slots[:, j : j + 1] == slot_ids).astype(F32)
    far, up_up, up_down, own_up, own_down, counts, owner = together(
        far, up_up, up_down, own_up, own_down, counts, owner
    )

    second = jnp.concatenate([down, far], axis=0)
    second_up, second_down = shift(second, 2, 1), shift(second, 2, -1)
    first_up = jnp.concatenate([own_up, up_up], axis=0)
    early = [own, up, second, first_up, own_down, up_down]
    early = early, [swap(piece) for piece in early]
    places = [(0, 0), (-1, 0), (1, 0), (2, 0), (0, -1), (-1, -1), (0, 1), (-1, 1)]
    places += [(1, -1), (2, -1), (1, 1), (2, 1), (0, 2), (-1, 2), (1, 2), (2, 2)]
    at = [block_at(core, *place) for place in places] + [block_at(1 - core, *place) for place in places]
    side = [core, 1 - core] + [core] * 30
    at = jnp.stack([jnp.stack(at), jnp.stack(side)]).astype(jnp.int32)
    xs = queries, passages, arrived
    head, part = project_early(at, xs[:2], early[0] + early[1])
    second_up, second_down, first_up, part = together(second_up, second_down, first_up, part)

    first_far, second_far = shift(first_up, 2, 1), shift(second_down, 2, -1)
    middle = [second_up, second_down]
    other_middle = [swap(piece) for piece in middle]
    early = [keep_far(*some) for some in early]
    head, part = project_middle(at, 8, xs, early[0] + middle + early[1] + other_middle, part, head)
    first_far, second_far, part = together(first_far, second_far, part)
    late = [first_far, second_far, swap(first_far), swap(second_far)]
    head, emb, inverse, mixing, first, fetched_grad = project_last(at, xs, late, part, counts, head)
    returned = lax.all_to_all(
        fetched_grad.reshape(groups, capacity, width),
        ("x", "c"),
        split_axis=0,
        concat_axis=0,
        tiled=True,
    ).reshape(slot_count, width)

    to_x = [(x + step) % RING for step in range(RING)]
    cols = jnp.stack(
        [jnp.stack([2 * to + core for to in to_x]), jnp.stack([2 * to + 1 - core for to in to_x])]
    ).astype(jnp.int32)
    query_states, passage_states, first = together(queries, passages, first)
    query_dy, query_keep, query_send = slopes_of(0, cols, inverse, first, emb, mixing, emb)
    turned = turn(query_states, passage_states, swap(query_states), swap(passage_states))
    (query_grads,) = input_grad([query_dy], head, 0)
    returned, query_grads, query_send, turned = together(returned, query_grads, query_send, turned)
    query_other = swap(query_send)

    passage_dy, passage_keep, passage_send = slopes_of(
        1, cols, inverse, first, emb, owner, returned
    )
    passage_other = swap(passage_send)
    slopes = jnp.concatenate([query_keep, passage_keep, query_other, passage_other], axis=0)
    head_grads, query_grads, passage_grads = scatter_head(
        turned, slopes, core, head, query_dy, passage_dy, query_grads
    )
    return (query_grads, passage_grads, head_grads)


def solution(mesh):
    fine = Mesh(mesh.devices.reshape(4, 2, 4, 4), ("x", "c", "y", "z"))
    every = ("x", "c", "y", "z")
    return jax.shard_map(
        per_device,
        mesh=fine,
        in_specs=(
            P(every, None),
            P(every, None),
            P(("y", "z"), None),
            P(("x", "c"), ("y", "z"), None, None),
            P(every, None),
        ),
        out_specs=(P(every, None), P(every, None), P(("y", "z"), ("x", "c"))),
        check_vma=False,
    )
```
